32 devices in a mesh: section: 8 (over y, x, core), ctx: 4 (over z).
Axes of the slice: x: 2, y: 2, z: 4, core: 2. Of those that a mesh axis runs over, the one named last changes fastest.
Arguments:
- streams: bfloat16 [8, 512, 5120], P('section', 'ctx'), may hold values from -6 to 6
- conv_weight: bfloat16 [8, 4, 5120], P('section'), may hold values from -3 to 3
- beta_logit: float32 [8, 512, 16], P('section', 'ctx'), may hold values from -12 to 3
- gate_log: float32 [8, 512, 8], P('section', 'ctx'), may hold values from -2 to 0
- norm_gain: float32 [8, 1024], P('section'), may hold values from 0.25 to 1.75
- w_out: bfloat16 [8, 1024, 2048], P('section', None, 'ctx'), may hold values from -0.1875 to 0.1875
Outputs:
- handed: bfloat16 [8, 512, 2048], P('section', 'ctx')
The draws below stay inside these ranges and needn't reach their ends.
All inputs are finite; a program needn't handle non-finite values.
Results may differ from the reference program's by a relative error of at most 0.0049.
Values may be sent and summed in bfloat16 or wider, within the bound.
No kernel may reach another device: no remote copies, remote signals or barrier semaphores. Data moves between devices by JAX's collectives and lax.ppermute only.
A program may use at most 128 MiB of HBM per device.

```python
import math
import jax
import jax.numpy as jnp
from jax import lax

D = 2048
HEAD_TOTAL = 8
HK = 128
STEPS = 2
CONV = 4
SPAN = 128
TOK_DEV = 128
TOKEN_TOTAL = 512
RELAY_SECTIONS = 8
HD = 1024
CH = 5120


def log_uniform(random_subkey, out_shape, low_end, high_end):
    return jnp.exp(jax.random.uniform(random_subkey, out_shape, jnp.float32, math.log(low_end), math.log(high_end)))


def fast_heads(key):
    fast_share = 0.5
    picked = jax.random.uniform(jax.random.fold_in(key, 11), (RELAY_SECTIONS, 1, HEAD_TOTAL), jnp.float32)
    return picked < fast_share


def shard_factor(random_subkey, lanes):
    factor = log_uniform(random_subkey, (RELAY_SECTIONS, TOKEN_TOTAL // TOK_DEV, lanes), 0.5, 2.0)
    return jnp.repeat(factor, TOK_DEV, axis=1)


def draw_gate_log(key, part):
    is_fast = fast_heads(key)
    random_subkey = jax.random.fold_in(key, 23)
    fast_rate = log_uniform(jax.random.fold_in(random_subkey, 1), (RELAY_SECTIONS, 1, HEAD_TOTAL), 0.8, 1.3) / min(40, TOK_DEV)
    slow_rate = log_uniform(jax.random.fold_in(random_subkey, 2), (RELAY_SECTIONS, 1, HEAD_TOTAL), 0.05, 0.3) / TOKEN_TOTAL
    decay_rates = jnp.where(is_fast, fast_rate, slow_rate)
    roughness = log_uniform(jax.random.fold_in(random_subkey, 3), (RELAY_SECTIONS, TOKEN_TOTAL, HEAD_TOTAL), 0.5, 2.0)
    spike_positions = jax.random.randint(jax.random.fold_in(random_subkey, 4), (RELAY_SECTIONS, 2, 1), 0, TOKEN_TOTAL)
    spike_matches = jnp.sum((jnp.arange(TOKEN_TOTAL)[None, None, :] == spike_positions).astype(jnp.float32), axis=1)
    spike_removals = jax.random.uniform(jax.random.fold_in(random_subkey, 5), (RELAY_SECTIONS, TOKEN_TOTAL, HEAD_TOTAL), jnp.float32, math.log(0.55), math.log(0.8))
    gentle_portion = decay_rates * shard_factor(jax.random.fold_in(random_subkey, 6), HEAD_TOTAL) * roughness
    return spike_matches[..., None] * spike_removals - gentle_portion


def draw_beta_logit(key, part):
    is_fast = jnp.tile(fast_heads(key), (1, 1, STEPS))
    random_subkey = jax.random.fold_in(key, 37)
    fast_size = log_uniform(jax.random.fold_in(random_subkey, 1), (RELAY_SECTIONS, 1, STEPS * HEAD_TOTAL), 0.2, 0.7)
    slow_size = log_uniform(jax.random.fold_in(random_subkey, 2), (RELAY_SECTIONS, 1, STEPS * HEAD_TOTAL), 0.05, 0.25) * HK / TOKEN_TOTAL
    roughness = log_uniform(jax.random.fold_in(random_subkey, 4), (RELAY_SECTIONS, TOKEN_TOTAL, STEPS * HEAD_TOTAL), 0.5, 2.0)
    sizes_now = jnp.where(is_fast, fast_size, slow_size) * shard_factor(jax.random.fold_in(random_subkey, 3), STEPS * HEAD_TOTAL) * roughness
    sizes_now = jnp.minimum(sizes_now, 0.95)
    return jnp.log(sizes_now) - jnp.log1p(-sizes_now)


def steps_of(rng, dims, shards, low, top_value):
    def one(axis_at, shards_of):
        draws = jax.random.uniform(jax.random.fold_in(jax.random.fold_in(rng, 6), axis_at), (shards_of,), jnp.float32, low / len(shards), top_value / len(shards))
        return jnp.repeat(jnp.exp(draws), dims[axis_at] // shards_of).reshape((-1,) + (1,) * (len(dims) - axis_at - 1))

    gain = one(*shards[0])
    for cut in shards[1:]:
        gain = gain * one(*cut)
    return gain


def gaussian(own_key, shape, scale, limit, cuts=(), kind=jnp.bfloat16):
    entries = scale * jax.random.normal(own_key, shape, jnp.float32)
    if cuts:
        entries = entries * steps_of(own_key, shape, cuts, -0.22, 0.18)
    return jnp.clip(entries, -limit, limit).astype(kind)


def setup_inputs(seed: int = 0) -> dict:
    seeds = jax.random.split(jax.random.key(seed), 7)
    streams = gaussian(seeds[0], (RELAY_SECTIONS, TOKEN_TOTAL, CH), 1.0, 6.0, ((0, 8), (1, 4)))
    conv_weight = gaussian(seeds[1], (RELAY_SECTIONS, CONV, CH), CONV ** -0.5, 3.0, ((0, 8),))
    beta_logit = draw_beta_logit(jax.random.fold_in(seeds[6], 71), 0)
    gate_log = draw_gate_log(jax.random.fold_in(seeds[6], 71), 0)
    norm_gain = jnp.clip(1.0 + 0.15 * jax.random.normal(seeds[4], (RELAY_SECTIONS, HD), jnp.float32), 0.25, 1.75)
    w_out = gaussian(seeds[5], (RELAY_SECTIONS, HD, D), HD ** -0.5, 0.1875, ((0, 8), (2, 4)))
    return {"streams": streams, "conv_weight": conv_weight, "beta_logit": beta_logit, "gate_log": gate_log, "norm_gain": norm_gain, "w_out": w_out}


highest = lax.Precision.HIGHEST

def mix_taps(extended, tap_weights):
    tok_count = extended.shape[0] - tap_weights.shape[0] + 1
    summed = jnp.zeros((tok_count, extended.shape[1]), jnp.float32)
    for offset in range(tap_weights.shape[0]):
        summed = summed + tap_weights[offset].astype(jnp.float32) * extended[offset:offset + tok_count].astype(jnp.float32)
    return jax.nn.silu(summed)

def unit_rows(vectors):
    return vectors * lax.rsqrt(lax.optimization_barrier(jnp.sum(vectors * vectors, axis=-1, keepdims=True)) + 1e-06)

def head_major(active, beta_logit, gate_log):
    tok_count = active.shape[0]
    head_width = HEAD_TOTAL * HK
    queries = unit_rows(active[:, :head_width].reshape(tok_count, HEAD_TOTAL, HK)).transpose(1, 0, 2)
    keys_all = unit_rows(active[:, head_width:(1 + STEPS) * head_width].reshape(tok_count, STEPS, HEAD_TOTAL, HK))
    keys_all = keys_all.transpose(2, 0, 1, 3).reshape(HEAD_TOTAL, tok_count * STEPS, HK)
    values_all = active[:, (1 + STEPS) * head_width:].reshape(tok_count, STEPS, HEAD_TOTAL, HK)
    values_all = values_all.transpose(2, 0, 1, 3).reshape(HEAD_TOTAL, tok_count * STEPS, HK)
    step_size = jax.nn.sigmoid(beta_logit.reshape(tok_count, STEPS, HEAD_TOTAL)).transpose(2, 0, 1).reshape(HEAD_TOTAL, tok_count * STEPS)
    opening = (lax.broadcasted_iota(jnp.int32, (1, STEPS, 1), 1) == 0).astype(gate_log.dtype)
    log_gate = (gate_log[:, None, :] * opening).transpose(2, 0, 1).reshape(HEAD_TOTAL, tok_count * STEPS)
    return (queries, keys_all, values_all, step_size, log_gate)

def span_terms(queries, keys_all, values_all, step_size, log_gate):
    head_count, virtual, head_dim = keys_all.shape
    blocks = virtual // SPAN
    per_block = SPAN // STEPS
    queries = queries.reshape(head_count, blocks, per_block, head_dim)
    keys_all = keys_all.reshape(head_count, blocks, SPAN, head_dim)
    values_all = values_all.reshape(head_count, blocks, SPAN, head_dim)
    step_size = step_size.reshape(head_count, blocks, SPAN)
    cumulate = jnp.cumsum(log_gate.reshape(head_count, blocks, SPAN), axis=-1)
    query_log = cumulate[..., STEPS - 1::STEPS]
    row_index = lax.broadcasted_iota(jnp.int32, (SPAN, SPAN), 0)
    col_index = lax.broadcasted_iota(jnp.int32, (SPAN, SPAN), 1)
    strict = col_index < row_index
    spread = cumulate[..., :, None] - cumulate[..., None, :]
    damping = jnp.where(strict, jnp.exp(jnp.where(strict, spread, 0.0)), 0.0)
    key_inner = jnp.einsum('hcid,hcjd->hcij', keys_all, keys_all, precision=highest)
    unit_lower = jnp.eye(SPAN, dtype=key_inner.dtype) + step_size[..., :, None] * damping * key_inner
    right_sides = jnp.concatenate([step_size[..., None] * values_all, (step_size * jnp.exp(cumulate))[..., None] * keys_all], axis=-1)
    solved = jax.scipy.linalg.solve_triangular(unit_lower, right_sides, lower=True, unit_diagonal=True)
    value_part = solved[..., :head_dim]
    key_part = solved[..., head_dim:]
    to_end = keys_all * jnp.exp(cumulate[..., -1:] - cumulate)[..., None]
    carried = jnp.exp(cumulate[..., -1])[..., None, None] * jnp.eye(head_dim, dtype=key_inner.dtype)
    carried = carried - jnp.einsum('hcid,hcie->hcde', to_end, key_part, precision=highest)
    written = jnp.einsum('hcid,hcie->hcde', to_end, value_part, precision=highest)
    query_row = lax.broadcasted_iota(jnp.int32, (per_block, SPAN), 0) * STEPS + STEPS - 1
    query_col = lax.broadcasted_iota(jnp.int32, (per_block, SPAN), 1)
    allowed = query_col <= query_row
    query_spread = query_log[..., :, None] - cumulate[..., None, :]
    query_damping = jnp.where(allowed, jnp.exp(jnp.where(allowed, query_spread, 0.0)), 0.0)
    scores = jnp.einsum('hcpd,hcid->hcpi', queries, keys_all, precision=highest) * query_damping
    direct = jnp.einsum('hcpi,hcie->hcpe', scores, value_part, precision=highest)
    reach_map = queries * jnp.exp(query_log)[..., None] - jnp.einsum('hcpi,hcie->hcpe', scores, key_part, precision=highest)
    return (jnp.moveaxis(carried, 1, 0), jnp.moveaxis(written, 1, 0), jnp.moveaxis(direct, 1, 0), jnp.moveaxis(reach_map, 1, 0))

def advance(state_now, piece_terms):
    carried, written, direct, reach_map = piece_terms
    span_out = direct + jnp.einsum('hpd,hde->hpe', reach_map, state_now, precision=highest)
    state_now = jnp.einsum('hde,hef->hdf', carried, state_now, precision=highest) + written
    return (state_now, span_out)

def normalize(outputs, norm_gain):
    tok_count = outputs.shape[0]
    inverse_rms = lax.rsqrt(lax.optimization_barrier(jnp.mean(outputs * outputs, axis=-1, keepdims=True)) + 1e-05)
    return (outputs * inverse_rms * norm_gain.reshape(HEAD_TOTAL, HK)).reshape(tok_count, HEAD_TOTAL * HK).astype(jnp.bfloat16)

def mixer_layer(streams, conv_weight, beta_logit, gate_log, norm_gain, w_out):
    zero_rows = jnp.zeros((CONV - 1, streams.shape[1]), streams.dtype)
    active = mix_taps(jnp.concatenate([zero_rows, streams], axis=0), conv_weight)
    span_parts = span_terms(*head_major(active, beta_logit, gate_log))
    state_start = jnp.zeros((HEAD_TOTAL, HK, HK), jnp.float32)
    _, outputs = lax.scan(advance, state_start, span_parts)
    outputs = outputs.transpose(0, 2, 1, 3).reshape(streams.shape[0], HEAD_TOTAL, HK)
    normed = normalize(outputs, norm_gain)
    return jnp.dot(normed.astype(jnp.float32), w_out.astype(jnp.float32), preferred_element_type=jnp.float32).astype(jnp.bfloat16)

def reference(streams, conv_weight, beta_logit, gate_log, norm_gain, w_out):
    mixed_rows = lax.map(lambda section_args: mixer_layer(*section_args), (streams, conv_weight, beta_logit, gate_log, norm_gain, w_out))
    return jnp.roll(mixed_rows, 1, axis=0)
```

```python
import functools
import jax
import jax.numpy as jnp
from jax import lax
from jax.experimental import pallas as pl
from jax.experimental.pallas import tpu as pltpu
from jax.sharding import PartitionSpec as P

HK = 128
STEPS = 2
CONV = 4
LEVELS = (1, 2, 4, 8, 16, 32)
f32, bf16 = jnp.float32, jnp.bfloat16


def dot(a, b):
    return jnp.dot(a, b, preferred_element_type=f32)


def split(x):
    high = x.astype(bf16)
    return high, (x - high.astype(f32)).astype(bf16)


def dot3(a, b):
    ah, al = split(a)
    bh, bl = split(b)
    return dot(
        jnp.concatenate([ah, ah, al], axis=1), jnp.concatenate([bh, bl, bh], axis=0)
    )


def pair_rows(left, right):
    zero = jnp.zeros_like(left)
    return jnp.concatenate(
        [jnp.concatenate([left, zero], axis=1), jnp.concatenate([zero, right], axis=1)], axis=0
    )


def blockwise(x):
    return pair_rows(x[:, :HK], x[:, HK:])


def pick(table, lane):
    index = lax.broadcasted_iota(jnp.int32, table.shape, 1)
    return jnp.sum(jnp.where(index == lane, table, 0.0), axis=1, keepdims=True)


def terms_kernel(group, heads, *refs):
    xs, rims, taps = refs[0:5], refs[5:10], refs[10:15]
    beta_ref, gate_ref = refs[15:17]
    map_ref, add_ref, direct_ref, reach_ref = refs[17:21]
    ext = refs[21]
    toks = xs[0].shape[0]
    half = toks // 2
    step = pl.program_id(0)

    acts = []
    for part in range(5):
        ext[part, 8 - (CONV - 1) : 8] = rims[part][...].astype(f32)
        ext[part, 8:] = xs[part][...].astype(f32)
        total = None
        for tap in range(CONV):
            low = 8 - (CONV - 1) + tap
            term = taps[part][tap : tap + 1].astype(f32) * ext[part, low : low + toks]
            total = term if total is None else total + term
        acts.append(total * (1.0 / (1.0 + jnp.exp(-total))))

    virt = lax.broadcasted_iota(jnp.int32, (2 * half, toks), 0)
    tok = lax.broadcasted_iota(jnp.int32, (2 * half, toks), 1)
    virt_t = lax.broadcasted_iota(jnp.int32, (toks, 2 * half), 1)
    tok_t = lax.broadcasted_iota(jnp.int32, (toks, 2 * half), 0)
    gates = gate_ref[...]
    gates_t = gates.T
    steps = 1.0 / (1.0 + jnp.exp(-beta_ref[...]))
    sums, sums_t = [], []
    for u in range(2):
        inside = (tok >= u * half) & (tok - u * half <= virt % half)
        inside_t = (tok_t >= u * half) & (tok_t - u * half <= virt_t % half)
        sums.append(
            jnp.dot(inside.astype(f32), gates, precision=lax.Precision.HIGHEST, preferred_element_type=f32)
        )
        sums_t.append(
            jnp.dot(gates_t, inside_t.astype(f32), precision=lax.Precision.HIGHEST, preferred_element_type=f32)
        )

    size = 2 * half
    row = lax.broadcasted_iota(jnp.int32, (size, size), 0)
    col = lax.broadcasted_iota(jnp.int32, (size, size), 1)
    row_tok, col_tok = row % half, col % half
    strict = (col_tok < row_tok) | ((col_tok == row_tok) & (col < row))
    upto = (col_tok <= row_tok)[:half]
    eye = (row == col).astype(f32)
    same = row_tok == col_tok
    twice = lambda x: jnp.concatenate([x, x], axis=1)
    level_masks = [
        twice(
            ((row_tok // (2 * b)) == (col_tok // (2 * b)))
            & ((row_tok // b) % 2 == 1)
            & ((col_tok // b) % 2 == 0)
        )
        for b in LEVELS
    ]

    rows_of = lambda x, u: x[u * half : (u + 1) * half]
    work = []
    for i in range(group):
        head = step * group + i
        lanes = slice(i * HK, (i + 1) * HK)
        unit = lambda x: x * lax.rsqrt(jnp.sum(x * x, axis=-1, keepdims=True) + 1e-06)
        q = unit(acts[0][:, lanes])
        k0, k1 = unit(acts[1][:, lanes]), unit(acts[2][:, lanes])
        v0, v1 = acts[3][:, lanes], acts[4][:, lanes]
        b0, b1 = pick(steps, head), pick(steps, heads + head)
        for u in range(2):
            keys = jnp.concatenate([rows_of(k0, u), rows_of(k1, u)], axis=0)
            vals = jnp.concatenate([rows_of(v0, u), rows_of(v1, u)], axis=0)
            size_col = jnp.concatenate([rows_of(b0, u), rows_of(b1, u)], axis=0)
            c_col = pick(sums[u], head)
            index = lax.broadcasted_iota(jnp.int32, sums_t[u].shape, 0)
            c_row = jnp.sum(jnp.where(index == head, sums_t[u], 0.0), axis=0, keepdims=True)
            c_end = c_col[half - 1 : half]
            queries = rows_of(q, u)
            keys_t = keys.T
            gram = dot3(jnp.concatenate([keys, queries], axis=0), keys_t)
            damp = jnp.exp(jnp.minimum(c_col[:half] - c_row, 0.0))
            lower = jnp.where(
                strict, size_col * jnp.concatenate([damp, damp], axis=0) * gram[:size], 0.0
            )
            scores = jnp.where(upto, damp * gram[size:], 0.0)
            grown = jnp.exp(c_col)
            right = jnp.concatenate([size_col * vals, (size_col * grown) * keys], axis=1)
            to_end_t = keys_t * jnp.exp(c_end - c_row)
            outer = jnp.concatenate([to_end_t, scores], axis=0)
            work.append((lower, right, outer, queries * grown[:half], jnp.exp(c_end) * eye))

    lows, invs = [], []
    for i in range(group):
        low = jnp.concatenate([work[2 * i][0], work[2 * i + 1][0]], axis=1)
        lows.append(low.astype(bf16))
        invs.append((twice(eye) - jnp.where(twice(same), low, 0.0)).astype(bf16))
    for mask in level_masks:
        inner = [
            dot(jnp.where(mask, lows[i], jnp.zeros_like(lows[i])), blockwise(invs[i])).astype(bf16)
            for i in range(group)
        ]
        invs = [
            invs[i] - dot(invs[i], blockwise(inner[i])).astype(bf16) for i in range(group)
        ]

    results = []
    for i in range(group):
        for u in range(2):
            lower, right, outer, reach0, map0 = work[2 * i + u]
            inv = invs[i][:, u * HK : (u + 1) * HK]
            first = dot(inv, right.astype(bf16))
            rest = right - first - dot3(lower, first)
            solved = first + dot(inv, rest.astype(bf16))
            both = dot3(outer, solved)
            results.append(
                (
                    map0 - both[:size, HK:],
                    both[:size, :HK],
                    both[size:, :HK],
                    reach0 - both[size:, HK:],
                )
            )
    for i in range(group):
        map1, add1, direct1, reach1 = results[2 * i]
        map2, add2, direct2, reach2 = results[2 * i + 1]
        joined = dot3(
            jnp.concatenate([map2, reach2], axis=0), jnp.concatenate([map1, add1], axis=1)
        )
        lanes = slice(i * HK, (i + 1) * HK)
        map_ref[i] = joined[:size, :HK]
        add_ref[i] = joined[:size, HK:] + add2
        direct_ref[:half, lanes] = direct1
        direct_ref[half:, lanes] = joined[size:, HK:] + direct2
        reach_ref[:half, lanes] = reach1
        reach_ref[half:, lanes] = joined[size:, :HK]


def shard_terms(streams, rim, conv_weight, beta_logit, gate_log, group=4):
    toks, channels = streams.shape
    heads = gate_log.shape[1]
    width = group * HK
    blocks = heads // group
    spec = lambda rows, part: pl.BlockSpec((rows, width), lambda g, part=part: (0, part * blocks + g))
    whole = lambda x: pl.BlockSpec(x.shape, lambda g: (0,) * x.ndim)
    flops = 60 * heads * 2 * 128 * 128 * 256
    return pl.pallas_call(
        functools.partial(terms_kernel, group, heads),
        grid=(blocks,),
        in_specs=[spec(toks, p) for p in range(5)]
        + [spec(rim.shape[0], p) for p in range(5)]
        + [spec(conv_weight.shape[0], p) for p in range(5)]
        + [whole(beta_logit), whole(gate_log)],
        out_specs=[
            pl.BlockSpec((group, HK, HK), lambda g: (g, 0, 0)),
            pl.BlockSpec((group, HK, HK), lambda g: (g, 0, 0)),
            pl.BlockSpec((toks, width), lambda g: (0, g)),
            pl.BlockSpec((toks, width), lambda g: (0, g)),
        ],
        out_shape=[
            jax.ShapeDtypeStruct((heads, HK, HK), f32),
            jax.ShapeDtypeStruct((heads, HK, HK), f32),
            jax.ShapeDtypeStruct((toks, heads * HK), f32),
            jax.ShapeDtypeStruct((toks, heads * HK), f32),
        ],
        scratch_shapes=[pltpu.VMEM((5, 8 + toks, width), f32)],
        compiler_params=pltpu.CompilerParams(vmem_limit_bytes=48 * 2**20),
        cost_estimate=pl.CostEstimate(flops=flops, bytes_accessed=4 * 2**20, transcendentals=0),
    )(*[streams] * 5, *[rim] * 5, *[conv_weight] * 5, beta_logit, gate_log)


def hand_on_kernel(map_ref, add_ref, state_ref, out_ref):
    for head in range(map_ref.shape[0]):
        high, low = split(map_ref[head])
        state = state_ref[head]
        grown = dot(
            jnp.concatenate([high, low], axis=1), jnp.concatenate([state, state], axis=0)
        )
        out_ref[head] = (grown + add_ref[head]).astype(bf16)


def hand_on(total_map, total_add, state):
    heads = total_map.shape[0]
    return pl.pallas_call(
        hand_on_kernel,
        out_shape=jax.ShapeDtypeStruct(state.shape, bf16),
        compiler_params=pltpu.CompilerParams(vmem_limit_bytes=16 * 2**20),
        cost_estimate=pl.CostEstimate(
            flops=4 * heads * HK**3, bytes_accessed=heads * HK * HK * 12, transcendentals=0
        ),
    )(total_map, total_add, state)


def project_kernel(count, *refs):
    states = refs[: count - 1]
    direct_ref, reach_ref, gain_ref, own_ref = refs[count - 1 : count + 3]
    rights = refs[count + 3 : 2 * count + 2]
    lefts = refs[2 * count + 2 : 3 * count + 1]
    out_ref, slots, sems = refs[3 * count + 1 :]
    mine = lax.axis_index("ctx")
    heads = states[0].shape[0]
    cols = own_ref.shape[1]

    def copy(source, slot):
        return pltpu.make_async_copy(source, slots.at[slot], sems.at[slot])

    copy(own_ref, 0).start()
    for turn in range(1, count):
        pl.when(mine >= turn)(lambda: copy(rights[turn - 1], turn).start())
        pl.when(mine < turn)(lambda: copy(lefts[count - turn - 1], turn).start())
    parts = []
    for head in range(heads):
        lanes = slice(head * HK, (head + 1) * HK)
        state = states[0][head]
        for other in states[1:]:
            state = state + other[head]
        high, low = split(reach_ref[:, lanes])
        out = direct_ref[:, lanes] + dot(
            jnp.concatenate([high, low], axis=1), jnp.concatenate([state, state], axis=0)
        )
        inverse = lax.rsqrt(jnp.mean(out * out, axis=-1, keepdims=True) + 1e-05)
        parts.append((out * inverse * gain_ref[:, lanes]).astype(bf16))
    normed = jnp.concatenate(parts, axis=1)
    for turn in range(count):
        copy(own_ref, turn).wait()
        owner = lax.rem(mine + count - turn, count)
        place = pl.ds(pl.multiple_of(owner * cols, HK), cols)
        out_ref[:, place] = dot(normed, slots[turn]).astype(bf16)


def project(states, direct, reach, gain, own, rights, lefts):
    count = len(states) + 1
    toks, width = direct.shape
    cols = own.shape[1]
    vmem = pl.BlockSpec(memory_space=pltpu.VMEM)
    hbm = pl.BlockSpec(memory_space=pl.ANY)
    return pl.pallas_call(
        functools.partial(project_kernel, count),
        in_specs=[vmem] * (count - 1) + [vmem] * 3 + [hbm] * (2 * count - 1),
        out_specs=vmem,
        out_shape=jax.ShapeDtypeStruct((toks, count * cols), bf16),
        scratch_shapes=[
            pltpu.VMEM((count, width, cols), bf16),
            pltpu.SemaphoreType.DMA((count,)),
        ],
        compiler_params=pltpu.CompilerParams(vmem_limit_bytes=32 * 2**20),
        cost_estimate=pl.CostEstimate(
            flops=2 * toks * width * count * cols,
            bytes_accessed=2 * width * count * cols,
            transcendentals=0,
        ),
    )(*states, direct, reach, gain, own, *rights, *lefts)


def moved(value, pairs):
    return lax.ppermute(value, "ctx", pairs)


def on_device(streams, conv_weight, beta_logit, gate_log, norm_gain, w_out):
    count = lax.axis_size("ctx")
    toks = streams.shape[1]
    rim = moved(streams[0, toks - (CONV - 1) :], [(c, c + 1) for c in range(count - 1)])
    rights, lefts = [w_out[0]], [w_out[0]]
    for turn in range(1, count):
        rights.append(moved(rights[-1], [(c, c + 1) for c in range(turn - 1, count - 1)]))
        lefts.append(moved(lefts[-1], [(c, c - 1) for c in range(1, count - turn + 1)]))
    total_map, total_add, direct, reach = shard_terms(
        streams[0], rim, conv_weight[0], beta_logit[0], gate_log[0]
    )
    states = [moved(total_add.astype(bf16), [(0, 1)])]
    for turn in range(1, count - 1):
        states.append(moved(hand_on(total_map, total_add, states[-1]), [(turn, turn + 1)]))
    mixed = project(states, direct, reach, norm_gain, w_out[0], rights[1:], lefts[1:])
    sections = lax.axis_size("section")
    return lax.ppermute(
        mixed[None], "section", [(s, (s + 1) % sections) for s in range(sections)]
    )


def solution(mesh):
    placed = (
        P("section", "ctx", None),
        P("section", None, None),
        P("section", "ctx", None),
        P("section", "ctx", None),
        P("section", None),
        P("section", None, "ctx"),
    )
    return jax.shard_map(
        on_device, mesh=mesh, in_specs=placed, out_specs=P("section", "ctx", None), check_vma=False
    )
```

```python
import functools
import jax
import jax.numpy as jnp
from jax import lax
from jax.experimental import pallas as pl
from jax.experimental.pallas import tpu as pltpu
from jax.sharding import PartitionSpec as P

HK = 128
STEPS = 2
CONV = 4
LEVELS = (1, 2, 4, 8, 16, 32)
f32, bf16 = jnp.float32, jnp.bfloat16


def dot(a, b):
    return jnp.dot(a, b, preferred_element_type=f32)


def split(x):
    high = x.astype(bf16)
    return high, (x - high.astype(f32)).astype(bf16)


def dot3(a, b):
    ah, al = split(a)
    bh, bl = split(b)
    return dot(
        jnp.concatenate([ah, ah, al], axis=1), jnp.concatenate([bh, bl, bh], axis=0)
    )


def pair_rows(left, right):
    zero = jnp.zeros_like(left)
    return jnp.concatenate(
        [jnp.concatenate([left, zero], axis=1), jnp.concatenate([zero, right], axis=1)], axis=0
    )


def blockwise(x):
    return pair_rows(x[:, :HK], x[:, HK:])


def pick(table, lane):
    index = lax.broadcasted_iota(jnp.int32, table.shape, 1)
    return jnp.sum(jnp.where(index == lane, table, 0.0), axis=1, keepdims=True)


def half_terms(u, heads, half, acts, beta_t, gate_t):
    size, toks = STEPS * half, 2 * half
    virt = lax.broadcasted_iota(jnp.int32, (size, toks), 0)
    tok = lax.broadcasted_iota(jnp.int32, (size, toks), 1)
    inside = ((tok >= u * half) & (tok - u * half <= virt % half)).astype(f32)
    exact = dict(precision=lax.Precision.HIGHEST, preferred_element_type=f32)
    over_lanes = (((1,), (1,)), ((), ()))
    sums = lax.dot_general(inside, gate_t, over_lanes, **exact)
    sums_t = lax.dot_general(gate_t, inside, over_lanes, **exact)
    steps = (1.0 / (1.0 + jnp.exp(-beta_t))).T[u * half : (u + 1) * half]

    row = lax.broadcasted_iota(jnp.int32, (size, size), 0)
    col = lax.broadcasted_iota(jnp.int32, (size, size), 1)
    row_tok, col_tok = row % half, col % half
    strict = (col_tok < row_tok) | ((col_tok == row_tok) & (col < row))
    upto = (col_tok <= row_tok)[:half]
    eye = (row == col).astype(f32)
    same = row_tok == col_tok
    twice = lambda x: jnp.concatenate([x, x], axis=1)
    level_masks = [
        twice(
            ((row_tok // (2 * b)) == (col_tok // (2 * b)))
            & ((row_tok // b) % 2 == 1)
            & ((col_tok // b) % 2 == 0)
        )
        for b in LEVELS
    ]

    work = []
    for head in range(heads):
        lanes = slice(head * HK, (head + 1) * HK)
        unit = lambda x: x * lax.rsqrt(jnp.sum(x * x, axis=-1, keepdims=True) + 1e-06)
        queries = unit(acts[0][:, lanes])
        keys = unit(jnp.concatenate([acts[1][:, lanes], acts[2][:, lanes]], axis=0))
        vals = jnp.concatenate([acts[3][:, lanes], acts[4][:, lanes]], axis=0)
        size_col = jnp.concatenate([pick(steps, head), pick(steps, heads + head)], axis=0)
        c_col = pick(sums, head)
        c_row = sums_t[head : head + 1]
        c_end = c_col[half - 1 : half]
        keys_t = keys.T
        gram = dot3(jnp.concatenate([keys, queries], axis=0), keys_t)
        damp = jnp.exp(jnp.minimum(c_col[:half] - c_row, 0.0))
        lower = jnp.where(
            strict, size_col * jnp.concatenate([damp, damp], axis=0) * gram[:size], 0.0
        )
        scores = jnp.where(upto, damp * gram[size:], 0.0)
        grown = jnp.exp(c_col)
        right = jnp.concatenate([size_col * vals, (size_col * grown) * keys], axis=1)
        to_end_t = keys_t * jnp.exp(c_end - c_row)
        outer = jnp.concatenate([to_end_t, scores], axis=0)
        work.append((lower, right, outer, queries * grown[:half], jnp.exp(c_end) * eye))

    pairs = range(heads // 2)
    lows, invs = [], []
    for i in pairs:
        low = jnp.concatenate([work[2 * i][0], work[2 * i + 1][0]], axis=1)
        lows.append(low.astype(bf16))
        invs.append((twice(eye) - jnp.where(twice(same), low, 0.0)).astype(bf16))
    for mask in level_masks:
        inner = [
            dot(jnp.where(mask, lows[i], jnp.zeros_like(lows[i])), blockwise(invs[i])).astype(bf16)
            for i in pairs
        ]
        invs = [invs[i] - dot(invs[i], blockwise(inner[i])).astype(bf16) for i in pairs]

    results = []
    for head in range(heads):
        lower, right, outer, reach0, map0 = work[head]
        inv = invs[head // 2][:, head % 2 * HK : (head % 2 + 1) * HK]
        first = dot(inv, right.astype(bf16))
        rest = right - first - dot3(lower, first)
        solved = first + dot(inv, rest.astype(bf16))
        both = dot3(outer, solved)
        results.append(
            (
                map0 - both[:size, HK:],
                both[:size, :HK],
                both[size:, :HK],
                reach0 - both[size:, HK:],
            )
        )
    return results


def activations(ext, taps_ref, half, heads):
    width = heads * HK
    acts = []
    for part in range(5):
        lanes = slice(part * width, (part + 1) * width)
        total = None
        for tap in range(CONV):
            low = 8 - (CONV - 1) + tap
            term = taps_ref[tap : tap + 1, lanes].astype(f32) * ext[low : low + half, lanes]
            total = term if total is None else total + term
        acts.append(total * (1.0 / (1.0 + jnp.exp(-total))))
    return acts


def later_kernel(x_ref, taps_ref, beta_ref, gate_ref, map_ref, add_ref, direct_ref, reach_ref, ext):
    heads, toks = gate_ref.shape
    half = toks // 2
    ext[...] = x_ref[half - 16 :].astype(f32)[8:]
    acts = activations(ext, taps_ref, half, heads)
    found = half_terms(1, heads, half, acts, beta_ref[...], gate_ref[...])
    for head, (map2, add2, direct2, reach2) in enumerate(found):
        lanes = slice(head * HK, (head + 1) * HK)
        map_ref[head] = map2
        add_ref[head] = add2
        direct_ref[:, lanes] = direct2
        reach_ref[:, lanes] = reach2


def earlier_kernel(
    x_ref, rim_ref, taps_ref, beta_ref, gate_ref, map2_ref, add2_ref, direct2_ref, reach2_ref,
    map_ref, add_ref, sent_ref, direct_ref, reach_ref, ext,
):
    heads, toks = gate_ref.shape
    half = toks // 2
    ext[8 - (CONV - 1) : 8] = rim_ref[...].astype(f32)
    ext[8:] = x_ref[:half].astype(f32)
    acts = activations(ext, taps_ref, half, heads)
    found = half_terms(0, heads, half, acts, beta_ref[...], gate_ref[...])
    for head, (map1, add1, direct1, reach1) in enumerate(found):
        lanes = slice(head * HK, (head + 1) * HK)
        joined = dot3(
            jnp.concatenate([map2_ref[head], reach2_ref[:, lanes]], axis=0),
            jnp.concatenate([map1, add1], axis=1),
        )
        total = joined[:HK, HK:] + add2_ref[head]
        map_ref[head] = joined[:HK, :HK]
        add_ref[head] = total
        sent_ref[head] = total.astype(bf16)
        direct_ref[:half, lanes] = direct1
        direct_ref[half:, lanes] = joined[HK:, HK:] + direct2_ref[:, lanes]
        reach_ref[:half, lanes] = reach1
        reach_ref[half:, lanes] = joined[HK:, :HK]


def shard_terms(streams, rim, conv_weight, beta_t, gate_t):
    toks, channels = streams.shape
    heads = gate_t.shape[0]
    half = toks // 2
    vmem = pl.BlockSpec(memory_space=pltpu.VMEM)
    shape = jax.ShapeDtypeStruct
    square = (heads, HK, HK)
    params = dict(
        scratch_shapes=[pltpu.VMEM((8 + half, channels), f32)],
        compiler_params=pltpu.CompilerParams(vmem_limit_bytes=40 * 2**20),
        cost_estimate=pl.CostEstimate(
            flops=30 * heads * HK**3 * 2, bytes_accessed=4 * 2**20, transcendentals=0
        ),
    )
    later = pl.pallas_call(
        later_kernel,
        in_specs=[vmem] * 4,
        out_specs=[vmem] * 4,
        out_shape=[shape(square, f32)] * 2 + [shape((half, heads * HK), f32)] * 2,
        **params,
    )(streams, conv_weight, beta_t, gate_t)
    return pl.pallas_call(
        earlier_kernel,
        in_specs=[vmem] * 9,
        out_specs=[vmem] * 5,
        out_shape=[shape(square, f32)] * 2
        + [shape(square, bf16)]
        + [shape((toks, heads * HK), f32)] * 2,
        **params,
    )(streams, rim, conv_weight, beta_t, gate_t, *later)


def hand_on_kernel(map_ref, add_ref, state_ref, out_ref):
    for head in range(map_ref.shape[0]):
        high, low = split(map_ref[head])
        state = state_ref[head]
        grown = dot(
            jnp.concatenate([high, low], axis=1), jnp.concatenate([state, state], axis=0)
        )
        out_ref[head] = (grown + add_ref[head]).astype(bf16)


def hand_on(total_map, total_add, state):
    heads = total_map.shape[0]
    return pl.pallas_call(
        hand_on_kernel,
        out_shape=jax.ShapeDtypeStruct(state.shape, bf16),
        compiler_params=pltpu.CompilerParams(vmem_limit_bytes=16 * 2**20),
        cost_estimate=pl.CostEstimate(
            flops=4 * heads * HK**3, bytes_accessed=heads * HK * HK * 12, transcendentals=0
        ),
    )(total_map, total_add, state)


def project_kernel(count, *refs):
    states = refs[: count - 1]
    direct_ref, reach_ref, gain_ref, own_ref = refs[count - 1 : count + 3]
    rights = refs[count + 3 : 2 * count + 2]
    lefts = refs[2 * count + 2 : 3 * count + 1]
    out_ref, slots, sems = refs[3 * count + 1 :]
    mine = lax.axis_index("ctx")
    heads = states[0].shape[0]
    cols = own_ref.shape[1]

    def copy(source, slot):
        return pltpu.make_async_copy(source, slots.at[slot], sems.at[slot])

    copy(own_ref, 0).start()
    for turn in range(1, count):
        pl.when(mine >= turn)(lambda: copy(rights[turn - 1], turn).start())
        pl.when(mine < turn)(lambda: copy(lefts[count - turn - 1], turn).start())
    parts = []
    for head in range(heads):
        lanes = slice(head * HK, (head + 1) * HK)
        state = states[0][head]
        for other in states[1:]:
            state = state + other[head]
        high, low = split(reach_ref[:, lanes])
        out = direct_ref[:, lanes] + dot(
            jnp.concatenate([high, low], axis=1), jnp.concatenate([state, state], axis=0)
        )
        inverse = lax.rsqrt(jnp.mean(out * out, axis=-1, keepdims=True) + 1e-05)
        parts.append((out * inverse * gain_ref[:, lanes]).astype(bf16))
    normed = jnp.concatenate(parts, axis=1)
    for turn in range(count):
        copy(own_ref, turn).wait()
        owner = lax.rem(mine + count - turn, count)
        place = pl.ds(pl.multiple_of(owner * cols, HK), cols)
        out_ref[:, place] = dot(normed, slots[turn]).astype(bf16)


def project(states, direct, reach, gain, own, rights, lefts):
    count = len(states) + 1
    toks, width = direct.shape
    cols = own.shape[1]
    vmem = pl.BlockSpec(memory_space=pltpu.VMEM)
    hbm = pl.BlockSpec(memory_space=pl.ANY)
    return pl.pallas_call(
        functools.partial(project_kernel, count),
        in_specs=[vmem] * (count - 1) + [vmem] * 3 + [hbm] * (2 * count - 1),
        out_specs=vmem,
        out_shape=jax.ShapeDtypeStruct((toks, count * cols), bf16),
        scratch_shapes=[
            pltpu.VMEM((count, width, cols), bf16),
            pltpu.SemaphoreType.DMA((count,)),
        ],
        compiler_params=pltpu.CompilerParams(vmem_limit_bytes=32 * 2**20),
        cost_estimate=pl.CostEstimate(
            flops=2 * toks * width * count * cols,
            bytes_accessed=2 * width * count * cols,
            transcendentals=0,
        ),
    )(*states, direct, reach, gain, own, *rights, *lefts)


def norm_kernel(direct_ref, reach_ref, gain_ref, *refs):
    states, out_ref = refs[:-1], refs[-1]
    for head in range(states[0].shape[0]):
        lanes = slice(head * HK, (head + 1) * HK)
        state = states[0][head]
        for other in states[1:]:
            state = state + other[head]
        high, low = split(reach_ref[:, lanes])
        out = direct_ref[:, lanes] + dot(
            jnp.concatenate([high, low], axis=1), jnp.concatenate([state, state], axis=0)
        )
        inverse = lax.rsqrt(jnp.mean(out * out, axis=-1, keepdims=True) + 1e-05)
        out_ref[:, lanes] = (out * inverse * gain_ref[:, lanes]).astype(bf16)


def normalize(direct, reach, gain, states):
    vmem = pl.BlockSpec(memory_space=pltpu.VMEM)
    return pl.pallas_call(
        norm_kernel,
        in_specs=[vmem] * (3 + len(states)),
        out_specs=vmem,
        out_shape=jax.ShapeDtypeStruct(direct.shape, bf16),
        compiler_params=pltpu.CompilerParams(vmem_limit_bytes=16 * 2**20),
        cost_estimate=pl.CostEstimate(
            flops=4 * direct.size * HK, bytes_accessed=10 * direct.size, transcendentals=0
        ),
    )(direct, reach, gain, *states)


def own_columns_kernel(rows_ref, own_ref, left_ref, right_ref, two_ref, one_ref):
    mine = lax.axis_index("ctx")
    rows = rows_ref[...]
    cols = own_ref.shape[1]
    two_ref[:, :cols] = dot(rows, own_ref[...]).astype(bf16)

    @pl.when(mine < 2)
    def _():
        two_ref[:, cols:] = dot(rows, right_ref[...]).astype(bf16)
        one_ref[...] = dot(rows, left_ref[...]).astype(bf16)

    @pl.when(mine >= 2)
    def _():
        two_ref[:, cols:] = dot(rows, left_ref[...]).astype(bf16)
        one_ref[...] = dot(rows, right_ref[...]).astype(bf16)


def others_columns_kernel(far_ref, near_ref, own_ref, left_ref, right_ref, two_ref, one_ref):
    mine = lax.axis_index("ctx")
    cols = own_ref.shape[1]
    far = far_ref[...]
    two_ref[:, :cols] = dot(far, own_ref[...]).astype(bf16)

    @pl.when(mine < 2)
    def _():
        two_ref[:, cols:] = dot(far, left_ref[...]).astype(bf16)
        one_ref[...] = dot(near_ref[...], left_ref[...]).astype(bf16)

    @pl.when(mine >= 2)
    def _():
        two_ref[:, cols:] = dot(far, right_ref[...]).astype(bf16)
        one_ref[...] = dot(near_ref[...], right_ref[...]).astype(bf16)


def columns(kernel, rows, own, left, right):
    vmem = pl.BlockSpec(memory_space=pltpu.VMEM)
    toks, cols = rows[0].shape[0], own.shape[1]
    return pl.pallas_call(
        kernel,
        in_specs=[vmem] * (len(rows) + 3),
        out_specs=[vmem] * 2,
        out_shape=[
            jax.ShapeDtypeStruct((toks, 2 * cols), bf16),
            jax.ShapeDtypeStruct((toks, cols), bf16),
        ],
        compiler_params=pltpu.CompilerParams(vmem_limit_bytes=32 * 2**20),
        cost_estimate=pl.CostEstimate(
            flops=6 * own.size * toks, bytes_accessed=8 * own.size, transcendentals=0
        ),
    )(*rows, own, left, right)


def assemble_kernel(own_two, own_one, far_two, near_one, out_ref, sems):
    mine = lax.axis_index("ctx")
    cols = own_one.shape[1]
    first, second = pl.ds(0, cols), pl.ds(cols, cols)
    sources = (
        (own_two.at[:, first], own_two.at[:, second], far_two.at[:, first], far_two.at[:, second]),
        (own_one, own_two.at[:, first], own_two.at[:, second], near_one),
        (near_one, own_two.at[:, second], own_two.at[:, first], own_one),
        (far_two.at[:, second], far_two.at[:, first], own_two.at[:, second], own_two.at[:, first]),
    )
    for place, blocks in enumerate(sources):

        @pl.when(mine == place)
        def _():
            copies = [
                pltpu.make_async_copy(
                    block, out_ref.at[:, pl.ds(index * cols, cols)], sems.at[index]
                )
                for index, block in enumerate(blocks)
            ]
            for copy in copies:
                copy.start()
            for copy in copies:
                copy.wait()


def assemble(parts):
    vmem = pl.BlockSpec(memory_space=pltpu.VMEM)
    toks, cols = parts[1].shape
    return pl.pallas_call(
        assemble_kernel,
        in_specs=[vmem] * 4,
        out_specs=pl.BlockSpec(memory_space=pl.ANY),
        out_shape=jax.ShapeDtypeStruct((toks, 4 * cols), bf16),
        scratch_shapes=[pltpu.SemaphoreType.DMA((4,))],
        cost_estimate=pl.CostEstimate(
            flops=0, bytes_accessed=16 * toks * cols, transcendentals=0
        ),
    )(*parts)


def moved(value, pairs):
    return lax.ppermute(value, "ctx", pairs)


def handed(value, pairs):
    sections, count = lax.axis_size("section"), lax.axis_size("ctx")
    return lax.ppermute(
        value,
        ("section", "ctx"),
        [
            (s * count + a, (s + 1) % sections * count + b)
            for s in range(sections)
            for a, b in pairs
        ],
    )


def on_device(streams, conv_weight, beta_logit, gate_log, norm_gain, w_out):
    count = lax.axis_size("ctx")
    toks = streams.shape[1]
    rim = moved(streams[0, toks - (CONV - 1) :], [(c, c + 1) for c in range(count - 1)])
    own = w_out[0]
    rights = [moved(own, [(c, c + 1) for c in range(count - 1)])]
    lefts = [moved(own, [(c, c - 1) for c in range(1, count)])]
    if count != 4:
        for turn in range(2, count):
            rights.append(moved(rights[-1], [(c, c + 1) for c in range(turn - 1, count - 1)]))
            lefts.append(moved(lefts[-1], [(c, c - 1) for c in range(1, count - turn + 1)]))
    total_map, total_add, sent, direct, reach = shard_terms(
        streams[0], rim, conv_weight[0], beta_logit[0].T, gate_log[0].T
    )
    states = [moved(sent, [(0, 1)])]
    for turn in range(1, count - 1):
        states.append(moved(hand_on(total_map, total_add, states[-1]), [(turn, turn + 1)]))
    if count != 4:
        mixed = project(states, direct, reach, norm_gain, own, rights, lefts)
        return handed(mixed, [(c, c) for c in range(count)])[None]
    early = normalize(direct, reach, norm_gain, states[:-1])
    near = moved(early, [(1, 2), (2, 1)])
    normed = normalize(direct, reach, norm_gain, states)
    far = moved(normed, [(0, 2), (3, 1)])
    own_two, own_one = columns(own_columns_kernel, [normed], own, rights[0], lefts[0])
    far_two, near_one = columns(others_columns_kernel, [far, near], own, rights[0], lefts[0])
    return assemble(
        [
            handed(own_two, [(c, c) for c in range(4)]),
            handed(own_one, [(1, 1), (2, 2)]),
            handed(far_two, [(1, 3), (2, 0)]),
            handed(near_one, [(1, 2), (2, 1)]),
        ]
    )[None]


def solution(mesh):
    placed = (
        P("section", "ctx", None),
        P("section", None, None),
        P("section", "ctx", None),
        P("section", "ctx", None),
        P("section", None),
        P("section", None, "ctx"),
    )
    return jax.shard_map(
        on_device, mesh=mesh, in_specs=placed, out_specs=P("section", "ctx", None), check_vma=False
    )
```

```python
import functools
import jax
import jax.numpy as jnp
from jax import lax
from jax.experimental import pallas as pl
from jax.experimental.pallas import tpu as pltpu
from jax.sharding import PartitionSpec as P

HK = 128
STEPS = 2
CONV = 4
LEVELS = (1, 2, 4, 8, 16, 32)
f32, bf16 = jnp.float32, jnp.bfloat16


def dot(a, b):
    return jnp.dot(a, b, preferred_element_type=f32)


def split(x):
    high = x.astype(bf16)
    return high, (x - high.astype(f32)).astype(bf16)


def dot3(a, b):
    ah, al = split(a)
    bh, bl = split(b)
    return dot(
        jnp.concatenate([ah, ah, al], axis=1), jnp.concatenate([bh, bl, bh], axis=0)
    )


def pair_rows(left, right):
    zero = jnp.zeros_like(left)
    return jnp.concatenate(
        [jnp.concatenate([left, zero], axis=1), jnp.concatenate([zero, right], axis=1)], axis=0
    )


def blockwise(x):
    return pair_rows(x[:, :HK], x[:, HK:])


def pick(table, lane):
    index = lax.broadcasted_iota(jnp.int32, table.shape, 1)
    return jnp.sum(jnp.where(index == lane, table, 0.0), axis=1, keepdims=True)


def half_terms(u, heads, half, acts, beta_t, gate_t):
    size, toks = STEPS * half, 2 * half
    virt = lax.broadcasted_iota(jnp.int32, (size, toks), 0)
    tok = lax.broadcasted_iota(jnp.int32, (size, toks), 1)
    inside = ((tok >= u * half) & (tok - u * half <= virt % half)).astype(f32)
    exact = dict(precision=lax.Precision.HIGHEST, preferred_element_type=f32)
    over_lanes = (((1,), (1,)), ((), ()))
    sums = lax.dot_general(inside, gate_t, over_lanes, **exact)
    sums_t = lax.dot_general(gate_t, inside, over_lanes, **exact)
    steps = (1.0 / (1.0 + jnp.exp(-beta_t))).T[u * half : (u + 1) * half]

    row = lax.broadcasted_iota(jnp.int32, (size, size), 0)
    col = lax.broadcasted_iota(jnp.int32, (size, size), 1)
    row_tok, col_tok = row % half, col % half
    strict = (col_tok < row_tok) | ((col_tok == row_tok) & (col < row))
    upto = (col_tok <= row_tok)[:half]
    eye = (row == col).astype(f32)
    same = row_tok == col_tok
    twice = lambda x: jnp.concatenate([x, x], axis=1)
    level_masks = [
        twice(
            ((row_tok // (2 * b)) == (col_tok // (2 * b)))
            & ((row_tok // b) % 2 == 1)
            & ((col_tok // b) % 2 == 0)
        )
        for b in LEVELS
    ]

    work = []
    for head in range(heads):
        lanes = slice(head * HK, (head + 1) * HK)
        unit = lambda x: x * lax.rsqrt(jnp.sum(x * x, axis=-1, keepdims=True) + 1e-06)
        queries = unit(acts[0][:, lanes])
        keys = unit(jnp.concatenate([acts[1][:, lanes], acts[2][:, lanes]], axis=0))
        vals = jnp.concatenate([acts[3][:, lanes], acts[4][:, lanes]], axis=0)
        size_col = jnp.concatenate([pick(steps, head), pick(steps, heads + head)], axis=0)
        c_col = pick(sums, head)
        c_row = sums_t[head : head + 1]
        c_end = c_col[half - 1 : half]
        keys_t = keys.T
        gram = dot3(jnp.concatenate([keys, queries], axis=0), keys_t)
        damp = jnp.exp(jnp.minimum(c_col[:half] - c_row, 0.0))
        lower = jnp.where(
            strict, size_col * jnp.concatenate([damp, damp], axis=0) * gram[:size], 0.0
        )
        scores = jnp.where(upto, damp * gram[size:], 0.0)
        grown = jnp.exp(c_col)
        right = jnp.concatenate([size_col * vals, (size_col * grown) * keys], axis=1)
        to_end_t = keys_t * jnp.exp(c_end - c_row)
        outer = jnp.concatenate([to_end_t, scores], axis=0)
        work.append((lower, right, outer, queries * grown[:half], jnp.exp(c_end) * eye))

    pairs = range(heads // 2)
    lows, invs = [], []
    for i in pairs:
        low = jnp.concatenate([work[2 * i][0], work[2 * i + 1][0]], axis=1)
        lows.append(low.astype(bf16))
        invs.append((twice(eye) - jnp.where(twice(same), low, 0.0)).astype(bf16))
    for mask in level_masks:
        inner = [
            dot(jnp.where(mask, lows[i], jnp.zeros_like(lows[i])), blockwise(invs[i])).astype(bf16)
            for i in pairs
        ]
        invs = [invs[i] - dot(invs[i], blockwise(inner[i])).astype(bf16) for i in pairs]

    results = []
    for head in range(heads):
        lower, right, outer, reach0, map0 = work[head]
        inv = invs[head // 2][:, head % 2 * HK : (head % 2 + 1) * HK]
        first = dot(inv, right.astype(bf16))
        rest = right - first - dot3(lower, first)
        solved = first + dot(inv, rest.astype(bf16))
        both = dot3(outer, solved)
        results.append(
            (
                map0 - both[:size, HK:],
                both[:size, :HK],
                both[size:, :HK],
                reach0 - both[size:, HK:],
            )
        )
    return results


def activations(ext, taps_ref, half, heads):
    width = heads * HK
    acts = []
    for part in range(5):
        lanes = slice(part * width, (part + 1) * width)
        total = None
        for tap in range(CONV):
            low = 8 - (CONV - 1) + tap
            term = taps_ref[tap : tap + 1, lanes].astype(f32) * ext[low : low + half, lanes]
            total = term if total is None else total + term
        acts.append(total * (1.0 / (1.0 + jnp.exp(-total))))
    return acts


def terms_kernel(
    x_hbm, rim_ref, taps_hbm, beta_hbm, gate_hbm,
    map_ref, add_ref, sent_ref, direct_ref, reach_ref, both_ref,
    x_ref, taps_ref, beta_ref, gate_ref, ext, sems,
):
    copies = [
        pltpu.make_async_copy(source, target, sems.at[index])
        for index, (source, target) in enumerate(
            ((x_hbm, x_ref), (taps_hbm, taps_ref), (beta_hbm, beta_ref), (gate_hbm, gate_ref))
        )
    ]
    for copy in copies:
        copy.start()
    for copy in copies:
        copy.wait()
    heads, toks = gate_ref.shape
    half = toks // 2
    ext[0] = x_ref[half - 16 :].astype(f32)[8:]
    ext[1, 8 - (CONV - 1) : 8] = rim_ref[...].astype(f32)
    ext[1, 8:] = x_ref[:half].astype(f32)
    later, earlier = (
        half_terms(
            u, heads, half, activations(ext.at[1 - u], taps_ref, half, heads), beta_ref[...], gate_ref[...]
        )
        for u in (1, 0)
    )
    for head in range(heads):
        lanes = slice(head * HK, (head + 1) * HK)
        map1, add1, direct1, reach1 = earlier[head]
        map2, add2, direct2, reach2 = later[head]
        joined = dot3(
            jnp.concatenate([map2, reach2], axis=0), jnp.concatenate([map1, add1], axis=1)
        )
        total = joined[:HK, HK:] + add2
        direct2 = joined[HK:, HK:] + direct2
        reach2 = joined[HK:, :HK]
        map_ref[head] = joined[:HK, :HK]
        add_ref[head] = total
        sent_ref[head] = total.astype(bf16)
        for rows, direct, reach in (
            (slice(0, half), direct1, reach1),
            (slice(half, toks), direct2, reach2),
        ):
            direct_ref[rows, lanes] = direct
            reach_ref[rows, lanes] = reach
            both_ref[0, rows, lanes] = direct.astype(bf16)
            both_ref[1, rows, lanes] = reach.astype(bf16)


def shard_terms(streams, rim, conv_weight, beta_t, gate_t):
    toks, channels = streams.shape
    heads = gate_t.shape[0]
    half = toks // 2
    vmem = pl.BlockSpec(memory_space=pltpu.VMEM)
    hbm = pl.BlockSpec(memory_space=pl.ANY)
    shape = jax.ShapeDtypeStruct
    square, rows = (heads, HK, HK), (toks, heads * HK)
    return pl.pallas_call(
        terms_kernel,
        in_specs=[hbm, vmem, hbm, hbm, hbm],
        out_specs=[vmem] * 6,
        out_shape=[
            shape(square, f32),
            shape(square, f32),
            shape(square, bf16),
            shape(rows, f32),
            shape(rows, f32),
            shape((2,) + rows, bf16),
        ],
        scratch_shapes=[
            pltpu.VMEM(streams.shape, bf16),
            pltpu.VMEM(conv_weight.shape, bf16),
            pltpu.VMEM(beta_t.shape, f32),
            pltpu.VMEM(gate_t.shape, f32),
            pltpu.VMEM((2, 8 + half, channels), f32),
            pltpu.SemaphoreType.DMA((4,)),
        ],
        compiler_params=pltpu.CompilerParams(vmem_limit_bytes=44 * 2**20),
        cost_estimate=pl.CostEstimate(
            flops=60 * heads * HK**3 * 2, bytes_accessed=4 * 2**20, transcendentals=0
        ),
    )(streams, rim, conv_weight, beta_t, gate_t)


def hand_on_kernel(map_ref, add_ref, state_ref, out_ref):
    for head in range(map_ref.shape[0]):
        high, low = split(map_ref[head])
        state = state_ref[head]
        grown = dot(
            jnp.concatenate([high, low], axis=1), jnp.concatenate([state, state], axis=0)
        )
        out_ref[head] = (grown + add_ref[head]).astype(bf16)


def hand_on(total_map, total_add, state):
    heads = total_map.shape[0]
    return pl.pallas_call(
        hand_on_kernel,
        out_shape=jax.ShapeDtypeStruct(state.shape, bf16),
        compiler_params=pltpu.CompilerParams(vmem_limit_bytes=16 * 2**20),
        cost_estimate=pl.CostEstimate(
            flops=4 * heads * HK**3, bytes_accessed=heads * HK * HK * 12, transcendentals=0
        ),
    )(total_map, total_add, state)


def project_kernel(count, *refs):
    states = refs[: count - 1]
    direct_ref, reach_ref, gain_ref, own_ref = refs[count - 1 : count + 3]
    rights = refs[count + 3 : 2 * count + 2]
    lefts = refs[2 * count + 2 : 3 * count + 1]
    out_ref, slots, sems = refs[3 * count + 1 :]
    mine = lax.axis_index("ctx")
    heads = states[0].shape[0]
    cols = own_ref.shape[1]

    def copy(source, slot):
        return pltpu.make_async_copy(source, slots.at[slot], sems.at[slot])

    copy(own_ref, 0).start()
    for turn in range(1, count):
        pl.when(mine >= turn)(lambda: copy(rights[turn - 1], turn).start())
        pl.when(mine < turn)(lambda: copy(lefts[count - turn - 1], turn).start())
    parts = []
    for head in range(heads):
        lanes = slice(head * HK, (head + 1) * HK)
        state = states[0][head]
        for other in states[1:]:
            state = state + other[head]
        high, low = split(reach_ref[:, lanes])
        out = direct_ref[:, lanes] + dot(
            jnp.concatenate([high, low], axis=1), jnp.concatenate([state, state], axis=0)
        )
        inverse = lax.rsqrt(jnp.mean(out * out, axis=-1, keepdims=True) + 1e-05)
        parts.append((out * inverse * gain_ref[:, lanes]).astype(bf16))
    normed = jnp.concatenate(parts, axis=1)
    for turn in range(count):
        copy(own_ref, turn).wait()
        owner = lax.rem(mine + count - turn, count)
        place = pl.ds(pl.multiple_of(owner * cols, HK), cols)
        out_ref[:, place] = dot(normed, slots[turn]).astype(bf16)


def project(states, direct, reach, gain, own, rights, lefts):
    count = len(states) + 1
    toks, width = direct.shape
    cols = own.shape[1]
    vmem = pl.BlockSpec(memory_space=pltpu.VMEM)
    hbm = pl.BlockSpec(memory_space=pl.ANY)
    return pl.pallas_call(
        functools.partial(project_kernel, count),
        in_specs=[vmem] * (count - 1) + [vmem] * 3 + [hbm] * (2 * count - 1),
        out_specs=vmem,
        out_shape=jax.ShapeDtypeStruct((toks, count * cols), bf16),
        scratch_shapes=[
            pltpu.VMEM((count, width, cols), bf16),
            pltpu.SemaphoreType.DMA((count,)),
        ],
        compiler_params=pltpu.CompilerParams(vmem_limit_bytes=32 * 2**20),
        cost_estimate=pl.CostEstimate(
            flops=2 * toks * width * count * cols,
            bytes_accessed=2 * width * count * cols,
            transcendentals=0,
        ),
    )(*states, direct, reach, gain, own, *rights, *lefts)


def normed_rows(direct, reach, state, gain):
    out = direct + dot(reach, state)
    return (out * lax.rsqrt(jnp.mean(out * out, axis=-1, keepdims=True) + 1e-05) * gain).astype(bf16)


def normed_kernel(
    map_ref, add_ref, direct_ref, reach_ref, gain_ref, both_ref, first_ref, second_ref,
    own_ref, next_ref, sent_ref,
):
    mine = lax.axis_index("ctx")
    for head in range(map_ref.shape[0]):
        lanes = slice(head * HK, (head + 1) * HK)
        gain = gain_ref[:, lanes]
        state = first_ref[head] + second_ref[head]
        twice = jnp.concatenate([state, state], axis=0)
        halves = lambda x: jnp.concatenate(split(x), axis=1)
        own_ref[:, lanes] = normed_rows(direct_ref[:, lanes], halves(reach_ref[:, lanes]), twice, gain)
        left = (dot(halves(map_ref[head]), twice) + add_ref[head]).astype(bf16)
        next_ref[:, lanes] = normed_rows(both_ref[0, :, lanes].astype(f32), both_ref[1, :, lanes], left, gain)

    @pl.when(mine == 2)
    def _():
        sent_ref[...] = next_ref[...]

    @pl.when(mine != 2)
    def _():
        sent_ref[...] = own_ref[...]


def normed(*operands):
    vmem = pl.BlockSpec(memory_space=pltpu.VMEM)
    direct = operands[2]
    return pl.pallas_call(
        normed_kernel,
        in_specs=[vmem] * 8,
        out_specs=[vmem] * 3,
        out_shape=[jax.ShapeDtypeStruct(direct.shape, bf16)] * 3,
        compiler_params=pltpu.CompilerParams(vmem_limit_bytes=16 * 2**20),
        cost_estimate=pl.CostEstimate(
            flops=10 * direct.size * HK, bytes_accessed=16 * direct.size, transcendentals=0
        ),
    )(*operands)


def near_columns_kernel(
    own_rows, next_rows, own_ref, left_ref, right_ref, own_two, next_two, one_ref
):
    mine = lax.axis_index("ctx")
    cols = own_ref.shape[1]
    first, second = slice(0, cols), slice(cols, 2 * cols)

    def put(out_ref, where, rows, weight):
        out_ref[:, where] = dot(rows[...], weight[...]).astype(bf16)

    @pl.when(mine < 3)
    def _():
        put(own_two, first, own_rows, own_ref)
        put(own_two, second, own_rows, right_ref)

    @pl.when(mine == 1)
    def _():
        put(next_two, first, next_rows, left_ref)
        put(next_two, second, next_rows, own_ref)
        put(one_ref, first, own_rows, left_ref)

    @pl.when(mine == 2)
    def _():
        put(next_two, first, next_rows, own_ref)
        put(next_two, second, next_rows, right_ref)
        put(one_ref, first, next_rows, left_ref)


def far_columns_kernel(rows_ref, own_ref, left_ref, right_ref, one_ref, last_ref):
    mine = lax.axis_index("ctx")

    @pl.when(mine == 2)
    def _():
        one_ref[...] = dot(rows_ref[...], right_ref[...]).astype(bf16)

    @pl.when(mine != 2)
    def _():
        one_ref[...] = dot(rows_ref[...], left_ref[...]).astype(bf16)

    @pl.when(mine == 3)
    def _():
        last_ref[...] = dot(rows_ref[...], own_ref[...]).astype(bf16)


def columns(kernel, rows, widths, own, left, right):
    vmem = pl.BlockSpec(memory_space=pltpu.VMEM)
    toks, cols = rows[0].shape[0], own.shape[1]
    return pl.pallas_call(
        kernel,
        in_specs=[vmem] * (len(rows) + 3),
        out_specs=[vmem] * len(widths),
        out_shape=[jax.ShapeDtypeStruct((toks, width * cols), bf16) for width in widths],
        compiler_params=pltpu.CompilerParams(vmem_limit_bytes=32 * 2**20),
        cost_estimate=pl.CostEstimate(
            flops=2 * sum(widths) * own.size * toks, bytes_accessed=6 * own.size, transcendentals=0
        ),
    )(*rows, own, left, right)


def assemble_kernel(own_two, next_two, one, far_one, far_last, out_ref, sems):
    mine = lax.axis_index("ctx")
    cols = one.shape[1]
    block = lambda ref, index: ref.at[:, pl.ds(index * cols, cols)]
    sources = (
        (block(own_two, 0), block(own_two, 1), far_one, far_last),
        (one, block(own_two, 0), block(own_two, 1), far_one),
        (block(next_two, 0), block(next_two, 1), block(own_two, 0), block(own_two, 1)),
        (far_one, one, block(next_two, 0), block(next_two, 1)),
    )
    for place, blocks in enumerate(sources):

        @pl.when(mine == place)
        def _():
            copies = [
                pltpu.make_async_copy(source, block(out_ref, index), sems.at[index])
                for index, source in enumerate(blocks)
            ]
            for copy in copies:
                copy.start()
            for copy in copies:
                copy.wait()


def assemble(*parts):
    hbm = pl.BlockSpec(memory_space=pl.ANY)
    toks, cols = parts[-1].shape
    return pl.pallas_call(
        assemble_kernel,
        in_specs=[hbm] * len(parts),
        out_specs=hbm,
        out_shape=jax.ShapeDtypeStruct((toks, 4 * cols), bf16),
        scratch_shapes=[pltpu.SemaphoreType.DMA((4,))],
        cost_estimate=pl.CostEstimate(
            flops=0, bytes_accessed=16 * toks * cols, transcendentals=0
        ),
    )(*parts)


def moved(value, pairs):
    return lax.ppermute(value, "ctx", pairs)


def handed(value, pairs):
    sections, count = lax.axis_size("section"), lax.axis_size("ctx")
    return lax.ppermute(
        value,
        ("section", "ctx"),
        [
            (s * count + a, (s + 1) % sections * count + b)
            for s in range(sections)
            for a, b in pairs
        ],
    )


def on_device(streams, conv_weight, beta_logit, gate_log, norm_gain, w_out):
    count = lax.axis_size("ctx")
    toks = streams.shape[1]
    rim = moved(streams[0, toks - (CONV - 1) :], [(c, c + 1) for c in range(count - 1)])
    rim, own = lax.optimization_barrier((rim, w_out[0]))
    rights = [moved(own, [(c, c + 1) for c in range(count - 1)])]
    lefts = [moved(own, [(c, c - 1) for c in range(1, count)])]
    if count != 4:
        for turn in range(2, count):
            rights.append(moved(rights[-1], [(c, c + 1) for c in range(turn - 1, count - 1)]))
            lefts.append(moved(lefts[-1], [(c, c - 1) for c in range(1, count - turn + 1)]))
    total_map, total_add, sent, direct, reach, both = shard_terms(
        streams[0], rim, conv_weight[0], beta_logit[0].T, gate_log[0].T
    )
    if count != 4:
        states = [moved(sent, [(0, 1)])]
        for turn in range(1, count - 1):
            states.append(moved(hand_on(total_map, total_add, states[-1]), [(turn, turn + 1)]))
        mixed = project(states, direct, reach, norm_gain, own, rights, lefts)
        return handed(mixed, [(c, c) for c in range(count)])[None]
    weights = (own, rights[0], lefts[0])
    first = moved(sent, [(0, 1)])
    both = moved(both, [(3, 2), (2, 1)])
    second = moved(hand_on(total_map, total_add, first), [(1, 2)])
    own_rows, next_rows, sent_rows = normed(
        total_map, total_add, direct, reach, norm_gain, both, first, second
    )
    far_rows = moved(sent_rows, [(0, 3), (1, 2), (2, 1)])
    own_two, next_two, one = columns(near_columns_kernel, [own_rows, next_rows], (2, 2, 1), *weights)
    far_one, far_last = columns(far_columns_kernel, [far_rows], (1, 1), *weights)
    return assemble(
        handed(own_two, [(0, 0), (1, 1), (2, 2)]),
        handed(next_two, [(1, 2), (2, 3)]),
        handed(one, [(1, 1), (2, 3)]),
        handed(far_one, [(3, 0), (2, 1), (1, 3)]),
        handed(far_last, [(3, 0)]),
    )[None]


def solution(mesh):
    placed = (
        P("section", "ctx", None),
        P("section", None, None),
        P("section", "ctx", None),
        P("section", "ctx", None),
        P("section", None),
        P("section", None, "ctx"),
    )
    return jax.shard_map(
        on_device, mesh=mesh, in_specs=placed, out_specs=P("section", "ctx", None), check_vma=False
    )
```

```python
import functools
import jax
import jax.numpy as jnp
from jax import lax
from jax.experimental import pallas as pl
from jax.experimental.pallas import tpu as pltpu
from jax.sharding import PartitionSpec as P

HK = 128
STEPS = 2
CONV = 4
LEVELS = (1, 2, 4, 8, 16, 32)
f32, bf16 = jnp.float32, jnp.bfloat16


def dot(a, b):
    return jnp.dot(a, b, preferred_element_type=f32)


def split(x):
    high = x.astype(bf16)
    return high, (x - high.astype(f32)).astype(bf16)


def dot3(a, b):
    ah, al = split(a)
    bh, bl = split(b)
    return dot(
        jnp.concatenate([ah, ah, al], axis=1), jnp.concatenate([bh, bl, bh], axis=0)
    )


def pair_rows(left, right):
    zero = jnp.zeros_like(left)
    return jnp.concatenate(
        [jnp.concatenate([left, zero], axis=1), jnp.concatenate([zero, right], axis=1)], axis=0
    )


def blockwise(x):
    return pair_rows(x[:, :HK], x[:, HK:])


def pick(table, lane):
    index = lax.broadcasted_iota(jnp.int32, table.shape, 1)
    return jnp.sum(jnp.where(index == lane, table, 0.0), axis=1, keepdims=True)


def half_terms(u, heads, half, acts, beta_t, gate_t):
    size, toks = STEPS * half, 2 * half
    virt = lax.broadcasted_iota(jnp.int32, (size, toks), 0)
    tok = lax.broadcasted_iota(jnp.int32, (size, toks), 1)
    inside = ((tok >= u * half) & (tok - u * half <= virt % half)).astype(f32)
    exact = dict(precision=lax.Precision.HIGHEST, preferred_element_type=f32)
    over_lanes = (((1,), (1,)), ((), ()))
    sums = lax.dot_general(inside, gate_t, over_lanes, **exact)
    sums_t = lax.dot_general(gate_t, inside, over_lanes, **exact)
    steps = (1.0 / (1.0 + jnp.exp(-beta_t))).T[u * half : (u + 1) * half]

    row = lax.broadcasted_iota(jnp.int32, (size, size), 0)
    col = lax.broadcasted_iota(jnp.int32, (size, size), 1)
    row_tok, col_tok = row % half, col % half
    strict = (col_tok < row_tok) | ((col_tok == row_tok) & (col < row))
    upto = (col_tok <= row_tok)[:half]
    eye = (row == col).astype(f32)
    same = row_tok == col_tok
    twice = lambda x: jnp.concatenate([x, x], axis=1)
    level_masks = [
        twice(
            ((row_tok // (2 * b)) == (col_tok // (2 * b)))
            & ((row_tok // b) % 2 == 1)
            & ((col_tok // b) % 2 == 0)
        )
        for b in LEVELS
    ]

    work = []
    for head in range(heads):
        lanes = slice(head * HK, (head + 1) * HK)
        unit = lambda x: x * lax.rsqrt(jnp.sum(x * x, axis=-1, keepdims=True) + 1e-06)
        queries = unit(acts[0][:, lanes])
        keys = unit(jnp.concatenate([acts[1][:, lanes], acts[2][:, lanes]], axis=0))
        vals = jnp.concatenate([acts[3][:, lanes], acts[4][:, lanes]], axis=0)
        size_col = jnp.concatenate([pick(steps, head), pick(steps, heads + head)], axis=0)
        c_col = pick(sums, head)
        c_row = sums_t[head : head + 1]
        c_end = c_col[half - 1 : half]
        keys_t = keys.T
        gram = dot3(jnp.concatenate([keys, queries], axis=0), keys_t)
        damp = jnp.exp(jnp.minimum(c_col[:half] - c_row, 0.0))
        lower = jnp.where(
            strict, size_col * jnp.concatenate([damp, damp], axis=0) * gram[:size], 0.0
        )
        scores = jnp.where(upto, damp * gram[size:], 0.0)
        grown = jnp.exp(c_col)
        right = jnp.concatenate([size_col * vals, (size_col * grown) * keys], axis=1)
        to_end_t = keys_t * jnp.exp(c_end - c_row)
        outer = jnp.concatenate([to_end_t, scores], axis=0)
        work.append((lower, right, outer, queries * grown[:half], jnp.exp(c_end) * eye))

    pairs = range(heads // 2)
    lows, invs = [], []
    for i in pairs:
        low = jnp.concatenate([work[2 * i][0], work[2 * i + 1][0]], axis=1)
        lows.append(low.astype(bf16))
        invs.append((twice(eye) - jnp.where(twice(same), low, 0.0)).astype(bf16))
    for mask in level_masks:
        inner = [
            dot(jnp.where(mask, lows[i], jnp.zeros_like(lows[i])), blockwise(invs[i])).astype(bf16)
            for i in pairs
        ]
        invs = [invs[i] - dot(invs[i], blockwise(inner[i])).astype(bf16) for i in pairs]

    results = []
    for head in range(heads):
        lower, right, outer, reach0, map0 = work[head]
        inv = invs[head // 2][:, head % 2 * HK : (head % 2 + 1) * HK]
        first = dot(inv, right.astype(bf16))
        rest = right - first - dot3(lower, first)
        solved = first + dot(inv, rest.astype(bf16))
        both = dot3(outer, solved)
        results.append(
            (
                map0 - both[:size, HK:],
                both[:size, :HK],
                both[size:, :HK],
                reach0 - both[size:, HK:],
            )
        )
    return results


def activations(ext, taps_ref, half, heads):
    width = heads * HK
    acts = []
    for part in range(5):
        lanes = slice(part * width, (part + 1) * width)
        total = None
        for tap in range(CONV):
            low = 8 - (CONV - 1) + tap
            term = taps_ref[tap : tap + 1, lanes].astype(f32) * ext[low : low + half, lanes]
            total = term if total is None else total + term
        acts.append(total * (1.0 / (1.0 + jnp.exp(-total))))
    return acts


def load_kernel(*refs):
    sources, targets, edge_ref, sems = refs[:4], refs[4:8], refs[8], refs[9]
    copies = [
        pltpu.make_async_copy(source, target, sems.at[index])
        for index, (source, target) in enumerate(zip(sources, targets))
    ]
    for copy in copies:
        copy.start()
    for copy in copies:
        copy.wait()
    toks = targets[0].shape[0]
    edge_ref[...] = targets[0][toks - 16 :].astype(f32)[16 - (CONV - 1) :].astype(bf16)


def conv_kernel(x_ref, taps_ref, out_ref, ext):
    half, channels = out_ref.shape
    ext[...] = x_ref[half - 16 :].astype(f32)[8:]
    width = channels // 5
    for part, act in enumerate(activations(ext, taps_ref, half, width // HK)):
        out_ref[:, part * width : (part + 1) * width] = act


def later_kernel(act_ref, beta_ref, gate_ref, map_ref, add_ref, direct_ref, reach_ref):
    heads, toks = gate_ref.shape
    width = heads * HK
    acts = [act_ref[:, part * width : (part + 1) * width] for part in range(5)]
    found = half_terms(1, heads, toks // 2, acts, beta_ref[...], gate_ref[...])
    for head, (map2, add2, direct2, reach2) in enumerate(found):
        lanes = slice(head * HK, (head + 1) * HK)
        map_ref[head] = map2
        add_ref[head] = add2
        direct_ref[:, lanes] = direct2
        reach_ref[:, lanes] = reach2


def earlier_kernel(
    rim_ref, x_ref, taps_ref, beta_ref, gate_ref, map2_ref, add2_ref, direct2_ref, reach2_ref,
    map_ref, add_ref, sent_ref, direct_ref, reach_ref, both_ref, ext,
):
    heads, toks = gate_ref.shape
    half = toks // 2
    ext[8 - (CONV - 1) : 8] = rim_ref[...].astype(f32)
    ext[8:] = x_ref[:half].astype(f32)
    acts = activations(ext, taps_ref, half, heads)
    found = half_terms(0, heads, half, acts, beta_ref[...], gate_ref[...])
    for head, (map1, add1, direct1, reach1) in enumerate(found):
        lanes = slice(head * HK, (head + 1) * HK)
        joined = dot3(
            jnp.concatenate([map2_ref[head], reach2_ref[:, lanes]], axis=0),
            jnp.concatenate([map1, add1], axis=1),
        )
        total = joined[:HK, HK:] + add2_ref[head]
        map_ref[head] = joined[:HK, :HK]
        add_ref[head] = total
        sent_ref[head] = total.astype(bf16)
        for rows, direct, reach in (
            (slice(0, half), direct1, reach1),
            (slice(half, toks), joined[HK:, HK:] + direct2_ref[:, lanes], joined[HK:, :HK]),
        ):
            direct_ref[rows, lanes] = direct
            reach_ref[rows, lanes] = reach
            both_ref[0, rows, lanes] = direct.astype(bf16)
            both_ref[1, rows, lanes] = reach.astype(bf16)


def kernel_call(kernel, operands, out_shapes, limit=16, scratch=(), cost=2**16, space=pltpu.VMEM):
    return pl.pallas_call(
        kernel,
        in_specs=[pl.BlockSpec(memory_space=space)] * len(operands),
        out_specs=[pl.BlockSpec(memory_space=pltpu.VMEM)] * len(out_shapes),
        out_shape=[jax.ShapeDtypeStruct(*shape) for shape in out_shapes],
        scratch_shapes=scratch,
        compiler_params=pltpu.CompilerParams(vmem_limit_bytes=limit * 2**20),
        cost_estimate=pl.CostEstimate(flops=2**20, bytes_accessed=cost, transcendentals=0),
    )(*operands)


def load(*sources):
    sources = [pltpu.with_memory_space_constraint(x, pltpu.HBM) for x in sources]
    edge = ((CONV - 1, sources[0].shape[1]), bf16)
    return pl.pallas_call(
        load_kernel,
        in_specs=[pl.BlockSpec(memory_space=pltpu.HBM)] * len(sources),
        out_specs=[pl.BlockSpec(memory_space=pltpu.VMEM)] * (len(sources) + 1),
        out_shape=[pltpu.VMEM(x.shape, x.dtype) for x in sources] + [pltpu.VMEM(*edge)],
        scratch_shapes=[pltpu.SemaphoreType.DMA((len(sources),))],
        compiler_params=pltpu.CompilerParams(vmem_limit_bytes=2**22),
    )(*sources)


def later_activations(x, taps):
    toks, channels = x.shape
    half = toks // 2
    return kernel_call(
        conv_kernel,
        (x, taps),
        [((half, channels), f32)],
        scratch=[pltpu.VMEM((8 + half, channels), f32)],
        cost=2**27,
    )[0]


def shard_terms(later_acts, rim, x, taps, beta_t, gate_t):
    toks, channels = x.shape
    heads = gate_t.shape[0]
    half = toks // 2
    square, rows, half_rows = (heads, HK, HK), (toks, heads * HK), (half, heads * HK)
    later = kernel_call(
        later_kernel,
        (later_acts, beta_t, gate_t),
        [(square, f32)] * 2 + [(half_rows, f32)] * 2,
        limit=32,
    )
    return kernel_call(
        earlier_kernel,
        (rim, x, taps, beta_t, gate_t, *later),
        [(square, f32)] * 2 + [(square, bf16)] + [(rows, f32)] * 2 + [((2,) + rows, bf16)],
        limit=32,
        scratch=[pltpu.VMEM((8 + half, channels), f32)],
    )


def hand_on_kernel(map_ref, add_ref, state_ref, out_ref):
    for head in range(map_ref.shape[0]):
        high, low = split(map_ref[head])
        state = state_ref[head]
        grown = dot(
            jnp.concatenate([high, low], axis=1), jnp.concatenate([state, state], axis=0)
        )
        out_ref[head] = (grown + add_ref[head]).astype(bf16)


def hand_on(total_map, total_add, state):
    heads = total_map.shape[0]
    return pl.pallas_call(
        hand_on_kernel,
        out_shape=jax.ShapeDtypeStruct(state.shape, bf16),
        compiler_params=pltpu.CompilerParams(vmem_limit_bytes=16 * 2**20),
        cost_estimate=pl.CostEstimate(
            flops=4 * heads * HK**3, bytes_accessed=heads * HK * HK * 12, transcendentals=0
        ),
    )(total_map, total_add, state)


def project_kernel(count, *refs):
    states = refs[: count - 1]
    direct_ref, reach_ref, gain_ref, own_ref = refs[count - 1 : count + 3]
    rights = refs[count + 3 : 2 * count + 2]
    lefts = refs[2 * count + 2 : 3 * count + 1]
    out_ref, slots, sems = refs[3 * count + 1 :]
    mine = lax.axis_index("ctx")
    heads = states[0].shape[0]
    cols = own_ref.shape[1]

    def copy(source, slot):
        return pltpu.make_async_copy(source, slots.at[slot], sems.at[slot])

    copy(own_ref, 0).start()
    for turn in range(1, count):
        pl.when(mine >= turn)(lambda: copy(rights[turn - 1], turn).start())
        pl.when(mine < turn)(lambda: copy(lefts[count - turn - 1], turn).start())
    parts = []
    for head in range(heads):
        lanes = slice(head * HK, (head + 1) * HK)
        state = states[0][head]
        for other in states[1:]:
            state = state + other[head]
        high, low = split(reach_ref[:, lanes])
        out = direct_ref[:, lanes] + dot(
            jnp.concatenate([high, low], axis=1), jnp.concatenate([state, state], axis=0)
        )
        inverse = lax.rsqrt(jnp.mean(out * out, axis=-1, keepdims=True) + 1e-05)
        parts.append((out * inverse * gain_ref[:, lanes]).astype(bf16))
    normed = jnp.concatenate(parts, axis=1)
    for turn in range(count):
        copy(own_ref, turn).wait()
        owner = lax.rem(mine + count - turn, count)
        place = pl.ds(pl.multiple_of(owner * cols, HK), cols)
        out_ref[:, place] = dot(normed, slots[turn]).astype(bf16)


def project(states, direct, reach, gain, own, rights, lefts):
    count = len(states) + 1
    toks, width = direct.shape
    cols = own.shape[1]
    vmem = pl.BlockSpec(memory_space=pltpu.VMEM)
    hbm = pl.BlockSpec(memory_space=pl.ANY)
    return pl.pallas_call(
        functools.partial(project_kernel, count),
        in_specs=[vmem] * (count - 1) + [vmem] * 3 + [hbm] * (2 * count - 1),
        out_specs=vmem,
        out_shape=jax.ShapeDtypeStruct((toks, count * cols), bf16),
        scratch_shapes=[
            pltpu.VMEM((count, width, cols), bf16),
            pltpu.SemaphoreType.DMA((count,)),
        ],
        compiler_params=pltpu.CompilerParams(vmem_limit_bytes=32 * 2**20),
        cost_estimate=pl.CostEstimate(
            flops=2 * toks * width * count * cols,
            bytes_accessed=2 * width * count * cols,
            transcendentals=0,
        ),
    )(*states, direct, reach, gain, own, *rights, *lefts)


def on_shard(place):
    return pl.when(lax.axis_index("ctx") == place)


def head_lanes(heads):
    return [(head, slice(head * HK, (head + 1) * HK)) for head in range(heads)]


def normed_rows(out, gain):
    return (out * lax.rsqrt(jnp.mean(out * out, axis=-1, keepdims=True) + 1e-05) * gain).astype(bf16)


def project_to(out_ref, rows, *weights):
    cols = weights[0].shape[1]
    for index, weight in enumerate(weights):
        out_ref[:, index * cols : (index + 1) * cols] = dot(rows, weight[...]).astype(bf16)


def rows_with_state(direct_ref, reach_ref, gain_ref, state_ref, out_ref):
    for head, lanes in head_lanes(state_ref.shape[0]):
        state = state_ref[head]
        out = direct_ref[:, lanes] + dot(
            jnp.concatenate(split(reach_ref[:, lanes]), axis=1), jnp.concatenate([state, state], axis=0)
        )
        out_ref[:, lanes] = normed_rows(out, gain_ref[:, lanes])


def rows_of_next(both_ref, gain_ref, head, lanes, state):
    out = both_ref[0, :, lanes].astype(f32) + dot(both_ref[1, :, lanes], state)
    return normed_rows(out, gain_ref[:, lanes])


def first_rows_kernel(direct_ref, gain_ref, out_ref):
    @on_shard(0)
    def _():
        for head, lanes in head_lanes(direct_ref.shape[1] // HK):
            out_ref[:, lanes] = normed_rows(direct_ref[:, lanes], gain_ref[:, lanes])


def second_rows_kernel(direct_ref, reach_ref, gain_ref, state_ref, out_ref):
    @on_shard(1)
    def _():
        rows_with_state(direct_ref, reach_ref, gain_ref, state_ref, out_ref)


def third_columns_kernel(both_ref, gain_ref, state_ref, left_ref, out_ref, rows_ref):
    @on_shard(1)
    def _():
        for head, lanes in head_lanes(state_ref.shape[0]):
            rows_ref[:, lanes] = rows_of_next(both_ref, gain_ref, head, lanes, state_ref[head])
        project_to(out_ref, rows_ref[...], left_ref)


def fourth_rows_kernel(map_ref, add_ref, both_ref, gain_ref, state_ref, out_ref):
    @on_shard(2)
    def _():
        for head, lanes in head_lanes(state_ref.shape[0]):
            state = state_ref[head]
            left = add_ref[head] + dot(
                jnp.concatenate(split(map_ref[head]), axis=1), jnp.concatenate([state, state], axis=0)
            )
            out_ref[:, lanes] = rows_of_next(both_ref, gain_ref, head, lanes, left.astype(bf16))


def near_columns_kernel(
    direct_ref, reach_ref, gain_ref, state_ref, rows0_ref, rows1_ref, rows3_ref, own_ref, left_ref, right_ref,
    own_three, next_three, rows_ref,
):
    weights = (own_ref, right_ref, left_ref)

    @on_shard(0)
    def _():
        project_to(own_three, rows0_ref[...], *weights[:2])

    @on_shard(1)
    def _():
        project_to(own_three, rows1_ref[...], *weights)

    @on_shard(2)
    def _():
        project_to(next_three, rows3_ref[...], *weights)
        rows_with_state(direct_ref, reach_ref, gain_ref, state_ref, rows_ref)
        project_to(own_three, rows_ref[...], *weights)


def first_columns_kernel(rows_ref, own_ref, left_ref, out_ref):
    @on_shard(3)
    def _():
        project_to(out_ref, rows_ref[...], left_ref, own_ref)


def far_columns_kernel(rows1_ref, rows3_ref, left_ref, right_ref, out_ref):
    @on_shard(1)
    def _():
        project_to(out_ref, rows3_ref[...], left_ref)

    @on_shard(2)
    def _():
        project_to(out_ref, rows1_ref[...], right_ref)


def call(kernel, operands, out_shapes, scratch=()):
    vmem = pl.BlockSpec(memory_space=pltpu.VMEM)
    shapes = [jax.ShapeDtypeStruct(shape, bf16) for shape in out_shapes]
    found = pl.pallas_call(
        kernel,
        in_specs=[vmem] * len(operands),
        out_specs=[vmem] * len(shapes),
        out_shape=shapes,
        scratch_shapes=[pltpu.VMEM(shape, bf16) for shape in scratch],
        compiler_params=pltpu.CompilerParams(vmem_limit_bytes=16 * 2**20),
        cost_estimate=pl.CostEstimate(flops=2**20, bytes_accessed=2**16, transcendentals=0),
    )(*operands)
    return found if len(shapes) > 1 else found[0]


def assemble_kernel(own_three, next_three, third_one, first_two, far_one, out_ref):
    cols = far_one.shape[1]
    own = [(own_three, index) for index in range(3)]
    after = [(next_three, index) for index in range(3)]
    sources = (
        (own[0], own[1], (first_two, 0), (first_two, 1)),
        (own[2], own[0], own[1], (far_one, 0)),
        ((third_one, 0), own[2], own[0], own[1]),
        ((far_one, 0), after[2], after[0], after[1]),
    )
    for place, blocks in enumerate(sources):

        @on_shard(place)
        def _():
            for index, (ref, block) in enumerate(blocks):
                out_ref[:, index * cols : (index + 1) * cols] = ref[:, block * cols : (block + 1) * cols]


def moved(value, pairs):
    return lax.ppermute(value, "ctx", pairs)


def handed(value, pairs):
    sections, count = lax.axis_size("section"), lax.axis_size("ctx")
    return lax.ppermute(
        value,
        ("section", "ctx"),
        [
            (s * count + a, (s + 1) % sections * count + b)
            for s in range(sections)
            for a, b in pairs
        ],
    )


def on_device(streams, conv_weight, beta_logit, gate_log, norm_gain, w_out):
    count = lax.axis_size("ctx")
    toks, width = streams.shape[1], norm_gain.shape[1]
    x, taps, beta_t, gate_t, edge = load(
        streams[0], conv_weight[0], beta_logit[0].T, gate_log[0].T
    )
    rim = moved(edge, [(c, c + 1) for c in range(count - 1)])
    later_acts = later_activations(x, taps)
    rim, later_acts, own = lax.optimization_barrier((rim, later_acts, w_out[0]))
    rights = [moved(own, [(c, c + 1) for c in range(count - 1)])]
    lefts = [moved(own, [(c, c - 1) for c in range(1, count)])]
    if count != 4:
        for turn in range(2, count):
            rights.append(moved(rights[-1], [(c, c + 1) for c in range(turn - 1, count - 1)]))
            lefts.append(moved(lefts[-1], [(c, c - 1) for c in range(1, count - turn + 1)]))
    total_map, total_add, sent, direct, reach, both = shard_terms(
        later_acts, rim, x, taps, beta_t, gate_t
    )
    if count != 4:
        states = [moved(sent, [(0, 1)])]
        for turn in range(1, count - 1):
            states.append(moved(hand_on(total_map, total_add, states[-1]), [(turn, turn + 1)]))
        mixed = project(states, direct, reach, norm_gain, own, rights, lefts)
        return handed(mixed, [(c, c) for c in range(count)])[None]

    left, right = rights[0], lefts[0]
    cols = own.shape[1]
    rows = (toks, width)
    one, two, three = ((toks, blocks * cols) for blocks in (1, 2, 3))
    first = moved(sent, [(0, 1)])
    both = moved(both, [(3, 2), (2, 1)])
    rows0 = call(first_rows_kernel, [direct, norm_gain], [rows])
    far0 = moved(rows0, [(0, 3)])
    first, far0 = lax.optimization_barrier((first, far0))
    out1 = hand_on(total_map, total_add, first)
    second = moved(out1, [(1, 2)])
    rows1 = call(second_rows_kernel, [direct, reach, norm_gain, first], [rows])
    far1 = moved(rows1, [(1, 2)])
    third_one = call(third_columns_kernel, [both, norm_gain, out1, left], [one], [rows])
    first_two = call(first_columns_kernel, [far0, own, left], [two])
    third_one, first_two, rows1 = lax.optimization_barrier((third_one, first_two, rows1))
    third_one, first_two = handed(third_one, [(1, 2)]), handed(first_two, [(3, 0)])
    rows3 = call(fourth_rows_kernel, [total_map, total_add, both, norm_gain, second], [rows])
    far3 = moved(rows3, [(2, 1)])
    own_three, next_three = call(
        near_columns_kernel,
        [direct, reach, norm_gain, second, rows0, rows1, rows3, own, left, right],
        [three, three],
        [rows],
    )
    far_one = call(far_columns_kernel, [far1, far3, left, right], [one])
    return call(
        assemble_kernel,
        [
            handed(own_three, [(0, 0), (1, 1), (2, 2)]),
            handed(next_three, [(2, 3)]),
            third_one,
            first_two,
            handed(far_one, [(2, 1), (1, 3)]),
        ],
        [(toks, 4 * cols)],
    )[None]


def solution(mesh):
    placed = (
        P("section", "ctx", None),
        P("section", None, None),
        P("section", "ctx", None),
        P("section", "ctx", None),
        P("section", None),
        P("section", None, "ctx"),
    )
    return jax.shard_map(
        on_device, mesh=mesh, in_specs=placed, out_specs=P("section", "ctx", None), check_vma=False
    )
```

```python
import functools
import jax
import jax.numpy as jnp
from jax import lax
from jax.experimental import pallas as pl
from jax.experimental.pallas import tpu as pltpu
from jax.sharding import PartitionSpec as P

HK = 128
STEPS = 2
CONV = 4
LEVELS = (1, 2, 4, 8, 16, 32)
f32, bf16 = jnp.float32, jnp.bfloat16


def dot(a, b):
    return jnp.dot(a, b, preferred_element_type=f32)


def split(x):
    high = x.astype(bf16)
    return high, (x - high.astype(f32)).astype(bf16)


def dot3(a, b):
    ah, al = split(a)
    bh, bl = split(b)
    return dot(
        jnp.concatenate([ah, ah, al], axis=1), jnp.concatenate([bh, bl, bh], axis=0)
    )


def pair_rows(left, right):
    zero = jnp.zeros_like(left)
    return jnp.concatenate(
        [jnp.concatenate([left, zero], axis=1), jnp.concatenate([zero, right], axis=1)], axis=0
    )


def blockwise(x):
    return pair_rows(x[:, :HK], x[:, HK:])


def pick(table, lane):
    index = lax.broadcasted_iota(jnp.int32, table.shape, 1)
    return jnp.sum(jnp.where(index == lane, table, 0.0), axis=1, keepdims=True)


def half_terms(u, heads, half, acts, beta_t, gate_t):
    size, toks = STEPS * half, 2 * half
    virt = lax.broadcasted_iota(jnp.int32, (size, toks), 0)
    tok = lax.broadcasted_iota(jnp.int32, (size, toks), 1)
    inside = ((tok >= u * half) & (tok - u * half <= virt % half)).astype(f32)
    exact = dict(precision=lax.Precision.HIGHEST, preferred_element_type=f32)
    over_lanes = (((1,), (1,)), ((), ()))
    sums = lax.dot_general(inside, gate_t, over_lanes, **exact)
    sums_t = lax.dot_general(gate_t, inside, over_lanes, **exact)
    steps = (1.0 / (1.0 + jnp.exp(-beta_t))).T[u * half : (u + 1) * half]

    row = lax.broadcasted_iota(jnp.int32, (size, size), 0)
    col = lax.broadcasted_iota(jnp.int32, (size, size), 1)
    row_tok, col_tok = row % half, col % half
    strict = (col_tok < row_tok) | ((col_tok == row_tok) & (col < row))
    upto = (col_tok <= row_tok)[:half]
    eye = (row == col).astype(f32)
    same = row_tok == col_tok
    twice = lambda x: jnp.concatenate([x, x], axis=1)
    level_masks = [
        twice(
            ((row_tok // (2 * b)) == (col_tok // (2 * b)))
            & ((row_tok // b) % 2 == 1)
            & ((col_tok // b) % 2 == 0)
        )
        for b in LEVELS
    ]

    work = []
    for head in range(heads):
        lanes = slice(head * HK, (head + 1) * HK)
        unit = lambda x: x * lax.rsqrt(jnp.sum(x * x, axis=-1, keepdims=True) + 1e-06)
        queries = unit(acts[0][:, lanes])
        keys = unit(jnp.concatenate([acts[1][:, lanes], acts[2][:, lanes]], axis=0))
        vals = jnp.concatenate([acts[3][:, lanes], acts[4][:, lanes]], axis=0)
        size_col = jnp.concatenate([pick(steps, head), pick(steps, heads + head)], axis=0)
        c_col = pick(sums, head)
        c_row = sums_t[head : head + 1]
        c_end = c_col[half - 1 : half]
        keys_t = keys.T
        gram = dot3(jnp.concatenate([keys, queries], axis=0), keys_t)
        damp = jnp.exp(jnp.minimum(c_col[:half] - c_row, 0.0))
        lower = jnp.where(
            strict, size_col * jnp.concatenate([damp, damp], axis=0) * gram[:size], 0.0
        )
        scores = jnp.where(upto, damp * gram[size:], 0.0)
        grown = jnp.exp(c_col)
        right = jnp.concatenate([size_col * vals, (size_col * grown) * keys], axis=1)
        to_end_t = keys_t * jnp.exp(c_end - c_row)
        outer = jnp.concatenate([to_end_t, scores], axis=0)
        work.append((lower, right, outer, queries * grown[:half], jnp.exp(c_end) * eye))

    pairs = range(heads // 2)
    lows, invs = [], []
    for i in pairs:
        low = jnp.concatenate([work[2 * i][0], work[2 * i + 1][0]], axis=1)
        lows.append(low.astype(bf16))
        invs.append((twice(eye) - jnp.where(twice(same), low, 0.0)).astype(bf16))
    for mask in level_masks:
        inner = [
            dot(jnp.where(mask, lows[i], jnp.zeros_like(lows[i])), blockwise(invs[i])).astype(bf16)
            for i in pairs
        ]
        invs = [invs[i] - dot(invs[i], blockwise(inner[i])).astype(bf16) for i in pairs]

    results = []
    for head in range(heads):
        lower, right, outer, reach0, map0 = work[head]
        inv = invs[head // 2][:, head % 2 * HK : (head % 2 + 1) * HK]
        first = dot(inv, right.astype(bf16))
        rest = right - first - dot3(lower, first)
        solved = first + dot(inv, rest.astype(bf16))
        both = dot3(outer, solved)
        results.append(
            (
                map0 - both[:size, HK:],
                both[:size, :HK],
                both[size:, :HK],
                reach0 - both[size:, HK:],
            )
        )
    return results


def activations(ext, taps_ref, half, heads):
    width = heads * HK
    acts = []
    for part in range(5):
        lanes = slice(part * width, (part + 1) * width)
        total = None
        for tap in range(CONV):
            low = 8 - (CONV - 1) + tap
            term = taps_ref[tap : tap + 1, lanes].astype(f32) * ext[low : low + half, lanes]
            total = term if total is None else total + term
        acts.append(total * (1.0 / (1.0 + jnp.exp(-total))))
    return acts


def load_kernel(*refs):
    sources, targets, edge_ref, sems = refs[:4], refs[4:8], refs[8], refs[9]
    copies = [
        pltpu.make_async_copy(source, target, sems.at[index])
        for index, (source, target) in enumerate(zip(sources, targets))
    ]
    for copy in copies:
        copy.start()
    for copy in copies:
        copy.wait()
    toks = targets[0].shape[0]
    edge_ref[...] = targets[0][toks - 16 :].astype(f32)[16 - (CONV - 1) :].astype(bf16)


def conv_kernel(x_ref, taps_ref, out_ref, ext):
    half, channels = out_ref.shape
    ext[...] = x_ref[half - 16 :].astype(f32)[8:]
    width = channels // 5
    for part, act in enumerate(activations(ext, taps_ref, half, width // HK)):
        out_ref[:, part * width : (part + 1) * width] = act


def later_kernel(act_ref, beta_ref, gate_ref, map_ref, add_ref, direct_ref, reach_ref):
    heads, toks = gate_ref.shape
    width = heads * HK
    acts = [act_ref[:, part * width : (part + 1) * width] for part in range(5)]
    found = half_terms(1, heads, toks // 2, acts, beta_ref[...], gate_ref[...])
    for head, (map2, add2, direct2, reach2) in enumerate(found):
        lanes = slice(head * HK, (head + 1) * HK)
        map_ref[head] = map2
        add_ref[head] = add2
        direct_ref[:, lanes] = direct2
        reach_ref[:, lanes] = reach2


def earlier_kernel(
    rim_ref, x_ref, taps_ref, beta_ref, gate_ref, map2_ref, add2_ref, direct2_ref, reach2_ref,
    map_ref, add_ref, sent_ref, direct_ref, reach_ref, both_ref, ext,
):
    heads, toks = gate_ref.shape
    half = toks // 2
    ext[8 - (CONV - 1) : 8] = rim_ref[...].astype(f32)
    ext[8:] = x_ref[:half].astype(f32)
    acts = activations(ext, taps_ref, half, heads)
    found = half_terms(0, heads, half, acts, beta_ref[...], gate_ref[...])
    for head, (map1, add1, direct1, reach1) in enumerate(found):
        lanes = slice(head * HK, (head + 1) * HK)
        joined = dot3(
            jnp.concatenate([map2_ref[head], reach2_ref[:, lanes]], axis=0),
            jnp.concatenate([map1, add1], axis=1),
        )
        total = joined[:HK, HK:] + add2_ref[head]
        map_ref[head] = joined[:HK, :HK]
        add_ref[head] = total
        sent_ref[head] = total.astype(bf16)
        for rows, direct, reach in (
            (slice(0, half), direct1, reach1),
            (slice(half, toks), joined[HK:, HK:] + direct2_ref[:, lanes], joined[HK:, :HK]),
        ):
            direct_ref[rows, lanes] = direct
            reach_ref[rows, lanes] = reach
            both_ref[0, rows, lanes] = direct.astype(bf16)
            both_ref[1, rows, lanes] = reach.astype(bf16)


def kernel_call(kernel, operands, out_shapes, limit=16, scratch=(), cost=2**16, space=pltpu.VMEM):
    return pl.pallas_call(
        kernel,
        in_specs=[pl.BlockSpec(memory_space=space)] * len(operands),
        out_specs=[pl.BlockSpec(memory_space=pltpu.VMEM)] * len(out_shapes),
        out_shape=[jax.ShapeDtypeStruct(*shape) for shape in out_shapes],
        scratch_shapes=scratch,
        compiler_params=pltpu.CompilerParams(vmem_limit_bytes=limit * 2**20),
        cost_estimate=pl.CostEstimate(flops=2**20, bytes_accessed=cost, transcendentals=0),
    )(*operands)


def load(*sources):
    sources = [pltpu.with_memory_space_constraint(x, pltpu.HBM) for x in sources]
    edge = ((CONV - 1, sources[0].shape[1]), bf16)
    return pl.pallas_call(
        load_kernel,
        in_specs=[pl.BlockSpec(memory_space=pltpu.HBM)] * len(sources),
        out_specs=[pl.BlockSpec(memory_space=pltpu.VMEM)] * (len(sources) + 1),
        out_shape=[pltpu.VMEM(x.shape, x.dtype) for x in sources] + [pltpu.VMEM(*edge)],
        scratch_shapes=[pltpu.SemaphoreType.DMA((len(sources),))],
        compiler_params=pltpu.CompilerParams(vmem_limit_bytes=2**22),
    )(*sources)


def later_activations(x, taps):
    toks, channels = x.shape
    half = toks // 2
    return kernel_call(
        conv_kernel,
        (x, taps),
        [((half, channels), f32)],
        scratch=[pltpu.VMEM((8 + half, channels), f32)],
        cost=2**27,
    )[0]


def shard_terms(later_acts, rim, x, taps, beta_t, gate_t):
    toks, channels = x.shape
    heads = gate_t.shape[0]
    half = toks // 2
    square, rows, half_rows = (heads, HK, HK), (toks, heads * HK), (half, heads * HK)
    later = kernel_call(
        later_kernel,
        (later_acts, beta_t, gate_t),
        [(square, f32)] * 2 + [(half_rows, f32)] * 2,
        limit=32,
    )
    return kernel_call(
        earlier_kernel,
        (rim, x, taps, beta_t, gate_t, *later),
        [(square, f32)] * 2 + [(square, bf16)] + [(rows, f32)] * 2 + [((2,) + rows, bf16)],
        limit=32,
        scratch=[pltpu.VMEM((8 + half, channels), f32)],
    )


def hand_on_kernel(map_ref, add_ref, state_ref, out_ref):
    for head in range(map_ref.shape[0]):
        high, low = split(map_ref[head])
        state = state_ref[head]
        grown = dot(
            jnp.concatenate([high, low], axis=1), jnp.concatenate([state, state], axis=0)
        )
        out_ref[head] = (grown + add_ref[head]).astype(bf16)


def hand_on(total_map, total_add, state):
    heads = total_map.shape[0]
    return pl.pallas_call(
        hand_on_kernel,
        out_shape=jax.ShapeDtypeStruct(state.shape, bf16),
        compiler_params=pltpu.CompilerParams(vmem_limit_bytes=16 * 2**20),
        cost_estimate=pl.CostEstimate(
            flops=4 * heads * HK**3, bytes_accessed=heads * HK * HK * 12, transcendentals=0
        ),
    )(total_map, total_add, state)


def project_kernel(count, *refs):
    states = refs[: count - 1]
    direct_ref, reach_ref, gain_ref, own_ref = refs[count - 1 : count + 3]
    rights = refs[count + 3 : 2 * count + 2]
    lefts = refs[2 * count + 2 : 3 * count + 1]
    out_ref, slots, sems = refs[3 * count + 1 :]
    mine = lax.axis_index("ctx")
    heads = states[0].shape[0]
    cols = own_ref.shape[1]

    def copy(source, slot):
        return pltpu.make_async_copy(source, slots.at[slot], sems.at[slot])

    copy(own_ref, 0).start()
    for turn in range(1, count):
        pl.when(mine >= turn)(lambda: copy(rights[turn - 1], turn).start())
        pl.when(mine < turn)(lambda: copy(lefts[count - turn - 1], turn).start())
    parts = []
    for head in range(heads):
        lanes = slice(head * HK, (head + 1) * HK)
        state = states[0][head]
        for other in states[1:]:
            state = state + other[head]
        high, low = split(reach_ref[:, lanes])
        out = direct_ref[:, lanes] + dot(
            jnp.concatenate([high, low], axis=1), jnp.concatenate([state, state], axis=0)
        )
        inverse = lax.rsqrt(jnp.mean(out * out, axis=-1, keepdims=True) + 1e-05)
        parts.append((out * inverse * gain_ref[:, lanes]).astype(bf16))
    normed = jnp.concatenate(parts, axis=1)
    for turn in range(count):
        copy(own_ref, turn).wait()
        owner = lax.rem(mine + count - turn, count)
        place = pl.ds(pl.multiple_of(owner * cols, HK), cols)
        out_ref[:, place] = dot(normed, slots[turn]).astype(bf16)


def project(states, direct, reach, gain, own, rights, lefts):
    count = len(states) + 1
    toks, width = direct.shape
    cols = own.shape[1]
    vmem = pl.BlockSpec(memory_space=pltpu.VMEM)
    hbm = pl.BlockSpec(memory_space=pl.ANY)
    return pl.pallas_call(
        functools.partial(project_kernel, count),
        in_specs=[vmem] * (count - 1) + [vmem] * 3 + [hbm] * (2 * count - 1),
        out_specs=vmem,
        out_shape=jax.ShapeDtypeStruct((toks, count * cols), bf16),
        scratch_shapes=[
            pltpu.VMEM((count, width, cols), bf16),
            pltpu.SemaphoreType.DMA((count,)),
        ],
        compiler_params=pltpu.CompilerParams(vmem_limit_bytes=32 * 2**20),
        cost_estimate=pl.CostEstimate(
            flops=2 * toks * width * count * cols,
            bytes_accessed=2 * width * count * cols,
            transcendentals=0,
        ),
    )(*states, direct, reach, gain, own, *rights, *lefts)


def on_shard(place):
    return pl.when(lax.axis_index("ctx") == place)


def head_lanes(heads):
    return [(head, slice(head * HK, (head + 1) * HK)) for head in range(heads)]


def normed_rows(out, gain):
    return (out * lax.rsqrt(jnp.mean(out * out, axis=-1, keepdims=True) + 1e-05) * gain).astype(bf16)


def project_to(out_ref, rows, *weights):
    cols = weights[0].shape[1]
    for index, weight in enumerate(weights):
        out_ref[:, index * cols : (index + 1) * cols] = dot(rows, weight[...]).astype(bf16)


def rows_with_state(direct_ref, reach_ref, gain_ref, state_ref, out_ref):
    for head, lanes in head_lanes(state_ref.shape[0]):
        state = state_ref[head]
        out = direct_ref[:, lanes] + dot(
            jnp.concatenate(split(reach_ref[:, lanes]), axis=1), jnp.concatenate([state, state], axis=0)
        )
        out_ref[:, lanes] = normed_rows(out, gain_ref[:, lanes])


def rows_of_next(both_ref, gain_ref, head, lanes, state):
    out = both_ref[0, :, lanes].astype(f32) + dot(both_ref[1, :, lanes], state)
    return normed_rows(out, gain_ref[:, lanes])


def first_rows_kernel(direct_ref, gain_ref, out_ref):
    @on_shard(0)
    def _():
        for head, lanes in head_lanes(direct_ref.shape[1] // HK):
            out_ref[:, lanes] = normed_rows(direct_ref[:, lanes], gain_ref[:, lanes])


def second_rows_kernel(direct_ref, reach_ref, gain_ref, state_ref, out_ref):
    @on_shard(1)
    def _():
        rows_with_state(direct_ref, reach_ref, gain_ref, state_ref, out_ref)


def third_columns_kernel(both_ref, gain_ref, state_ref, pair_ref, out_ref, rows_ref):
    @on_shard(1)
    def _():
        for head, lanes in head_lanes(state_ref.shape[0]):
            rows_ref[:, lanes] = rows_of_next(both_ref, gain_ref, head, lanes, state_ref[head])
        project_to(out_ref, rows_ref[...], pair_ref.at[0])


def fourth_rows_kernel(map_ref, add_ref, both_ref, gain_ref, state_ref, out_ref):
    @on_shard(2)
    def _():
        for head, lanes in head_lanes(state_ref.shape[0]):
            state = state_ref[head]
            left = add_ref[head] + dot(
                jnp.concatenate(split(map_ref[head]), axis=1), jnp.concatenate([state, state], axis=0)
            )
            out_ref[:, lanes] = rows_of_next(both_ref, gain_ref, head, lanes, left.astype(bf16))


def near_columns_kernel(
    direct_ref, reach_ref, gain_ref, state_ref, rows0_ref, rows1_ref, rows3_ref, pair_ref, middle_ref,
    own_three, next_three, rows_ref,
):
    low, high = pair_ref.at[0], pair_ref.at[1]

    @on_shard(0)
    def _():
        project_to(own_three, rows0_ref[...], low, high)

    @on_shard(1)
    def _():
        project_to(own_three, rows1_ref[...], high, middle_ref, low)

    @on_shard(2)
    def _():
        weights = (low, high, middle_ref)
        project_to(next_three, rows3_ref[...], *weights)
        rows_with_state(direct_ref, reach_ref, gain_ref, state_ref, rows_ref)
        project_to(own_three, rows_ref[...], *weights)


def first_columns_kernel(rows_ref, pair_ref, out_ref):
    @on_shard(3)
    def _():
        project_to(out_ref, rows_ref[...], pair_ref.at[0], pair_ref.at[1])


def far_columns_kernel(rows1_ref, rows3_ref, pair_ref, out_ref):
    @on_shard(1)
    def _():
        project_to(out_ref, rows3_ref[...], pair_ref.at[0])

    @on_shard(2)
    def _():
        project_to(out_ref, rows1_ref[...], pair_ref.at[1])


def call(kernel, operands, out_shapes, scratch=()):
    vmem = pl.BlockSpec(memory_space=pltpu.VMEM)
    shapes = [jax.ShapeDtypeStruct(shape, bf16) for shape in out_shapes]
    found = pl.pallas_call(
        kernel,
        in_specs=[vmem] * len(operands),
        out_specs=[vmem] * len(shapes),
        out_shape=shapes,
        scratch_shapes=[pltpu.VMEM(shape, bf16) for shape in scratch],
        compiler_params=pltpu.CompilerParams(vmem_limit_bytes=16 * 2**20),
        cost_estimate=pl.CostEstimate(flops=2**20, bytes_accessed=2**16, transcendentals=0),
    )(*operands)
    return found if len(shapes) > 1 else found[0]


def assemble_kernel(own_three, next_three, third_one, first_two, far_one, out_ref):
    cols = far_one.shape[1]
    own = [(own_three, index) for index in range(3)]
    after = [(next_three, index) for index in range(3)]
    sources = (
        (own[0], own[1], (first_two, 0), (first_two, 1)),
        (own[2], own[0], own[1], (far_one, 0)),
        ((third_one, 0), own[2], own[0], own[1]),
        ((far_one, 0), after[2], after[0], after[1]),
    )
    for place, blocks in enumerate(sources):

        @on_shard(place)
        def _():
            for index, (ref, block) in enumerate(blocks):
                out_ref[:, index * cols : (index + 1) * cols] = ref[:, block * cols : (block + 1) * cols]


def moved(value, pairs):
    return lax.ppermute(value, "ctx", pairs)


def handed(value, pairs):
    sections, count = lax.axis_size("section"), lax.axis_size("ctx")
    return lax.ppermute(
        value,
        ("section", "ctx"),
        [
            (s * count + a, (s + 1) % sections * count + b)
            for s in range(sections)
            for a, b in pairs
        ],
    )


def on_device(streams, conv_weight, beta_logit, gate_log, norm_gain, w_out):
    count = lax.axis_size("ctx")
    toks, width = streams.shape[1], norm_gain.shape[1]
    x, taps, beta_t, gate_t, edge = load(
        streams[0], conv_weight[0], beta_logit[0].T, gate_log[0].T
    )
    rim = moved(edge, [(c, c + 1) for c in range(count - 1)])
    later_acts = later_activations(x, taps)
    own = w_out[0]
    if count == 4:
        pair = lax.all_gather(own, "ctx", axis_index_groups=[[0, 1], [2, 3]])
        rim, later_acts, own = lax.optimization_barrier((rim, later_acts, own))
        middle = moved(own, [(1, 2), (2, 1)])
    else:
        rights, lefts = [own], [own]
        for turn in range(1, count):
            rights.append(moved(rights[-1], [(c, c + 1) for c in range(turn - 1, count - 1)]))
            lefts.append(moved(lefts[-1], [(c, c - 1) for c in range(1, count - turn + 1)]))
    total_map, total_add, sent, direct, reach, both = shard_terms(
        later_acts, rim, x, taps, beta_t, gate_t
    )
    if count != 4:
        states = [moved(sent, [(0, 1)])]
        for turn in range(1, count - 1):
            states.append(moved(hand_on(total_map, total_add, states[-1]), [(turn, turn + 1)]))
        mixed = project(states, direct, reach, norm_gain, own, rights[1:], lefts[1:])
        return handed(mixed, [(c, c) for c in range(count)])[None]

    cols = own.shape[1]
    rows = (toks, width)
    one, two, three = ((toks, blocks * cols) for blocks in (1, 2, 3))
    first = moved(sent, [(0, 1)])
    both = moved(both, [(3, 2), (2, 1)])
    rows0 = call(first_rows_kernel, [direct, norm_gain], [rows])
    far0 = moved(rows0, [(0, 3)])
    out1 = hand_on(total_map, total_add, first)
    second = moved(out1, [(1, 2)])
    rows1 = call(second_rows_kernel, [direct, reach, norm_gain, first], [rows])
    far1 = moved(rows1, [(1, 2)])
    third_one = call(third_columns_kernel, [both, norm_gain, out1, pair], [one], [rows])
    first_two = call(first_columns_kernel, [far0, pair], [two])
    rows3 = call(fourth_rows_kernel, [total_map, total_add, both, norm_gain, second], [rows])
    far3 = moved(rows3, [(2, 1)])
    own_three, next_three = call(
        near_columns_kernel,
        [direct, reach, norm_gain, second, rows0, rows1, rows3, pair, middle],
        [three, three],
        [rows],
    )
    far_one = call(far_columns_kernel, [far1, far3, pair], [one])
    far_one, third_one, first_two = lax.optimization_barrier((far_one, third_one, first_two))
    return call(
        assemble_kernel,
        [
            handed(own_three, [(0, 0), (1, 1), (2, 2)]),
            handed(next_three, [(2, 3)]),
            handed(third_one, [(1, 2)]),
            handed(first_two, [(3, 0)]),
            handed(far_one, [(2, 1), (1, 3)]),
        ],
        [(toks, 4 * cols)],
    )[None]


def solution(mesh):
    placed = (
        P("section", "ctx", None),
        P("section", None, None),
        P("section", "ctx", None),
        P("section", "ctx", None),
        P("section", None),
        P("section", None, "ctx"),
    )
    return jax.shard_map(
        on_device, mesh=mesh, in_specs=placed, out_specs=P("section", "ctx", None), check_vma=False
    )
```

```python
import functools
import jax
import jax.numpy as jnp
from jax import lax
from jax.experimental import pallas as pl
from jax.experimental.pallas import tpu as pltpu
from jax.sharding import PartitionSpec as P

HK = 128
STEPS = 2
CONV = 4
LEVELS = (1, 2, 4, 8, 16, 32)
f32, bf16 = jnp.float32, jnp.bfloat16


def dot(a, b):
    return jnp.dot(a, b, preferred_element_type=f32)


def split(x):
    high = x.astype(bf16)
    return high, (x - high.astype(f32)).astype(bf16)


def dot3(a, b):
    ah, al = split(a)
    bh, bl = split(b)
    return dot(
        jnp.concatenate([ah, ah, al], axis=1), jnp.concatenate([bh, bl, bh], axis=0)
    )


def pair_rows(left, right):
    zero = jnp.zeros_like(left)
    return jnp.concatenate(
        [jnp.concatenate([left, zero], axis=1), jnp.concatenate([zero, right], axis=1)], axis=0
    )


def blockwise(x):
    return pair_rows(x[:, :HK], x[:, HK:])


def pick(table, lane):
    index = lax.broadcasted_iota(jnp.int32, table.shape, 1)
    return jnp.sum(jnp.where(index == lane, table, 0.0), axis=1, keepdims=True)


def half_terms(u, heads, half, acts, beta_t, gate_t):
    size, toks = STEPS * half, 2 * half
    virt = lax.broadcasted_iota(jnp.int32, (size, toks), 0)
    tok = lax.broadcasted_iota(jnp.int32, (size, toks), 1)
    inside = ((tok >= u * half) & (tok - u * half <= virt % half)).astype(f32)
    exact = dict(precision=lax.Precision.HIGHEST, preferred_element_type=f32)
    over_lanes = (((1,), (1,)), ((), ()))
    sums = lax.dot_general(inside, gate_t, over_lanes, **exact)
    sums_t = lax.dot_general(gate_t, inside, over_lanes, **exact)
    steps = (1.0 / (1.0 + jnp.exp(-beta_t))).T[u * half : (u + 1) * half]

    row = lax.broadcasted_iota(jnp.int32, (size, size), 0)
    col = lax.broadcasted_iota(jnp.int32, (size, size), 1)
    row_tok, col_tok = row % half, col % half
    strict = (col_tok < row_tok) | ((col_tok == row_tok) & (col < row))
    upto = (col_tok <= row_tok)[:half]
    eye = (row == col).astype(f32)
    same = row_tok == col_tok
    twice = lambda x: jnp.concatenate([x, x], axis=1)
    level_masks = [
        twice(
            ((row_tok // (2 * b)) == (col_tok // (2 * b)))
            & ((row_tok // b) % 2 == 1)
            & ((col_tok // b) % 2 == 0)
        )
        for b in LEVELS
    ]

    work = []
    for head in range(heads):
        lanes = slice(head * HK, (head + 1) * HK)
        unit = lambda x: x * lax.rsqrt(jnp.sum(x * x, axis=-1, keepdims=True) + 1e-06)
        queries = unit(acts[0][:, lanes])
        keys = unit(jnp.concatenate([acts[1][:, lanes], acts[2][:, lanes]], axis=0))
        vals = jnp.concatenate([acts[3][:, lanes], acts[4][:, lanes]], axis=0)
        size_col = jnp.concatenate([pick(steps, head), pick(steps, heads + head)], axis=0)
        c_col = pick(sums, head)
        c_row = sums_t[head : head + 1]
        c_end = c_col[half - 1 : half]
        keys_t = keys.T
        gram = dot3(jnp.concatenate([keys, queries], axis=0), keys_t)
        damp = jnp.exp(jnp.minimum(c_col[:half] - c_row, 0.0))
        lower = jnp.where(
            strict, size_col * jnp.concatenate([damp, damp], axis=0) * gram[:size], 0.0
        )
        scores = jnp.where(upto, damp * gram[size:], 0.0)
        grown = jnp.exp(c_col)
        right = jnp.concatenate([size_col * vals, (size_col * grown) * keys], axis=1)
        to_end_t = keys_t * jnp.exp(c_end - c_row)
        outer = jnp.concatenate([to_end_t, scores], axis=0)
        work.append((lower, right, outer, queries * grown[:half], jnp.exp(c_end) * eye))

    pairs = range(heads // 2)
    lows, invs = [], []
    for i in pairs:
        low = jnp.concatenate([work[2 * i][0], work[2 * i + 1][0]], axis=1)
        lows.append(low.astype(bf16))
        invs.append((twice(eye) - jnp.where(twice(same), low, 0.0)).astype(bf16))
    for mask in level_masks:
        inner = [
            dot(jnp.where(mask, lows[i], jnp.zeros_like(lows[i])), blockwise(invs[i])).astype(bf16)
            for i in pairs
        ]
        invs = [invs[i] - dot(invs[i], blockwise(inner[i])).astype(bf16) for i in pairs]

    results = []
    for head in range(heads):
        lower, right, outer, reach0, map0 = work[head]
        inv = invs[head // 2][:, head % 2 * HK : (head % 2 + 1) * HK]
        first = dot(inv, right.astype(bf16))
        rest = right - first - dot3(lower, first)
        solved = first + dot(inv, rest.astype(bf16))
        both = dot3(outer, solved)
        results.append(
            (
                map0 - both[:size, HK:],
                both[:size, :HK],
                both[size:, :HK],
                reach0 - both[size:, HK:],
            )
        )
    return results


def activations(ext, taps_ref, half, heads):
    width = heads * HK
    acts = []
    for part in range(5):
        lanes = slice(part * width, (part + 1) * width)
        total = None
        for tap in range(CONV):
            low = 8 - (CONV - 1) + tap
            term = taps_ref[tap : tap + 1, lanes].astype(f32) * ext[low : low + half, lanes]
            total = term if total is None else total + term
        acts.append(total * (1.0 / (1.0 + jnp.exp(-total))))
    return acts


def load_kernel(*refs):
    sources, targets, edge_ref, sems = refs[:4], refs[4:8], refs[8], refs[9]
    copies = [
        pltpu.make_async_copy(source, target, sems.at[index])
        for index, (source, target) in enumerate(zip(sources, targets))
    ]
    for copy in copies:
        copy.start()
    for copy in copies:
        copy.wait()
    toks = targets[0].shape[0]
    edge_ref[...] = targets[0][toks - 16 :].astype(f32)[16 - (CONV - 1) :].astype(bf16)


def conv_kernel(x_ref, taps_ref, out_ref, ext):
    half, channels = out_ref.shape
    ext[...] = x_ref[half - 16 :].astype(f32)[8:]
    width = channels // 5
    for part, act in enumerate(activations(ext, taps_ref, half, width // HK)):
        out_ref[:, part * width : (part + 1) * width] = act


def later_kernel(act_ref, beta_ref, gate_ref, map_ref, add_ref, direct_ref, reach_ref):
    heads, toks = gate_ref.shape
    width = heads * HK
    acts = [act_ref[:, part * width : (part + 1) * width] for part in range(5)]
    found = half_terms(1, heads, toks // 2, acts, beta_ref[...], gate_ref[...])
    for head, (map2, add2, direct2, reach2) in enumerate(found):
        lanes = slice(head * HK, (head + 1) * HK)
        map_ref[head] = map2
        add_ref[head] = add2
        direct_ref[:, lanes] = direct2
        reach_ref[:, lanes] = reach2


def earlier_kernel(
    rim_ref, x_ref, taps_ref, beta_ref, gate_ref, map2_ref, add2_ref, direct2_ref, reach2_ref,
    map_ref, add_ref, sent_ref, direct_ref, reach_ref, both_ref, ext,
):
    heads, toks = gate_ref.shape
    half = toks // 2
    ext[8 - (CONV - 1) : 8] = rim_ref[...].astype(f32)
    ext[8:] = x_ref[:half].astype(f32)
    acts = activations(ext, taps_ref, half, heads)
    found = half_terms(0, heads, half, acts, beta_ref[...], gate_ref[...])
    for head, (map1, add1, direct1, reach1) in enumerate(found):
        lanes = slice(head * HK, (head + 1) * HK)
        joined = dot3(
            jnp.concatenate([map2_ref[head], reach2_ref[:, lanes]], axis=0),
            jnp.concatenate([map1, add1], axis=1),
        )
        total = joined[:HK, HK:] + add2_ref[head]
        map_ref[head] = joined[:HK, :HK]
        add_ref[head] = total
        sent_ref[head] = total.astype(bf16)
        for rows, direct, reach in (
            (slice(0, half), direct1, reach1),
            (slice(half, toks), joined[HK:, HK:] + direct2_ref[:, lanes], joined[HK:, :HK]),
        ):
            direct_ref[rows, lanes] = direct
            reach_ref[rows, lanes] = reach
            both_ref[0, rows, lanes] = direct.astype(bf16)
            both_ref[1, rows, lanes] = reach.astype(bf16)


def kernel_call(kernel, operands, out_shapes, limit=16, scratch=(), cost=2**16, space=pltpu.VMEM):
    return pl.pallas_call(
        kernel,
        in_specs=[pl.BlockSpec(memory_space=space)] * len(operands),
        out_specs=[pl.BlockSpec(memory_space=pltpu.VMEM)] * len(out_shapes),
        out_shape=[jax.ShapeDtypeStruct(*shape) for shape in out_shapes],
        scratch_shapes=scratch,
        compiler_params=pltpu.CompilerParams(vmem_limit_bytes=limit * 2**20),
        cost_estimate=pl.CostEstimate(flops=2**20, bytes_accessed=cost, transcendentals=0),
    )(*operands)


def load(*sources):
    sources = [pltpu.with_memory_space_constraint(x, pltpu.HBM) for x in sources]
    edge = ((CONV - 1, sources[0].shape[1]), bf16)
    return pl.pallas_call(
        load_kernel,
        in_specs=[pl.BlockSpec(memory_space=pltpu.HBM)] * len(sources),
        out_specs=[pl.BlockSpec(memory_space=pltpu.VMEM)] * (len(sources) + 1),
        out_shape=[pltpu.VMEM(x.shape, x.dtype) for x in sources] + [pltpu.VMEM(*edge)],
        scratch_shapes=[pltpu.SemaphoreType.DMA((len(sources),))],
        compiler_params=pltpu.CompilerParams(vmem_limit_bytes=2**22),
    )(*sources)


def later_activations(x, taps):
    toks, channels = x.shape
    half = toks // 2
    return kernel_call(
        conv_kernel,
        (x, taps),
        [((half, channels), f32)],
        scratch=[pltpu.VMEM((8 + half, channels), f32)],
    )[0]


def shard_terms(later_acts, rim, x, taps, beta_t, gate_t):
    toks, channels = x.shape
    heads = gate_t.shape[0]
    half = toks // 2
    square, rows, half_rows = (heads, HK, HK), (toks, heads * HK), (half, heads * HK)
    later = kernel_call(
        later_kernel,
        (later_acts, beta_t, gate_t),
        [(square, f32)] * 2 + [(half_rows, f32)] * 2,
        limit=32,
    )
    return kernel_call(
        earlier_kernel,
        (rim, x, taps, beta_t, gate_t, *later),
        [(square, f32)] * 2 + [(square, bf16)] + [(rows, f32)] * 2 + [((2,) + rows, bf16)],
        limit=32,
        scratch=[pltpu.VMEM((8 + half, channels), f32)],
    )


def hand_on_kernel(map_ref, add_ref, state_ref, out_ref):
    for head in range(map_ref.shape[0]):
        high, low = split(map_ref[head])
        state = state_ref[head]
        grown = dot(
            jnp.concatenate([high, low], axis=1), jnp.concatenate([state, state], axis=0)
        )
        out_ref[head] = (grown + add_ref[head]).astype(bf16)


def hand_on(total_map, total_add, state):
    heads = total_map.shape[0]
    return pl.pallas_call(
        hand_on_kernel,
        out_shape=jax.ShapeDtypeStruct(state.shape, bf16),
        compiler_params=pltpu.CompilerParams(vmem_limit_bytes=16 * 2**20),
        cost_estimate=pl.CostEstimate(
            flops=4 * heads * HK**3, bytes_accessed=heads * HK * HK * 12, transcendentals=0
        ),
    )(total_map, total_add, state)


def project_kernel(count, *refs):
    states = refs[: count - 1]
    direct_ref, reach_ref, gain_ref, own_ref = refs[count - 1 : count + 3]
    rights = refs[count + 3 : 2 * count + 2]
    lefts = refs[2 * count + 2 : 3 * count + 1]
    out_ref, slots, sems = refs[3 * count + 1 :]
    mine = lax.axis_index("ctx")
    heads = states[0].shape[0]
    cols = own_ref.shape[1]

    def copy(source, slot):
        return pltpu.make_async_copy(source, slots.at[slot], sems.at[slot])

    copy(own_ref, 0).start()
    for turn in range(1, count):
        pl.when(mine >= turn)(lambda: copy(rights[turn - 1], turn).start())
        pl.when(mine < turn)(lambda: copy(lefts[count - turn - 1], turn).start())
    parts = []
    for head in range(heads):
        lanes = slice(head * HK, (head + 1) * HK)
        state = states[0][head]
        for other in states[1:]:
            state = state + other[head]
        high, low = split(reach_ref[:, lanes])
        out = direct_ref[:, lanes] + dot(
            jnp.concatenate([high, low], axis=1), jnp.concatenate([state, state], axis=0)
        )
        inverse = lax.rsqrt(jnp.mean(out * out, axis=-1, keepdims=True) + 1e-05)
        parts.append((out * inverse * gain_ref[:, lanes]).astype(bf16))
    normed = jnp.concatenate(parts, axis=1)
    for turn in range(count):
        copy(own_ref, turn).wait()
        owner = lax.rem(mine + count - turn, count)
        place = pl.ds(pl.multiple_of(owner * cols, HK), cols)
        out_ref[:, place] = dot(normed, slots[turn]).astype(bf16)


def project(states, direct, reach, gain, own, rights, lefts):
    count = len(states) + 1
    toks, width = direct.shape
    cols = own.shape[1]
    vmem = pl.BlockSpec(memory_space=pltpu.VMEM)
    hbm = pl.BlockSpec(memory_space=pl.ANY)
    return pl.pallas_call(
        functools.partial(project_kernel, count),
        in_specs=[vmem] * (count - 1) + [vmem] * 3 + [hbm] * (2 * count - 1),
        out_specs=vmem,
        out_shape=jax.ShapeDtypeStruct((toks, count * cols), bf16),
        scratch_shapes=[
            pltpu.VMEM((count, width, cols), bf16),
            pltpu.SemaphoreType.DMA((count,)),
        ],
        compiler_params=pltpu.CompilerParams(vmem_limit_bytes=32 * 2**20),
        cost_estimate=pl.CostEstimate(
            flops=2 * toks * width * count * cols,
            bytes_accessed=2 * width * count * cols,
            transcendentals=0,
        ),
    )(*states, direct, reach, gain, own, *rights, *lefts)


def on_shard(place):
    return pl.when(lax.axis_index("ctx") == place)


def head_lanes(heads):
    return [(head, slice(head * HK, (head + 1) * HK)) for head in range(heads)]


def normed_rows(out, gain):
    return (out * lax.rsqrt(jnp.mean(out * out, axis=-1, keepdims=True) + 1e-05) * gain).astype(bf16)


def project_to(out_ref, rows, *weights):
    cols = out_ref.shape[1] // len(weights)
    for index, weight in enumerate(weights):
        parts = weight if isinstance(weight, tuple) else (weight,)
        depth = rows.shape[1] // len(parts)
        found = sum(dot(rows[:, i * depth : (i + 1) * depth], part[...]) for i, part in enumerate(parts))
        out_ref[:, index * cols : (index + 1) * cols] = found.astype(bf16)


def rows_with_state(direct_ref, reach_ref, gain_ref, state_ref, out_ref):
    for head, lanes in head_lanes(state_ref.shape[0]):
        state = state_ref[head]
        out = direct_ref[:, lanes] + dot(
            jnp.concatenate(split(reach_ref[:, lanes]), axis=1), jnp.concatenate([state, state], axis=0)
        )
        out_ref[:, lanes] = normed_rows(out, gain_ref[:, lanes])


def rows_of_next(both_ref, gain_ref, head, lanes, state):
    out = both_ref[0, :, lanes].astype(f32) + dot(both_ref[1, :, lanes], state)
    return normed_rows(out, gain_ref[:, lanes])


def first_rows_kernel(direct_ref, gain_ref, out_ref):
    @on_shard(0)
    def _():
        for head, lanes in head_lanes(direct_ref.shape[1] // HK):
            out_ref[:, lanes] = normed_rows(direct_ref[:, lanes], gain_ref[:, lanes])


def second_rows_kernel(direct_ref, reach_ref, gain_ref, state_ref, out_ref):
    @on_shard(1)
    def _():
        rows_with_state(direct_ref, reach_ref, gain_ref, state_ref, out_ref)


def third_columns_kernel(both_ref, gain_ref, state_ref, left_a, left_b, out_ref, rows_ref):
    @on_shard(1)
    def _():
        for head, lanes in head_lanes(state_ref.shape[0]):
            rows_ref[:, lanes] = rows_of_next(both_ref, gain_ref, head, lanes, state_ref[head])
        project_to(out_ref, rows_ref[...], (left_a, left_b))


def fourth_rows_kernel(map_ref, add_ref, both_ref, gain_ref, state_ref, out_ref):
    @on_shard(2)
    def _():
        for head, lanes in head_lanes(state_ref.shape[0]):
            state = state_ref[head]
            left = add_ref[head] + dot(
                jnp.concatenate(split(map_ref[head]), axis=1), jnp.concatenate([state, state], axis=0)
            )
            out_ref[:, lanes] = rows_of_next(both_ref, gain_ref, head, lanes, left.astype(bf16))


def near_columns_kernel(
    direct_ref, reach_ref, gain_ref, state_ref, rows0_ref, rows1_ref, rows3_ref, own_ref, left_ref, left_a, left_b, right_ref,
    own_three, next_three, rows_ref,
):
    @on_shard(0)
    def _():
        project_to(own_three.at[:, : 2 * own_ref.shape[1]], rows0_ref[...], own_ref, right_ref)

    @on_shard(1)
    def _():
        project_to(own_three, rows1_ref[...], own_ref, right_ref, (left_a, left_b))

    @on_shard(2)
    def _():
        weights = (own_ref, right_ref, left_ref)
        project_to(next_three, rows3_ref[...], *weights)
        rows_with_state(direct_ref, reach_ref, gain_ref, state_ref, rows_ref)
        project_to(own_three, rows_ref[...], *weights)


def first_columns_kernel(rows_ref, own_ref, left_ref, out_ref):
    @on_shard(3)
    def _():
        project_to(out_ref, rows_ref[...], left_ref, own_ref)


def far_columns_kernel(rows1_ref, rows3_ref, left_a, left_b, right_ref, out_ref):
    @on_shard(1)
    def _():
        project_to(out_ref, rows3_ref[...], (left_a, left_b))

    @on_shard(2)
    def _():
        project_to(out_ref, rows1_ref[...], right_ref)


def call(kernel, operands, out_shapes, scratch=()):
    vmem = pl.BlockSpec(memory_space=pltpu.VMEM)
    shapes = [jax.ShapeDtypeStruct(shape, bf16) for shape in out_shapes]
    found = pl.pallas_call(
        kernel,
        in_specs=[vmem] * len(operands),
        out_specs=[vmem] * len(shapes),
        out_shape=shapes,
        scratch_shapes=[pltpu.VMEM(shape, bf16) for shape in scratch],
        compiler_params=pltpu.CompilerParams(vmem_limit_bytes=16 * 2**20),
        cost_estimate=pl.CostEstimate(flops=2**20, bytes_accessed=2**16, transcendentals=0),
    )(*operands)
    return found if len(shapes) > 1 else found[0]


def assemble_kernel(own_three, next_three, third_one, first_two, far_one, out_ref):
    cols = far_one.shape[1]
    own = [(own_three, index) for index in range(3)]
    after = [(next_three, index) for index in range(3)]
    sources = (
        (own[0], own[1], (first_two, 0), (first_two, 1)),
        (own[2], own[0], own[1], (far_one, 0)),
        ((third_one, 0), own[2], own[0], own[1]),
        ((far_one, 0), after[2], after[0], after[1]),
    )
    for place, blocks in enumerate(sources):

        @on_shard(place)
        def _():
            for index, (ref, block) in enumerate(blocks):
                out_ref[:, index * cols : (index + 1) * cols] = ref[:, block * cols : (block + 1) * cols]


def moved(value, pairs):
    return lax.ppermute(value, "ctx", pairs)


def handed(value, pairs):
    sections, count = lax.axis_size("section"), lax.axis_size("ctx")
    return lax.ppermute(
        value,
        ("section", "ctx"),
        [
            (s * count + a, (s + 1) % sections * count + b)
            for s in range(sections)
            for a, b in pairs
        ],
    )


def on_device(streams, conv_weight, beta_logit, gate_log, norm_gain, w_out):
    count = lax.axis_size("ctx")
    toks, width = streams.shape[1], norm_gain.shape[1]
    x, taps, beta_t, gate_t, edge = load(
        streams[0], conv_weight[0], beta_logit[0].T, gate_log[0].T
    )
    rim = moved(edge, [(c, c + 1) for c in range(count - 1)])
    later_acts = later_activations(x, taps)
    whole = own = w_out[0]
    lefts = [moved(own, [(c, c - 1) for c in range(1, count)])]
    if count == 4:
        top, rest = own[: width // 2], own[width // 2 :]
        rim, later_acts, own, top = lax.optimization_barrier((rim, later_acts, own, top))
        left = moved(own, [(1, 2), (2, 3)])
        top = moved(top, [(0, 1)])
    else:
        rights = [moved(own, [(c, c + 1) for c in range(count - 1)])]
        for turn in range(2, count):
            rights.append(moved(rights[-1], [(c, c + 1) for c in range(turn - 1, count - 1)]))
            lefts.append(moved(lefts[-1], [(c, c - 1) for c in range(1, count - turn + 1)]))
    total_map, total_add, sent, direct, reach, both = shard_terms(
        later_acts, rim, x, taps, beta_t, gate_t
    )
    if count != 4:
        states = [moved(sent, [(0, 1)])]
        for turn in range(1, count - 1):
            states.append(moved(hand_on(total_map, total_add, states[-1]), [(turn, turn + 1)]))
        mixed = project(states, direct, reach, norm_gain, own, rights, lefts)
        return handed(mixed, [(c, c) for c in range(count)])[None]

    right = lefts[0]
    cols = own.shape[1]
    rows = (toks, width)
    one, two, three = ((toks, blocks * cols) for blocks in (1, 2, 3))
    sent, top, right = lax.optimization_barrier((sent, top, lefts[0]))
    first = moved(sent, [(0, 1)])
    both = moved(both, [(3, 2), (2, 1)])
    out1 = hand_on(total_map, total_add, first)
    second = moved(out1, [(1, 2)])
    rows0 = call(first_rows_kernel, [direct, norm_gain], [rows])
    far0 = moved(rows0, [(0, 3)])
    rows1 = call(second_rows_kernel, [direct, reach, norm_gain, first], [rows])
    rows1, rest = lax.optimization_barrier((rows1, rest))
    far1 = moved(rows1, [(1, 2)])
    rest = moved(rest, [(0, 1)])
    both, second = lax.optimization_barrier((both, second))
    rows3 = call(fourth_rows_kernel, [total_map, total_add, both, norm_gain, second], [rows])
    far3 = moved(rows3, [(2, 1)])
    own_three, next_three = call(
        near_columns_kernel,
        [direct, reach, norm_gain, second, rows0, rows1, rows3, whole, left, top, rest, right],
        [three, three],
        [rows],
    )
    third_one = call(third_columns_kernel, [both, norm_gain, out1, top, rest], [one], [rows])
    first_two = call(first_columns_kernel, [far0, whole, left], [two])
    far_one = call(far_columns_kernel, [far1, far3, top, rest, right], [one])
    far_one, third_one = lax.optimization_barrier((far_one, third_one))
    return call(
        assemble_kernel,
        [
            handed(own_three, [(0, 0), (1, 1), (2, 2)]),
            handed(next_three, [(2, 3)]),
            handed(third_one, [(1, 2)]),
            handed(first_two, [(3, 0)]),
            handed(far_one, [(2, 1), (1, 3)]),
        ],
        [(toks, 4 * cols)],
    )[None]


def solution(mesh):
    placed = (
        P("section", "ctx", None),
        P("section", None, None),
        P("section", "ctx", None),
        P("section", "ctx", None),
        P("section", None),
        P("section", None, "ctx"),
    )
    return jax.shard_map(
        on_device, mesh=mesh, in_specs=placed, out_specs=P("section", "ctx", None), check_vma=False
    )
```

```python
import functools
import jax
import jax.numpy as jnp
from jax import lax
from jax.experimental import pallas as pl
from jax.experimental.pallas import tpu as pltpu
from jax.sharding import PartitionSpec as P

HK = 128
STEPS = 2
CONV = 4
LEVELS = (1, 2, 4, 8, 16, 32)
f32, bf16 = jnp.float32, jnp.bfloat16


def dot(a, b):
    return jnp.dot(a, b, preferred_element_type=f32)


def split(x):
    high = x.astype(bf16)
    return high, (x - high.astype(f32)).astype(bf16)


def dot3(a, b):
    ah, al = split(a)
    bh, bl = split(b)
    return dot(
        jnp.concatenate([ah, ah, al], axis=1), jnp.concatenate([bh, bl, bh], axis=0)
    )


def pair_rows(left, right):
    zero = jnp.zeros_like(left)
    return jnp.concatenate(
        [jnp.concatenate([left, zero], axis=1), jnp.concatenate([zero, right], axis=1)], axis=0
    )


def blockwise(x):
    return pair_rows(x[:, :HK], x[:, HK:])


def pick(table, lane):
    index = lax.broadcasted_iota(jnp.int32, table.shape, 1)
    return jnp.sum(jnp.where(index == lane, table, 0.0), axis=1, keepdims=True)


def half_terms(u, heads, half, acts, beta_t, gate_t):
    size, toks = STEPS * half, 2 * half
    virt = lax.broadcasted_iota(jnp.int32, (size, toks), 0)
    tok = lax.broadcasted_iota(jnp.int32, (size, toks), 1)
    inside = ((tok >= u * half) & (tok - u * half <= virt % half)).astype(f32)
    exact = dict(precision=lax.Precision.HIGHEST, preferred_element_type=f32)
    over_lanes = (((1,), (1,)), ((), ()))
    sums = lax.dot_general(inside, gate_t, over_lanes, **exact)
    sums_t = lax.dot_general(gate_t, inside, over_lanes, **exact)
    steps = (1.0 / (1.0 + jnp.exp(-beta_t))).T[u * half : (u + 1) * half]

    row = lax.broadcasted_iota(jnp.int32, (size, size), 0)
    col = lax.broadcasted_iota(jnp.int32, (size, size), 1)
    row_tok, col_tok = row % half, col % half
    strict = (col_tok < row_tok) | ((col_tok == row_tok) & (col < row))
    upto = (col_tok <= row_tok)[:half]
    eye = (row == col).astype(f32)
    same = row_tok == col_tok
    twice = lambda x: jnp.concatenate([x, x], axis=1)
    level_masks = [
        twice(
            ((row_tok // (2 * b)) == (col_tok // (2 * b)))
            & ((row_tok // b) % 2 == 1)
            & ((col_tok // b) % 2 == 0)
        )
        for b in LEVELS
    ]

    work = []
    for head in range(heads):
        lanes = slice(head * HK, (head + 1) * HK)
        unit = lambda x: x * lax.rsqrt(jnp.sum(x * x, axis=-1, keepdims=True) + 1e-06)
        queries = unit(acts[0][:, lanes])
        keys = unit(jnp.concatenate([acts[1][:, lanes], acts[2][:, lanes]], axis=0))
        vals = jnp.concatenate([acts[3][:, lanes], acts[4][:, lanes]], axis=0)
        size_col = jnp.concatenate([pick(steps, head), pick(steps, heads + head)], axis=0)
        c_col = pick(sums, head)
        c_row = sums_t[head : head + 1]
        c_end = c_col[half - 1 : half]
        keys_t = keys.T
        gram = dot3(jnp.concatenate([keys, queries], axis=0), keys_t)
        damp = jnp.exp(jnp.minimum(c_col[:half] - c_row, 0.0))
        lower = jnp.where(
            strict, size_col * jnp.concatenate([damp, damp], axis=0) * gram[:size], 0.0
        )
        scores = jnp.where(upto, damp * gram[size:], 0.0)
        grown = jnp.exp(c_col)
        right = jnp.concatenate([size_col * vals, (size_col * grown) * keys], axis=1)
        to_end_t = keys_t * jnp.exp(c_end - c_row)
        outer = jnp.concatenate([to_end_t, scores], axis=0)
        work.append((lower, right, outer, queries * grown[:half], jnp.exp(c_end) * eye))

    pairs = range(heads // 2)
    lows, invs = [], []
    for i in pairs:
        low = jnp.concatenate([work[2 * i][0], work[2 * i + 1][0]], axis=1)
        lows.append(low.astype(bf16))
        invs.append((twice(eye) - jnp.where(twice(same), low, 0.0)).astype(bf16))
    for mask in level_masks:
        inner = [
            dot(jnp.where(mask, lows[i], jnp.zeros_like(lows[i])), blockwise(invs[i])).astype(bf16)
            for i in pairs
        ]
        invs = [invs[i] - dot(invs[i], blockwise(inner[i])).astype(bf16) for i in pairs]

    results = []
    for head in range(heads):
        lower, right, outer, reach0, map0 = work[head]
        inv = invs[head // 2][:, head % 2 * HK : (head % 2 + 1) * HK]
        first = dot(inv, right.astype(bf16))
        rest = right - first - dot3(lower, first)
        solved = first + dot(inv, rest.astype(bf16))
        both = dot3(outer, solved)
        results.append(
            (
                map0 - both[:size, HK:],
                both[:size, :HK],
                both[size:, :HK],
                reach0 - both[size:, HK:],
            )
        )
    return results


def activations(ext, taps_ref, half, heads):
    width = heads * HK
    acts = []
    for part in range(5):
        lanes = slice(part * width, (part + 1) * width)
        total = None
        for tap in range(CONV):
            low = 8 - (CONV - 1) + tap
            term = taps_ref[tap : tap + 1, lanes].astype(f32) * ext[low : low + half, lanes]
            total = term if total is None else total + term
        acts.append(total * (1.0 / (1.0 + jnp.exp(-total))))
    return acts


def load_kernel(*refs):
    sources, targets, edge_ref, sems = refs[:4], refs[4:8], refs[8], refs[9]
    copies = [
        pltpu.make_async_copy(source, target, sems.at[index])
        for index, (source, target) in enumerate(zip(sources, targets))
    ]
    for copy in copies:
        copy.start()
    for copy in copies:
        copy.wait()
    toks = targets[0].shape[0]
    edge_ref[...] = targets[0][toks - 16 :].astype(f32)[16 - (CONV - 1) :].astype(bf16)


def conv_kernel(x_ref, taps_ref, out_ref, ext):
    half, channels = out_ref.shape
    ext[...] = x_ref[half - 16 :].astype(f32)[8:]
    width = channels // 5
    for part, act in enumerate(activations(ext, taps_ref, half, width // HK)):
        out_ref[:, part * width : (part + 1) * width] = act


def later_kernel(act_ref, beta_ref, gate_ref, map_ref, add_ref, direct_ref, reach_ref):
    heads, toks = gate_ref.shape
    width = heads * HK
    acts = [act_ref[:, part * width : (part + 1) * width] for part in range(5)]
    found = half_terms(1, heads, toks // 2, acts, beta_ref[...], gate_ref[...])
    for head, (map2, add2, direct2, reach2) in enumerate(found):
        lanes = slice(head * HK, (head + 1) * HK)
        map_ref[head] = map2
        add_ref[head] = add2
        direct_ref[:, lanes] = direct2
        reach_ref[:, lanes] = reach2


def earlier_kernel(
    rim_ref, x_ref, taps_ref, beta_ref, gate_ref, map2_ref, add2_ref, direct2_ref, reach2_ref,
    map_ref, add_ref, sent_ref, direct_ref, reach_ref, both_ref, ext,
):
    heads, toks = gate_ref.shape
    half = toks // 2
    ext[8 - (CONV - 1) : 8] = rim_ref[...].astype(f32)
    ext[8:] = x_ref[:half].astype(f32)
    acts = activations(ext, taps_ref, half, heads)
    found = half_terms(0, heads, half, acts, beta_ref[...], gate_ref[...])
    for head, (map1, add1, direct1, reach1) in enumerate(found):
        lanes = slice(head * HK, (head + 1) * HK)
        joined = dot3(
            jnp.concatenate([map2_ref[head], reach2_ref[:, lanes]], axis=0),
            jnp.concatenate([map1, add1], axis=1),
        )
        total = joined[:HK, HK:] + add2_ref[head]
        map_ref[head] = joined[:HK, :HK]
        add_ref[head] = total
        sent_ref[head] = total.astype(bf16)
        for rows, direct, reach in (
            (slice(0, half), direct1, reach1),
            (slice(half, toks), joined[HK:, HK:] + direct2_ref[:, lanes], joined[HK:, :HK]),
        ):
            direct_ref[rows, lanes] = direct
            reach_ref[rows, lanes] = reach
            both_ref[0, rows, lanes] = direct.astype(bf16)
            both_ref[1, rows, lanes] = reach.astype(bf16)


def kernel_call(kernel, operands, out_shapes, limit=16, scratch=(), cost=2**16, space=pltpu.VMEM):
    return pl.pallas_call(
        kernel,
        in_specs=[pl.BlockSpec(memory_space=space)] * len(operands),
        out_specs=[pl.BlockSpec(memory_space=pltpu.VMEM)] * len(out_shapes),
        out_shape=[jax.ShapeDtypeStruct(*shape) for shape in out_shapes],
        scratch_shapes=scratch,
        compiler_params=pltpu.CompilerParams(vmem_limit_bytes=limit * 2**20),
        cost_estimate=pl.CostEstimate(flops=2**20, bytes_accessed=cost, transcendentals=0),
    )(*operands)


def load(*sources):
    sources = [pltpu.with_memory_space_constraint(x, pltpu.HBM) for x in sources]
    edge = ((CONV - 1, sources[0].shape[1]), bf16)
    return pl.pallas_call(
        load_kernel,
        in_specs=[pl.BlockSpec(memory_space=pltpu.HBM)] * len(sources),
        out_specs=[pl.BlockSpec(memory_space=pltpu.VMEM)] * (len(sources) + 1),
        out_shape=[pltpu.VMEM(x.shape, x.dtype) for x in sources] + [pltpu.VMEM(*edge)],
        scratch_shapes=[pltpu.SemaphoreType.DMA((len(sources),))],
        compiler_params=pltpu.CompilerParams(vmem_limit_bytes=2**22),
    )(*sources)


def later_activations(x, taps):
    toks, channels = x.shape
    half = toks // 2
    return kernel_call(
        conv_kernel,
        (x, taps),
        [((half, channels), f32)],
        scratch=[pltpu.VMEM((8 + half, channels), f32)],
    )[0]


def shard_terms(later_acts, rim, x, taps, beta_t, gate_t):
    toks, channels = x.shape
    heads = gate_t.shape[0]
    half = toks // 2
    square, rows, half_rows = (heads, HK, HK), (toks, heads * HK), (half, heads * HK)
    later = kernel_call(
        later_kernel,
        (later_acts, beta_t, gate_t),
        [(square, f32)] * 2 + [(half_rows, f32)] * 2,
        limit=32,
    )
    return kernel_call(
        earlier_kernel,
        (rim, x, taps, beta_t, gate_t, *later),
        [(square, f32)] * 2 + [(square, bf16)] + [(rows, f32)] * 2 + [((2,) + rows, bf16)],
        limit=32,
        scratch=[pltpu.VMEM((8 + half, channels), f32)],
    )


def hand_on_kernel(map_ref, add_ref, state_ref, out_ref):
    for head in range(map_ref.shape[0]):
        high, low = split(map_ref[head])
        state = state_ref[head]
        grown = dot(
            jnp.concatenate([high, low], axis=1), jnp.concatenate([state, state], axis=0)
        )
        out_ref[head] = (grown + add_ref[head]).astype(bf16)


def hand_on(total_map, total_add, state):
    heads = total_map.shape[0]
    return pl.pallas_call(
        hand_on_kernel,
        out_shape=jax.ShapeDtypeStruct(state.shape, bf16),
        compiler_params=pltpu.CompilerParams(vmem_limit_bytes=16 * 2**20),
        cost_estimate=pl.CostEstimate(
            flops=4 * heads * HK**3, bytes_accessed=heads * HK * HK * 12, transcendentals=0
        ),
    )(total_map, total_add, state)


def project_kernel(count, *refs):
    states = refs[: count - 1]
    direct_ref, reach_ref, gain_ref, own_ref = refs[count - 1 : count + 3]
    rights = refs[count + 3 : 2 * count + 2]
    lefts = refs[2 * count + 2 : 3 * count + 1]
    out_ref, slots, sems = refs[3 * count + 1 :]
    mine = lax.axis_index("ctx")
    heads = states[0].shape[0]
    cols = own_ref.shape[1]

    def copy(source, slot):
        return pltpu.make_async_copy(source, slots.at[slot], sems.at[slot])

    copy(own_ref, 0).start()
    for turn in range(1, count):
        pl.when(mine >= turn)(lambda: copy(rights[turn - 1], turn).start())
        pl.when(mine < turn)(lambda: copy(lefts[count - turn - 1], turn).start())
    parts = []
    for head in range(heads):
        lanes = slice(head * HK, (head + 1) * HK)
        state = states[0][head]
        for other in states[1:]:
            state = state + other[head]
        high, low = split(reach_ref[:, lanes])
        out = direct_ref[:, lanes] + dot(
            jnp.concatenate([high, low], axis=1), jnp.concatenate([state, state], axis=0)
        )
        inverse = lax.rsqrt(jnp.mean(out * out, axis=-1, keepdims=True) + 1e-05)
        parts.append((out * inverse * gain_ref[:, lanes]).astype(bf16))
    normed = jnp.concatenate(parts, axis=1)
    for turn in range(count):
        copy(own_ref, turn).wait()
        owner = lax.rem(mine + count - turn, count)
        place = pl.ds(pl.multiple_of(owner * cols, HK), cols)
        out_ref[:, place] = dot(normed, slots[turn]).astype(bf16)


def project(states, direct, reach, gain, own, rights, lefts):
    count = len(states) + 1
    toks, width = direct.shape
    cols = own.shape[1]
    vmem = pl.BlockSpec(memory_space=pltpu.VMEM)
    hbm = pl.BlockSpec(memory_space=pl.ANY)
    return pl.pallas_call(
        functools.partial(project_kernel, count),
        in_specs=[vmem] * (count - 1) + [vmem] * 3 + [hbm] * (2 * count - 1),
        out_specs=vmem,
        out_shape=jax.ShapeDtypeStruct((toks, count * cols), bf16),
        scratch_shapes=[
            pltpu.VMEM((count, width, cols), bf16),
            pltpu.SemaphoreType.DMA((count,)),
        ],
        compiler_params=pltpu.CompilerParams(vmem_limit_bytes=32 * 2**20),
        cost_estimate=pl.CostEstimate(
            flops=2 * toks * width * count * cols,
            bytes_accessed=2 * width * count * cols,
            transcendentals=0,
        ),
    )(*states, direct, reach, gain, own, *rights, *lefts)


def on_shard(place):
    return pl.when(lax.axis_index("ctx") == place)


def head_lanes(heads):
    return [(head, slice(head * HK, (head + 1) * HK)) for head in range(heads)]


def normed_rows(out, gain):
    return (out * lax.rsqrt(jnp.mean(out * out, axis=-1, keepdims=True) + 1e-05) * gain).astype(bf16)


def project_to(out_ref, rows, *weights):
    cols = weights[0].shape[1]
    for index, weight in enumerate(weights):
        out_ref[:, index * cols : (index + 1) * cols] = dot(rows, weight[...]).astype(bf16)


def rows_with_state(direct_ref, reach_ref, gain_ref, state_ref, out_ref):
    for head, lanes in head_lanes(state_ref.shape[0]):
        state = state_ref[head]
        out = direct_ref[:, lanes] + dot(
            jnp.concatenate(split(reach_ref[:, lanes]), axis=1), jnp.concatenate([state, state], axis=0)
        )
        out_ref[:, lanes] = normed_rows(out, gain_ref[:, lanes])


def rows_of_next(both_ref, gain_ref, head, lanes, state):
    out = both_ref[0, :, lanes].astype(f32) + dot(both_ref[1, :, lanes], state)
    return normed_rows(out, gain_ref[:, lanes])


def early_rows_kernel(direct_ref, reach_ref, gain_ref, state_ref, out_ref):
    @on_shard(0)
    def _():
        for head, lanes in head_lanes(state_ref.shape[0]):
            out_ref[:, lanes] = normed_rows(direct_ref[:, lanes], gain_ref[:, lanes])

    @on_shard(1)
    def _():
        rows_with_state(direct_ref, reach_ref, gain_ref, state_ref, out_ref)


def third_rows_kernel(both_ref, gain_ref, state_ref, out_ref):
    @on_shard(1)
    def _():
        for head, lanes in head_lanes(state_ref.shape[0]):
            out_ref[:, lanes] = rows_of_next(both_ref, gain_ref, head, lanes, state_ref[head])


def fourth_rows_kernel(map_ref, add_ref, both_ref, gain_ref, state_ref, out_ref):
    @on_shard(2)
    def _():
        for head, lanes in head_lanes(state_ref.shape[0]):
            state = state_ref[head]
            left = add_ref[head] + dot(
                jnp.concatenate(split(map_ref[head]), axis=1), jnp.concatenate([state, state], axis=0)
            )
            out_ref[:, lanes] = rows_of_next(both_ref, gain_ref, head, lanes, left.astype(bf16))


def near_columns_kernel(
    direct_ref, reach_ref, gain_ref, state_ref, early_ref, rows3_ref, own_ref, left_ref, right_ref,
    own_three, next_three, rows_ref,
):
    @pl.when(lax.axis_index("ctx") < 2)
    def _():
        project_to(own_three, early_ref[...], own_ref, right_ref)

    @on_shard(2)
    def _():
        weights = (own_ref, right_ref, left_ref)
        project_to(next_three, rows3_ref[...], *weights)
        rows_with_state(direct_ref, reach_ref, gain_ref, state_ref, rows_ref)
        project_to(own_three, rows_ref[...], *weights)


def early_columns_kernel(rows_ref, own_ref, left_ref, out_ref):
    @on_shard(0)
    def _():
        project_to(out_ref, rows_ref[...], own_ref)

    @on_shard(3)
    def _():
        project_to(out_ref, rows_ref[...], left_ref, own_ref)


def far_columns_kernel(rows1_ref, rows3_ref, own_ref, right_ref, out_ref):
    @on_shard(0)
    def _():
        project_to(out_ref, rows3_ref[...], own_ref)

    @on_shard(2)
    def _():
        project_to(out_ref, rows1_ref[...], right_ref)


def third_columns_kernel(rows_ref, own_ref, out_ref):
    @on_shard(0)
    def _():
        project_to(out_ref, rows_ref[...], own_ref)


def call(kernel, operands, out_shapes, scratch=()):
    vmem = pl.BlockSpec(memory_space=pltpu.VMEM)
    shapes = [jax.ShapeDtypeStruct(shape, bf16) for shape in out_shapes]
    found = pl.pallas_call(
        kernel,
        in_specs=[vmem] * len(operands),
        out_specs=[vmem] * len(shapes),
        out_shape=shapes,
        scratch_shapes=[pltpu.VMEM(shape, bf16) for shape in scratch],
        compiler_params=pltpu.CompilerParams(vmem_limit_bytes=16 * 2**20),
        cost_estimate=pl.CostEstimate(flops=2**20, bytes_accessed=2**16, transcendentals=0),
    )(*operands)
    return found if len(shapes) > 1 else found[0]


def assemble_kernel(own_three, next_three, third_one, early_two, far_one, out_ref):
    cols = far_one.shape[1]
    own = [(own_three, index) for index in range(3)]
    after = [(next_three, index) for index in range(3)]
    early = [(early_two, index) for index in range(2)]
    sources = (
        (own[0], own[1], early[0], early[1]),
        (early[0], own[0], own[1], (far_one, 0)),
        ((third_one, 0), own[2], own[0], own[1]),
        ((far_one, 0), after[2], after[0], after[1]),
    )
    for place, blocks in enumerate(sources):

        @on_shard(place)
        def _():
            for index, (ref, block) in enumerate(blocks):
                out_ref[:, index * cols : (index + 1) * cols] = ref[:, block * cols : (block + 1) * cols]


def moved(value, pairs):
    return lax.ppermute(value, "ctx", pairs)


def handed(value, pairs):
    sections, count = lax.axis_size("section"), lax.axis_size("ctx")
    return lax.ppermute(
        value,
        ("section", "ctx"),
        [
            (s * count + a, (s + 1) % sections * count + b)
            for s in range(sections)
            for a, b in pairs
        ],
    )


def on_device(streams, conv_weight, beta_logit, gate_log, norm_gain, w_out):
    count = lax.axis_size("ctx")
    toks, width = streams.shape[1], norm_gain.shape[1]
    x, taps, beta_t, gate_t, edge = load(
        streams[0], conv_weight[0], beta_logit[0].T, gate_log[0].T
    )
    rim = moved(edge, [(c, c + 1) for c in range(count - 1)])
    later_acts = later_activations(x, taps)
    own = w_out[0]
    lefts = [moved(own, [(c, c - 1) for c in range(1, count)])]
    if count == 4:
        rim, later_acts, held = lax.optimization_barrier((rim, later_acts, own))
        left = moved(held, [(1, 2), (2, 3)])
    else:
        rights = [moved(own, [(c, c + 1) for c in range(count - 1)])]
        for turn in range(2, count):
            rights.append(moved(rights[-1], [(c, c + 1) for c in range(turn - 1, count - 1)]))
            lefts.append(moved(lefts[-1], [(c, c - 1) for c in range(1, count - turn + 1)]))
    total_map, total_add, sent, direct, reach, both = shard_terms(
        later_acts, rim, x, taps, beta_t, gate_t
    )
    if count != 4:
        states = [moved(sent, [(0, 1)])]
        for turn in range(1, count - 1):
            states.append(moved(hand_on(total_map, total_add, states[-1]), [(turn, turn + 1)]))
        mixed = project(states, direct, reach, norm_gain, own, rights, lefts)
        return handed(mixed, [(c, c) for c in range(count)])[None]

    right = lefts[0]
    cols = own.shape[1]
    rows = (toks, width)
    one, two, three = ((toks, blocks * cols) for blocks in (1, 2, 3))
    sent, right = lax.optimization_barrier((sent, lefts[0]))
    first = moved(sent, [(0, 1)])
    both = moved(both, [(3, 2), (2, 1)])
    out1 = hand_on(total_map, total_add, first)
    second = moved(out1, [(1, 2)])
    early = call(early_rows_kernel, [direct, reach, norm_gain, first], [rows])
    early_far = moved(early, [(0, 3), (1, 0)])
    far1 = moved(early, [(1, 2)])
    both, second = lax.optimization_barrier((both, second))
    rows3 = call(fourth_rows_kernel, [total_map, total_add, both, norm_gain, second], [rows])
    far3 = moved(rows3, [(2, 0)])
    rows2 = call(third_rows_kernel, [both, norm_gain, out1], [rows])
    far2 = moved(rows2, [(1, 0)])
    own_three, next_three = call(
        near_columns_kernel,
        [direct, reach, norm_gain, second, early, rows3, own, left, right],
        [three, three],
        [rows],
    )
    early_two = call(early_columns_kernel, [early_far, own, left], [two])
    far_one = call(far_columns_kernel, [far1, far3, own, right], [one])
    far_one, far2 = lax.optimization_barrier((far_one, far2))
    third_one = call(third_columns_kernel, [far2, own], [one])
    return call(
        assemble_kernel,
        [
            handed(own_three, [(0, 0), (1, 1), (2, 2)]),
            handed(next_three, [(2, 3)]),
            handed(third_one, [(0, 2)]),
            handed(early_two, [(3, 0), (0, 1)]),
            handed(far_one, [(2, 1), (0, 3)]),
        ],
        [(toks, 4 * cols)],
    )[None]


def solution(mesh):
    placed = (
        P("section", "ctx", None),
        P("section", None, None),
        P("section", "ctx", None),
        P("section", "ctx", None),
        P("section", None),
        P("section", None, "ctx"),
    )
    return jax.shard_map(
        on_device, mesh=mesh, in_specs=placed, out_specs=P("section", "ctx", None), check_vma=False
    )
```

```python
import functools
import jax
import jax.numpy as jnp
from jax import lax
from jax.experimental import pallas as pl
from jax.experimental.pallas import tpu as pltpu
from jax.sharding import PartitionSpec as P

HK = 128
STEPS = 2
CONV = 4
LEVELS = 6
f32, bf16 = jnp.float32, jnp.bfloat16


def dot(a, b):
    return jnp.dot(a, b, preferred_element_type=f32)


def split(x):
    high = x.astype(bf16)
    return high, (x - high.astype(f32)).astype(bf16)


def dot3(a, b):
    ah, al = split(a)
    bh, bl = split(b)
    return dot(
        jnp.concatenate([ah, ah, al], axis=1), jnp.concatenate([bh, bl, bh], axis=0)
    )


def pair_rows(left, right):
    zero = jnp.zeros_like(left)
    return jnp.concatenate(
        [jnp.concatenate([left, zero], axis=1), jnp.concatenate([zero, right], axis=1)], axis=0
    )


def blockwise(x):
    return pair_rows(x[:, :HK], x[:, HK:])


def half_terms(u, heads, half, acts, beta_t, gate_t):
    size, toks = STEPS * half, 2 * half
    virt = lax.broadcasted_iota(jnp.int32, (size, toks), 0)
    tok = lax.broadcasted_iota(jnp.int32, (size, toks), 1) - u * half
    inside = ((tok >= 0) & (tok <= (virt & (half - 1)))).astype(f32)
    exact = dict(precision=lax.Precision.HIGHEST, preferred_element_type=f32)
    over_lanes = (((1,), (1,)), ((), ()))
    sums = lax.dot_general(inside, gate_t, over_lanes, **exact)
    sums_t = lax.dot_general(gate_t, inside, over_lanes, **exact)
    steps = (1.0 / (1.0 + jnp.exp(-beta_t))).T[u * half : (u + 1) * half]

    row = lax.broadcasted_iota(jnp.int32, (size, size), 0)
    col = lax.broadcasted_iota(jnp.int32, (size, size), 1)
    row_tok, col_tok = row & (half - 1), col & (half - 1)
    apart = row_tok ^ col_tok
    strict = (col_tok < row_tok) | ((apart == 0) & (col < row))
    upto = (col_tok <= row_tok)[:half]
    eye = (row == col).astype(f32)
    twice = lambda x: jnp.concatenate([x, x], axis=1)
    same = twice(apart == 0)
    before = twice(jnp.where(col_tok < row_tok, apart, 0))
    level_masks = [(before >> level) == 1 for level in range(LEVELS)]

    work = []
    for head in range(heads):
        lanes = slice(head * HK, (head + 1) * HK)
        unit = lambda x: x * lax.rsqrt(jnp.sum(x * x, axis=-1, keepdims=True) + 1e-06)
        queries = unit(acts[0][:, lanes])
        keys = unit(jnp.concatenate([acts[1][:, lanes], acts[2][:, lanes]], axis=0))
        vals = jnp.concatenate([acts[3][:, lanes], acts[4][:, lanes]], axis=0)
        size_col = jnp.concatenate(
            [steps[:, head : head + 1], steps[:, heads + head : heads + head + 1]], axis=0
        )
        c_col = sums[:, head : head + 1]
        c_row = sums_t[head : head + 1]
        c_end = c_col[half - 1 : half]
        keys_t = keys.T
        gram = dot3(jnp.concatenate([keys, queries], axis=0), keys_t)
        damp = jnp.exp(jnp.minimum(c_col[:half] - c_row, 0.0))
        lower = jnp.where(
            strict, size_col * jnp.concatenate([damp, damp], axis=0) * gram[:size], 0.0
        )
        scores = jnp.where(upto, damp * gram[size:], 0.0)
        grown = jnp.exp(c_col)
        right = jnp.concatenate([size_col * vals, (size_col * grown) * keys], axis=1)
        to_end_t = keys_t * jnp.exp(c_end - c_row)
        outer = jnp.concatenate([to_end_t, scores], axis=0)
        work.append((lower, right, outer, queries * grown[:half], jnp.exp(c_end) * eye))

    pairs = range(heads // 2)
    lows, invs = [], []
    for i in pairs:
        low = jnp.concatenate([work[2 * i][0], work[2 * i + 1][0]], axis=1)
        lows.append(low.astype(bf16))
        invs.append((twice(eye) - jnp.where(same, low, 0.0)).astype(bf16))
    for mask in level_masks:
        inner = [
            dot(jnp.where(mask, lows[i], jnp.zeros_like(lows[i])), blockwise(invs[i])).astype(bf16)
            for i in pairs
        ]
        invs = [invs[i] - dot(invs[i], blockwise(inner[i])).astype(bf16) for i in pairs]

    results = []
    for head in range(heads):
        lower, right, outer, reach0, map0 = work[head]
        inv = invs[head // 2][:, head % 2 * HK : (head % 2 + 1) * HK]
        first = dot(inv, right.astype(bf16))
        rest = right - first - dot3(lower, first)
        solved = first + dot(inv, rest.astype(bf16))
        both = dot3(outer, solved)
        results.append(
            (
                map0 - both[:size, HK:],
                both[:size, :HK],
                both[size:, :HK],
                reach0 - both[size:, HK:],
            )
        )
    return results


def activations(ext, taps_ref, half, heads):
    width = heads * HK
    acts = []
    for part in range(5):
        lanes = slice(part * width, (part + 1) * width)
        total = None
        for tap in range(CONV):
            low = 8 - (CONV - 1) + tap
            term = taps_ref[tap : tap + 1, lanes].astype(f32) * ext[low : low + half, lanes]
            total = term if total is None else total + term
        acts.append(total * (1.0 / (1.0 + jnp.exp(-total))))
    return acts


def load_kernel(*refs):
    sources, targets, edge_ref, sems = refs[:4], refs[4:8], refs[8], refs[9]
    copies = [
        pltpu.make_async_copy(source, target, sems.at[index])
        for index, (source, target) in enumerate(zip(sources, targets))
    ]
    for copy in copies:
        copy.start()
    for copy in copies:
        copy.wait()
    toks = targets[0].shape[0]
    edge_ref[...] = targets[0][toks - 16 :].astype(f32)[16 - (CONV - 1) :].astype(bf16)


def conv_kernel(x_ref, taps_ref, out_ref, ext):
    half, channels = out_ref.shape
    ext[...] = x_ref[half - 16 :].astype(f32)[8:]
    width = channels // 5
    for part, act in enumerate(activations(ext, taps_ref, half, width // HK)):
        out_ref[:, part * width : (part + 1) * width] = act


def later_kernel(act_ref, beta_ref, gate_ref, map_ref, add_ref, direct_ref, reach_ref):
    heads, toks = gate_ref.shape
    width = heads * HK
    acts = [act_ref[:, part * width : (part + 1) * width] for part in range(5)]
    found = half_terms(1, heads, toks // 2, acts, beta_ref[...], gate_ref[...])
    for head, (map2, add2, direct2, reach2) in enumerate(found):
        lanes = slice(head * HK, (head + 1) * HK)
        map_ref[head] = map2
        add_ref[head] = add2
        direct_ref[:, lanes] = direct2
        reach_ref[:, lanes] = reach2


def earlier_kernel(
    rim_ref, x_ref, taps_ref, beta_ref, gate_ref, map2_ref, add2_ref, direct2_ref, reach2_ref,
    map_ref, add_ref, sent_ref, direct_ref, reach_ref, both_ref, ext,
):
    heads, toks = gate_ref.shape
    half = toks // 2
    ext[8 - (CONV - 1) : 8] = rim_ref[...].astype(f32)
    ext[8:] = x_ref[:half].astype(f32)
    acts = activations(ext, taps_ref, half, heads)
    found = half_terms(0, heads, half, acts, beta_ref[...], gate_ref[...])
    for head, (map1, add1, direct1, reach1) in enumerate(found):
        lanes = slice(head * HK, (head + 1) * HK)
        joined = dot3(
            jnp.concatenate([map2_ref[head], reach2_ref[:, lanes]], axis=0),
            jnp.concatenate([map1, add1], axis=1),
        )
        total = joined[:HK, HK:] + add2_ref[head]
        map_ref[head] = joined[:HK, :HK]
        add_ref[head] = total
        sent_ref[head] = total.astype(bf16)
        for rows, direct, reach in (
            (slice(0, half), direct1, reach1),
            (slice(half, toks), joined[HK:, HK:] + direct2_ref[:, lanes], joined[HK:, :HK]),
        ):
            direct_ref[rows, lanes] = direct
            reach_ref[rows, lanes] = reach
            both_ref[0, rows, lanes] = direct.astype(bf16)
            both_ref[1, rows, lanes] = reach.astype(bf16)


def kernel_call(kernel, operands, out_shapes, limit=16, scratch=(), cost=2**16, space=pltpu.VMEM):
    return pl.pallas_call(
        kernel,
        in_specs=[pl.BlockSpec(memory_space=space)] * len(operands),
        out_specs=[pl.BlockSpec(memory_space=pltpu.VMEM)] * len(out_shapes),
        out_shape=[jax.ShapeDtypeStruct(*shape) for shape in out_shapes],
        scratch_shapes=scratch,
        compiler_params=pltpu.CompilerParams(vmem_limit_bytes=limit * 2**20),
        cost_estimate=pl.CostEstimate(flops=2**20, bytes_accessed=cost, transcendentals=0),
    )(*operands)


def load(*sources):
    sources = [pltpu.with_memory_space_constraint(x, pltpu.HBM) for x in sources]
    edge = ((CONV - 1, sources[0].shape[1]), bf16)
    return pl.pallas_call(
        load_kernel,
        in_specs=[pl.BlockSpec(memory_space=pltpu.HBM)] * len(sources),
        out_specs=[pl.BlockSpec(memory_space=pltpu.VMEM)] * (len(sources) + 1),
        out_shape=[pltpu.VMEM(x.shape, x.dtype) for x in sources] + [pltpu.VMEM(*edge)],
        scratch_shapes=[pltpu.SemaphoreType.DMA((len(sources),))],
        compiler_params=pltpu.CompilerParams(vmem_limit_bytes=2**22),
    )(*sources)


def later_activations(x, taps):
    toks, channels = x.shape
    half = toks // 2
    return kernel_call(
        conv_kernel,
        (x, taps),
        [((half, channels), f32)],
        scratch=[pltpu.VMEM((8 + half, channels), f32)],
    )[0]


def shard_terms(later_acts, rim, x, taps, beta_t, gate_t):
    toks, channels = x.shape
    heads = gate_t.shape[0]
    half = toks // 2
    square, rows, half_rows = (heads, HK, HK), (toks, heads * HK), (half, heads * HK)
    later = kernel_call(
        later_kernel,
        (later_acts, beta_t, gate_t),
        [(square, f32)] * 2 + [(half_rows, f32)] * 2,
        limit=32,
    )
    return kernel_call(
        earlier_kernel,
        (rim, x, taps, beta_t, gate_t, *later),
        [(square, f32)] * 2 + [(square, bf16)] + [(rows, f32)] * 2 + [((2,) + rows, bf16)],
        limit=32,
        scratch=[pltpu.VMEM((8 + half, channels), f32)],
    )


def hand_on_kernel(map_ref, add_ref, state_ref, out_ref):
    for head in range(map_ref.shape[0]):
        high, low = split(map_ref[head])
        state = state_ref[head]
        grown = dot(
            jnp.concatenate([high, low], axis=1), jnp.concatenate([state, state], axis=0)
        )
        out_ref[head] = (grown + add_ref[head]).astype(bf16)


def hand_on(total_map, total_add, state):
    heads = total_map.shape[0]
    return pl.pallas_call(
        hand_on_kernel,
        out_shape=jax.ShapeDtypeStruct(state.shape, bf16),
        compiler_params=pltpu.CompilerParams(vmem_limit_bytes=16 * 2**20),
        cost_estimate=pl.CostEstimate(
            flops=4 * heads * HK**3, bytes_accessed=heads * HK * HK * 12, transcendentals=0
        ),
    )(total_map, total_add, state)


def project_kernel(count, *refs):
    states = refs[: count - 1]
    direct_ref, reach_ref, gain_ref, own_ref = refs[count - 1 : count + 3]
    rights = refs[count + 3 : 2 * count + 2]
    lefts = refs[2 * count + 2 : 3 * count + 1]
    out_ref, slots, sems = refs[3 * count + 1 :]
    mine = lax.axis_index("ctx")
    heads = states[0].shape[0]
    cols = own_ref.shape[1]

    def copy(source, slot):
        return pltpu.make_async_copy(source, slots.at[slot], sems.at[slot])

    copy(own_ref, 0).start()
    for turn in range(1, count):
        pl.when(mine >= turn)(lambda: copy(rights[turn - 1], turn).start())
        pl.when(mine < turn)(lambda: copy(lefts[count - turn - 1], turn).start())
    parts = []
    for head in range(heads):
        lanes = slice(head * HK, (head + 1) * HK)
        state = states[0][head]
        for other in states[1:]:
            state = state + other[head]
        high, low = split(reach_ref[:, lanes])
        out = direct_ref[:, lanes] + dot(
            jnp.concatenate([high, low], axis=1), jnp.concatenate([state, state], axis=0)
        )
        inverse = lax.rsqrt(jnp.mean(out * out, axis=-1, keepdims=True) + 1e-05)
        parts.append((out * inverse * gain_ref[:, lanes]).astype(bf16))
    normed = jnp.concatenate(parts, axis=1)
    for turn in range(count):
        copy(own_ref, turn).wait()
        owner = lax.rem(mine + count - turn, count)
        place = pl.ds(pl.multiple_of(owner * cols, HK), cols)
        out_ref[:, place] = dot(normed, slots[turn]).astype(bf16)


def project(states, direct, reach, gain, own, rights, lefts):
    count = len(states) + 1
    toks, width = direct.shape
    cols = own.shape[1]
    vmem = pl.BlockSpec(memory_space=pltpu.VMEM)
    hbm = pl.BlockSpec(memory_space=pl.ANY)
    return pl.pallas_call(
        functools.partial(project_kernel, count),
        in_specs=[vmem] * (count - 1) + [vmem] * 3 + [hbm] * (2 * count - 1),
        out_specs=vmem,
        out_shape=jax.ShapeDtypeStruct((toks, count * cols), bf16),
        scratch_shapes=[
            pltpu.VMEM((count, width, cols), bf16),
            pltpu.SemaphoreType.DMA((count,)),
        ],
        compiler_params=pltpu.CompilerParams(vmem_limit_bytes=32 * 2**20),
        cost_estimate=pl.CostEstimate(
            flops=2 * toks * width * count * cols,
            bytes_accessed=2 * width * count * cols,
            transcendentals=0,
        ),
    )(*states, direct, reach, gain, own, *rights, *lefts)


def on_shard(place):
    return pl.when(lax.axis_index("ctx") == place)


def head_lanes(heads):
    return [(head, slice(head * HK, (head + 1) * HK)) for head in range(heads)]


def normed_rows(out, gain):
    return (out * lax.rsqrt(jnp.mean(out * out, axis=-1, keepdims=True) + 1e-05) * gain).astype(bf16)


def project_to(out_ref, rows, *weights):
    cols = out_ref.shape[1] // len(weights)
    for index, weight in enumerate(weights):
        parts = weight if isinstance(weight, tuple) else (weight,)
        depth = rows.shape[1] // len(parts)
        found = sum(dot(rows[:, i * depth : (i + 1) * depth], part[...]) for i, part in enumerate(parts))
        out_ref[:, index * cols : (index + 1) * cols] = found.astype(bf16)


def rows_with_state(direct_ref, reach_ref, gain_ref, state_ref, out_ref):
    for head, lanes in head_lanes(state_ref.shape[0]):
        state = state_ref[head]
        out = direct_ref[:, lanes] + dot(
            jnp.concatenate(split(reach_ref[:, lanes]), axis=1), jnp.concatenate([state, state], axis=0)
        )
        out_ref[:, lanes] = normed_rows(out, gain_ref[:, lanes])


def rows_of_next(both_ref, gain_ref, head, lanes, state):
    out = both_ref[0, :, lanes].astype(f32) + dot(both_ref[1, :, lanes], state)
    return normed_rows(out, gain_ref[:, lanes])


def first_rows_kernel(direct_ref, gain_ref, out_ref):
    @on_shard(0)
    def _():
        for head, lanes in head_lanes(direct_ref.shape[1] // HK):
            out_ref[:, lanes] = normed_rows(direct_ref[:, lanes], gain_ref[:, lanes])


def second_rows_kernel(direct_ref, reach_ref, gain_ref, state_ref, out_ref):
    @on_shard(1)
    def _():
        rows_with_state(direct_ref, reach_ref, gain_ref, state_ref, out_ref)


def middle_columns_kernel(both_ref, gain_ref, state_ref, rows1_ref, left_a, left_b, right_ref, out_ref, rows_ref):
    @on_shard(1)
    def _():
        for head, lanes in head_lanes(state_ref.shape[0]):
            rows_ref[:, lanes] = rows_of_next(both_ref, gain_ref, head, lanes, state_ref[head])
        project_to(out_ref, rows_ref[...], (left_a, left_b))

    @on_shard(2)
    def _():
        project_to(out_ref, rows1_ref[...], right_ref)


def fourth_rows_kernel(map_ref, add_ref, both_ref, gain_ref, state_ref, out_ref):
    @on_shard(2)
    def _():
        for head, lanes in head_lanes(state_ref.shape[0]):
            state = state_ref[head]
            left = add_ref[head] + dot(
                jnp.concatenate(split(map_ref[head]), axis=1), jnp.concatenate([state, state], axis=0)
            )
            out_ref[:, lanes] = rows_of_next(both_ref, gain_ref, head, lanes, left.astype(bf16))


def near_columns_kernel(
    direct_ref, reach_ref, gain_ref, state_ref, rows0_ref, rows1_ref, rows3_ref, own_ref, left_ref, left_a, left_b, right_ref,
    own_three, next_three, rows_ref,
):
    @on_shard(0)
    def _():
        project_to(own_three.at[:, : 2 * own_ref.shape[1]], rows0_ref[...], own_ref, right_ref)

    @on_shard(1)
    def _():
        project_to(own_three, rows1_ref[...], own_ref, right_ref, (left_a, left_b))

    @on_shard(2)
    def _():
        weights = (own_ref, right_ref, left_ref)
        project_to(next_three, rows3_ref[...], *weights)
        rows_with_state(direct_ref, reach_ref, gain_ref, state_ref, rows_ref)
        project_to(own_three, rows_ref[...], *weights)


def first_columns_kernel(rows_ref, own_ref, left_ref, out_ref):
    @on_shard(3)
    def _():
        project_to(out_ref, rows_ref[...], left_ref, own_ref)


def last_columns_kernel(rows3_ref, left_a, left_b, out_ref):
    @on_shard(1)
    def _():
        project_to(out_ref, rows3_ref[...], (left_a, left_b))


def call(kernel, operands, out_shapes, scratch=()):
    vmem = pl.BlockSpec(memory_space=pltpu.VMEM)
    shapes = [jax.ShapeDtypeStruct(shape, bf16) for shape in out_shapes]
    found = pl.pallas_call(
        kernel,
        in_specs=[vmem] * len(operands),
        out_specs=[vmem] * len(shapes),
        out_shape=shapes,
        scratch_shapes=[pltpu.VMEM(shape, bf16) for shape in scratch],
        compiler_params=pltpu.CompilerParams(vmem_limit_bytes=16 * 2**20),
        cost_estimate=pl.CostEstimate(flops=2**20, bytes_accessed=2**16, transcendentals=0),
    )(*operands)
    return found if len(shapes) > 1 else found[0]


def assemble_kernel(own_three, next_three, middle_one, first_two, last_one, out_ref):
    cols = last_one.shape[1]
    own = [(own_three, index) for index in range(3)]
    after = [(next_three, index) for index in range(3)]
    sources = (
        (own[0], own[1], (first_two, 0), (first_two, 1)),
        (own[2], own[0], own[1], (middle_one, 0)),
        ((middle_one, 0), own[2], own[0], own[1]),
        ((last_one, 0), after[2], after[0], after[1]),
    )
    for place, blocks in enumerate(sources):

        @on_shard(place)
        def _():
            for index, (ref, block) in enumerate(blocks):
                out_ref[:, index * cols : (index + 1) * cols] = ref[:, block * cols : (block + 1) * cols]


def moved(value, pairs):
    return lax.ppermute(value, "ctx", pairs)


def handed(value, pairs):
    sections, count = lax.axis_size("section"), lax.axis_size("ctx")
    return lax.ppermute(
        value,
        ("section", "ctx"),
        [
            (s * count + a, (s + 1) % sections * count + b)
            for s in range(sections)
            for a, b in pairs
        ],
    )


def on_device(streams, conv_weight, beta_logit, gate_log, norm_gain, w_out):
    count = lax.axis_size("ctx")
    toks, width = streams.shape[1], norm_gain.shape[1]
    x, taps, beta_t, gate_t, edge = load(
        streams[0], conv_weight[0], beta_logit[0].T, gate_log[0].T
    )
    rim = moved(edge, [(c, c + 1) for c in range(count - 1)])
    later_acts = later_activations(x, taps)
    whole = own = w_out[0]
    lefts = [moved(own, [(c, c - 1) for c in range(1, count)])]
    if count == 4:
        top, rest = own[: width // 2], own[width // 2 :]
        rim, later_acts, own, top = lax.optimization_barrier((rim, later_acts, own, top))
        left = moved(own, [(1, 2), (2, 3)])
        top = moved(top, [(0, 1)])
    else:
        rights = [moved(own, [(c, c + 1) for c in range(count - 1)])]
        for turn in range(2, count):
            rights.append(moved(rights[-1], [(c, c + 1) for c in range(turn - 1, count - 1)]))
            lefts.append(moved(lefts[-1], [(c, c - 1) for c in range(1, count - turn + 1)]))
    total_map, total_add, sent, direct, reach, both = shard_terms(
        later_acts, rim, x, taps, beta_t, gate_t
    )
    if count != 4:
        states = [moved(sent, [(0, 1)])]
        for turn in range(1, count - 1):
            states.append(moved(hand_on(total_map, total_add, states[-1]), [(turn, turn + 1)]))
        mixed = project(states, direct, reach, norm_gain, own, rights, lefts)
        return handed(mixed, [(c, c) for c in range(count)])[None]

    right = lefts[0]
    cols = own.shape[1]
    rows = (toks, width)
    one, two, three = ((toks, blocks * cols) for blocks in (1, 2, 3))
    sent, top, right = lax.optimization_barrier((sent, top, lefts[0]))
    first = moved(sent, [(0, 1)])
    both = moved(both, [(3, 2), (2, 1)])
    out1 = hand_on(total_map, total_add, first)
    second = moved(out1, [(1, 2)])
    rows0 = call(first_rows_kernel, [direct, norm_gain], [rows])
    far0 = moved(rows0, [(0, 3)])
    rows1 = call(second_rows_kernel, [direct, reach, norm_gain, first], [rows])
    far1 = moved(rows1, [(1, 2)])
    rest = moved(rest, [(0, 1)])
    both, second = lax.optimization_barrier((both, second))
    rows3 = call(fourth_rows_kernel, [total_map, total_add, both, norm_gain, second], [rows])
    far3 = moved(rows3, [(2, 1)])
    own_three, next_three = call(
        near_columns_kernel,
        [direct, reach, norm_gain, second, rows0, rows1, rows3, whole, left, top, rest, right],
        [three, three],
        [rows],
    )
    middle_one = call(
        middle_columns_kernel, [both, norm_gain, out1, far1, top, rest, right], [one], [rows]
    )
    first_two = call(first_columns_kernel, [far0, whole, left], [two])
    far3, middle_one = lax.optimization_barrier((far3, middle_one))
    last_one = call(last_columns_kernel, [far3, top, rest], [one])
    return call(
        assemble_kernel,
        [
            handed(own_three, [(0, 0), (1, 1), (2, 2)]),
            handed(next_three, [(2, 3)]),
            handed(middle_one, [(1, 2), (2, 1)]),
            handed(first_two, [(3, 0)]),
            handed(last_one, [(1, 3)]),
        ],
        [(toks, 4 * cols)],
    )[None]


def solution(mesh):
    placed = (
        P("section", "ctx", None),
        P("section", None, None),
        P("section", "ctx", None),
        P("section", "ctx", None),
        P("section", None),
        P("section", None, "ctx"),
    )
    return jax.shard_map(
        on_device, mesh=mesh, in_specs=placed, out_specs=P("section", "ctx", None), check_vma=False
    )
```

```python
import functools
import jax
import jax.numpy as jnp
from jax import lax
from jax.experimental import pallas as pl
from jax.experimental.pallas import tpu as pltpu
from jax.sharding import PartitionSpec as P

HK = 128
STEPS = 2
CONV = 4
LEVELS = 6
f32, bf16 = jnp.float32, jnp.bfloat16


def dot(a, b):
    return jnp.dot(a, b, preferred_element_type=f32)


def split(x):
    high = x.astype(bf16)
    return high, (x - high.astype(f32)).astype(bf16)


def dot3(a, b):
    ah, al = split(a)
    bh, bl = split(b)
    return dot(
        jnp.concatenate([ah, ah, al], axis=1), jnp.concatenate([bh, bl, bh], axis=0)
    )


def dot2(a, b):
    return dot(jnp.concatenate(split(a), axis=1), jnp.concatenate([b, b], axis=0))


def pair_rows(left, right):
    zero = jnp.zeros_like(left)
    return jnp.concatenate(
        [jnp.concatenate([left, zero], axis=1), jnp.concatenate([zero, right], axis=1)], axis=0
    )


def blockwise(x):
    return pair_rows(x[:, :HK], x[:, HK:])


def half_terms(u, heads, half, acts, beta_t, gate_t):
    size, toks = STEPS * half, 2 * half
    virt = lax.broadcasted_iota(jnp.int32, (size, toks), 0)
    tok = lax.broadcasted_iota(jnp.int32, (size, toks), 1) - u * half
    inside = ((tok >= 0) & (tok <= (virt & (half - 1)))).astype(f32)
    exact = dict(precision=lax.Precision.HIGHEST, preferred_element_type=f32)
    over_lanes = (((1,), (1,)), ((), ()))
    sums = lax.dot_general(inside, gate_t, over_lanes, **exact)
    sums_t = lax.dot_general(gate_t, inside, over_lanes, **exact)
    steps = (1.0 / (1.0 + jnp.exp(-beta_t))).T[u * half : (u + 1) * half]

    row = lax.broadcasted_iota(jnp.int32, (size, size), 0)
    col = lax.broadcasted_iota(jnp.int32, (size, size), 1)
    row_tok, col_tok = row & (half - 1), col & (half - 1)
    apart = row_tok ^ col_tok
    strict = (col_tok < row_tok) | ((apart == 0) & (col < row))
    upto = (col_tok <= row_tok)[:half]
    eye = (row == col).astype(f32)
    twice = lambda x: jnp.concatenate([x, x], axis=1)
    same = twice(apart == 0)
    before = twice(jnp.where(col_tok < row_tok, apart, 0))
    level_masks = [(before >> level) == 1 for level in range(LEVELS)]

    work = []
    for head in range(heads):
        lanes = slice(head * HK, (head + 1) * HK)
        unit = lambda x: x * lax.rsqrt(jnp.sum(x * x, axis=-1, keepdims=True) + 1e-06)
        queries = unit(acts[0][:, lanes])
        keys = unit(jnp.concatenate([acts[1][:, lanes], acts[2][:, lanes]], axis=0))
        vals = jnp.concatenate([acts[3][:, lanes], acts[4][:, lanes]], axis=0)
        size_col = jnp.concatenate(
            [steps[:, head : head + 1], steps[:, heads + head : heads + head + 1]], axis=0
        )
        c_col = sums[:, head : head + 1]
        c_row = sums_t[head : head + 1]
        c_end = c_col[half - 1 : half]
        keys_t = keys.T
        gram = dot3(jnp.concatenate([keys, queries], axis=0), keys_t)
        damp = jnp.exp(jnp.minimum(c_col[:half] - c_row, 0.0))
        lower = jnp.where(
            strict, size_col * jnp.concatenate([damp, damp], axis=0) * gram[:size], 0.0
        )
        scores = jnp.where(upto, damp * gram[size:], 0.0)
        grown = jnp.exp(c_col)
        right = jnp.concatenate([size_col * vals, (size_col * grown) * keys], axis=1)
        to_end_t = keys_t * jnp.exp(c_end - c_row)
        outer = jnp.concatenate([to_end_t, scores], axis=0)
        work.append((lower, right, outer, queries * grown[:half], jnp.exp(c_end) * eye))

    pairs = range(heads // 2)
    lows, invs = [], []
    for i in pairs:
        low = jnp.concatenate([work[2 * i][0], work[2 * i + 1][0]], axis=1)
        lows.append(low.astype(bf16))
        invs.append((twice(eye) - jnp.where(same, low, 0.0)).astype(bf16))
    for mask in level_masks:
        inner = [
            dot(jnp.where(mask, lows[i], jnp.zeros_like(lows[i])), blockwise(invs[i])).astype(bf16)
            for i in pairs
        ]
        invs = [invs[i] - dot(invs[i], blockwise(inner[i])).astype(bf16) for i in pairs]

    every = range(heads)
    of_head = lambda head: invs[head // 2][:, head % 2 * HK : (head % 2 + 1) * HK]
    firsts = [dot(of_head(head), work[head][1].astype(bf16)).astype(bf16) for head in every]
    rests = [
        work[head][1] - firsts[head].astype(f32) - dot2(work[head][0], firsts[head]) for head in every
    ]
    solved = [
        firsts[head].astype(f32) + dot(of_head(head), rests[head].astype(bf16)) for head in every
    ]
    joint = [dot3(work[head][2], solved[head]) for head in every]
    results = [
        (
            work[head][4] - joint[head][:size, HK:],
            joint[head][:size, :HK],
            joint[head][size:, :HK],
            work[head][3] - joint[head][size:, HK:],
        )
        for head in every
    ]
    return results


def activations(ext, taps_ref, half, heads):
    width = heads * HK
    acts = []
    for part in range(5):
        lanes = slice(part * width, (part + 1) * width)
        total = None
        for tap in range(CONV):
            low = 8 - (CONV - 1) + tap
            term = taps_ref[tap : tap + 1, lanes].astype(f32) * ext[low : low + half, lanes]
            total = term if total is None else total + term
        acts.append(total * (1.0 / (1.0 + jnp.exp(-total))))
    return acts


def load_kernel(*refs):
    sources, targets, edge_ref, sems = refs[:4], refs[4:8], refs[8], refs[9]
    copies = [
        pltpu.make_async_copy(source, target, sems.at[index])
        for index, (source, target) in enumerate(zip(sources, targets))
    ]
    for copy in copies:
        copy.start()
    for copy in copies:
        copy.wait()
    toks = targets[0].shape[0]
    edge_ref[...] = targets[0][toks - 16 :].astype(f32)[16 - (CONV - 1) :].astype(bf16)


def conv_kernel(x_ref, taps_ref, out_ref, ext):
    half, channels = out_ref.shape
    ext[...] = x_ref[half - 16 :].astype(f32)[8:]
    width = channels // 5
    for part, act in enumerate(activations(ext, taps_ref, half, width // HK)):
        out_ref[:, part * width : (part + 1) * width] = act


def later_kernel(act_ref, beta_ref, gate_ref, map_ref, add_ref, direct_ref, reach_ref):
    heads, toks = gate_ref.shape
    width = heads * HK
    acts = [act_ref[:, part * width : (part + 1) * width] for part in range(5)]
    found = half_terms(1, heads, toks // 2, acts, beta_ref[...], gate_ref[...])
    for head, (map2, add2, direct2, reach2) in enumerate(found):
        lanes = slice(head * HK, (head + 1) * HK)
        map_ref[head] = map2
        add_ref[head] = add2
        direct_ref[:, lanes] = direct2
        reach_ref[:, lanes] = reach2


def earlier_kernel(
    rim_ref, x_ref, taps_ref, beta_ref, gate_ref, map2_ref, add2_ref, direct2_ref, reach2_ref,
    map_ref, add_ref, sent_ref, direct_ref, reach_ref, both_ref, ext,
):
    heads, toks = gate_ref.shape
    half = toks // 2
    ext[8 - (CONV - 1) : 8] = rim_ref[...].astype(f32)
    ext[8:] = x_ref[:half].astype(f32)
    acts = activations(ext, taps_ref, half, heads)
    found = half_terms(0, heads, half, acts, beta_ref[...], gate_ref[...])
    all_joined = [
        dot3(
            jnp.concatenate(
                [map2_ref[head], reach2_ref[:, head * HK : (head + 1) * HK]], axis=0
            ),
            jnp.concatenate([map1, add1], axis=1),
        )
        for head, (map1, add1, _, _) in enumerate(found)
    ]
    for head, (_, _, direct1, reach1) in enumerate(found):
        lanes = slice(head * HK, (head + 1) * HK)
        joined = all_joined[head]
        total = joined[:HK, HK:] + add2_ref[head]
        map_ref[head] = joined[:HK, :HK]
        add_ref[head] = total
        sent_ref[head] = total.astype(bf16)
        for rows, direct, reach in (
            (slice(0, half), direct1, reach1),
            (slice(half, toks), joined[HK:, HK:] + direct2_ref[:, lanes], joined[HK:, :HK]),
        ):
            direct_ref[rows, lanes] = direct
            reach_ref[rows, lanes] = reach
            both_ref[0, rows, lanes] = direct.astype(bf16)
            both_ref[1, rows, lanes] = reach.astype(bf16)


def kernel_call(kernel, operands, out_shapes, limit=16, scratch=(), cost=2**16, space=pltpu.VMEM):
    return pl.pallas_call(
        kernel,
        in_specs=[pl.BlockSpec(memory_space=space)] * len(operands),
        out_specs=[pl.BlockSpec(memory_space=pltpu.VMEM)] * len(out_shapes),
        out_shape=[jax.ShapeDtypeStruct(*shape) for shape in out_shapes],
        scratch_shapes=scratch,
        compiler_params=pltpu.CompilerParams(vmem_limit_bytes=limit * 2**20),
        cost_estimate=pl.CostEstimate(flops=2**20, bytes_accessed=cost, transcendentals=0),
    )(*operands)


def load(*sources):
    sources = [pltpu.with_memory_space_constraint(x, pltpu.HBM) for x in sources]
    edge = ((CONV - 1, sources[0].shape[1]), bf16)
    return pl.pallas_call(
        load_kernel,
        in_specs=[pl.BlockSpec(memory_space=pltpu.HBM)] * len(sources),
        out_specs=[pl.BlockSpec(memory_space=pltpu.VMEM)] * (len(sources) + 1),
        out_shape=[pltpu.VMEM(x.shape, x.dtype) for x in sources] + [pltpu.VMEM(*edge)],
        scratch_shapes=[pltpu.SemaphoreType.DMA((len(sources),))],
        compiler_params=pltpu.CompilerParams(vmem_limit_bytes=2**22),
    )(*sources)


def later_activations(x, taps):
    toks, channels = x.shape
    half = toks // 2
    return kernel_call(
        conv_kernel,
        (x, taps),
        [((half, channels), f32)],
        scratch=[pltpu.VMEM((8 + half, channels), f32)],
    )[0]


def shard_terms(later_acts, rim, x, taps, beta_t, gate_t):
    toks, channels = x.shape
    heads = gate_t.shape[0]
    half = toks // 2
    square, rows, half_rows = (heads, HK, HK), (toks, heads * HK), (half, heads * HK)
    later = kernel_call(
        later_kernel,
        (later_acts, beta_t, gate_t),
        [(square, f32)] * 2 + [(half_rows, f32)] * 2,
        limit=32,
    )
    return kernel_call(
        earlier_kernel,
        (rim, x, taps, beta_t, gate_t, *later),
        [(square, f32)] * 2 + [(square, bf16)] + [(rows, f32)] * 2 + [((2,) + rows, bf16)],
        limit=32,
        scratch=[pltpu.VMEM((8 + half, channels), f32)],
    )


def hand_on_kernel(map_ref, add_ref, state_ref, out_ref):
    for head in range(map_ref.shape[0]):
        high, low = split(map_ref[head])
        state = state_ref[head]
        grown = dot(
            jnp.concatenate([high, low], axis=1), jnp.concatenate([state, state], axis=0)
        )
        out_ref[head] = (grown + add_ref[head]).astype(bf16)


def hand_on(total_map, total_add, state):
    heads = total_map.shape[0]
    return pl.pallas_call(
        hand_on_kernel,
        out_shape=jax.ShapeDtypeStruct(state.shape, bf16),
        compiler_params=pltpu.CompilerParams(vmem_limit_bytes=16 * 2**20),
        cost_estimate=pl.CostEstimate(
            flops=4 * heads * HK**3, bytes_accessed=heads * HK * HK * 12, transcendentals=0
        ),
    )(total_map, total_add, state)


def project_kernel(count, *refs):
    states = refs[: count - 1]
    direct_ref, reach_ref, gain_ref, own_ref = refs[count - 1 : count + 3]
    rights = refs[count + 3 : 2 * count + 2]
    lefts = refs[2 * count + 2 : 3 * count + 1]
    out_ref, slots, sems = refs[3 * count + 1 :]
    mine = lax.axis_index("ctx")
    heads = states[0].shape[0]
    cols = own_ref.shape[1]

    def copy(source, slot):
        return pltpu.make_async_copy(source, slots.at[slot], sems.at[slot])

    copy(own_ref, 0).start()
    for turn in range(1, count):
        pl.when(mine >= turn)(lambda: copy(rights[turn - 1], turn).start())
        pl.when(mine < turn)(lambda: copy(lefts[count - turn - 1], turn).start())
    parts = []
    for head in range(heads):
        lanes = slice(head * HK, (head + 1) * HK)
        state = states[0][head]
        for other in states[1:]:
            state = state + other[head]
        high, low = split(reach_ref[:, lanes])
        out = direct_ref[:, lanes] + dot(
            jnp.concatenate([high, low], axis=1), jnp.concatenate([state, state], axis=0)
        )
        inverse = lax.rsqrt(jnp.mean(out * out, axis=-1, keepdims=True) + 1e-05)
        parts.append((out * inverse * gain_ref[:, lanes]).astype(bf16))
    normed = jnp.concatenate(parts, axis=1)
    for turn in range(count):
        copy(own_ref, turn).wait()
        owner = lax.rem(mine + count - turn, count)
        place = pl.ds(pl.multiple_of(owner * cols, HK), cols)
        out_ref[:, place] = dot(normed, slots[turn]).astype(bf16)


def project(states, direct, reach, gain, own, rights, lefts):
    count = len(states) + 1
    toks, width = direct.shape
    cols = own.shape[1]
    vmem = pl.BlockSpec(memory_space=pltpu.VMEM)
    hbm = pl.BlockSpec(memory_space=pl.ANY)
    return pl.pallas_call(
        functools.partial(project_kernel, count),
        in_specs=[vmem] * (count - 1) + [vmem] * 3 + [hbm] * (2 * count - 1),
        out_specs=vmem,
        out_shape=jax.ShapeDtypeStruct((toks, count * cols), bf16),
        scratch_shapes=[
            pltpu.VMEM((count, width, cols), bf16),
            pltpu.SemaphoreType.DMA((count,)),
        ],
        compiler_params=pltpu.CompilerParams(vmem_limit_bytes=32 * 2**20),
        cost_estimate=pl.CostEstimate(
            flops=2 * toks * width * count * cols,
            bytes_accessed=2 * width * count * cols,
            transcendentals=0,
        ),
    )(*states, direct, reach, gain, own, *rights, *lefts)


def on_shard(place):
    return pl.when(lax.axis_index("ctx") == place)


def head_lanes(heads):
    return [(head, slice(head * HK, (head + 1) * HK)) for head in range(heads)]


def normed_rows(out, gain):
    return (out * lax.rsqrt(jnp.mean(out * out, axis=-1, keepdims=True) + 1e-05) * gain).astype(bf16)


def project_to(out_ref, rows, *weights):
    cols = out_ref.shape[1] // len(weights)
    for index, weight in enumerate(weights):
        parts = weight if isinstance(weight, tuple) else (weight,)
        depth = rows.shape[1] // len(parts)
        found = sum(dot(rows[:, i * depth : (i + 1) * depth], part[...]) for i, part in enumerate(parts))
        out_ref[:, index * cols : (index + 1) * cols] = found.astype(bf16)


def rows_with_state(direct_ref, reach_ref, gain_ref, state_ref, out_ref):
    for head, lanes in head_lanes(state_ref.shape[0]):
        state = state_ref[head]
        out = direct_ref[:, lanes] + dot(
            jnp.concatenate(split(reach_ref[:, lanes]), axis=1), jnp.concatenate([state, state], axis=0)
        )
        out_ref[:, lanes] = normed_rows(out, gain_ref[:, lanes])


def rows_of_next(both_ref, gain_ref, head, lanes, state):
    out = both_ref[0, :, lanes].astype(f32) + dot(both_ref[1, :, lanes], state)
    return normed_rows(out, gain_ref[:, lanes])


def first_rows_kernel(direct_ref, gain_ref, out_ref):
    @on_shard(0)
    def _():
        for head, lanes in head_lanes(direct_ref.shape[1] // HK):
            out_ref[:, lanes] = normed_rows(direct_ref[:, lanes], gain_ref[:, lanes])


def second_rows_kernel(direct_ref, reach_ref, gain_ref, state_ref, out_ref):
    @on_shard(1)
    def _():
        rows_with_state(direct_ref, reach_ref, gain_ref, state_ref, out_ref)


def middle_columns_kernel(both_ref, gain_ref, state_ref, rows1_ref, left_a, left_b, right_ref, out_ref, rows_ref):
    @on_shard(1)
    def _():
        for head, lanes in head_lanes(state_ref.shape[0]):
            rows_ref[:, lanes] = rows_of_next(both_ref, gain_ref, head, lanes, state_ref[head])
        project_to(out_ref, rows_ref[...], (left_a, left_b))

    @on_shard(2)
    def _():
        project_to(out_ref, rows1_ref[...], right_ref)


def fourth_rows_kernel(map_ref, add_ref, both_ref, gain_ref, state_ref, out_ref):
    @on_shard(2)
    def _():
        for head, lanes in head_lanes(state_ref.shape[0]):
            state = state_ref[head]
            left = add_ref[head] + dot(
                jnp.concatenate(split(map_ref[head]), axis=1), jnp.concatenate([state, state], axis=0)
            )
            out_ref[:, lanes] = rows_of_next(both_ref, gain_ref, head, lanes, left.astype(bf16))


def near_columns_kernel(
    direct_ref, reach_ref, gain_ref, state_ref, rows0_ref, rows1_ref, rows3_ref, own_ref, left_ref, left_a, left_b, right_ref,
    own_three, next_three, rows_ref,
):
    @on_shard(0)
    def _():
        project_to(own_three.at[:, : 2 * own_ref.shape[1]], rows0_ref[...], own_ref, right_ref)

    @on_shard(1)
    def _():
        project_to(own_three, rows1_ref[...], own_ref, right_ref, (left_a, left_b))

    @on_shard(2)
    def _():
        weights = (own_ref, right_ref, left_ref)
        project_to(next_three, rows3_ref[...], *weights)
        rows_with_state(direct_ref, reach_ref, gain_ref, state_ref, rows_ref)
        project_to(own_three, rows_ref[...], *weights)


def first_columns_kernel(rows_ref, own_ref, left_ref, out_ref):
    @on_shard(3)
    def _():
        project_to(out_ref, rows_ref[...], left_ref, own_ref)


def last_columns_kernel(rows3_ref, left_a, left_b, out_ref):
    @on_shard(1)
    def _():
        project_to(out_ref, rows3_ref[...], (left_a, left_b))


def call(kernel, operands, out_shapes, scratch=()):
    vmem = pl.BlockSpec(memory_space=pltpu.VMEM)
    shapes = [jax.ShapeDtypeStruct(shape, bf16) for shape in out_shapes]
    found = pl.pallas_call(
        kernel,
        in_specs=[vmem] * len(operands),
        out_specs=[vmem] * len(shapes),
        out_shape=shapes,
        scratch_shapes=[pltpu.VMEM(shape, bf16) for shape in scratch],
        compiler_params=pltpu.CompilerParams(vmem_limit_bytes=16 * 2**20),
        cost_estimate=pl.CostEstimate(flops=2**20, bytes_accessed=2**16, transcendentals=0),
    )(*operands)
    return found if len(shapes) > 1 else found[0]


def assemble_kernel(own_three, next_three, middle_one, first_two, last_one, out_ref):
    cols = last_one.shape[1]
    own = [(own_three, index) for index in range(3)]
    after = [(next_three, index) for index in range(3)]
    sources = (
        (own[0], own[1], (first_two, 0), (first_two, 1)),
        (own[2], own[0], own[1], (middle_one, 0)),
        ((middle_one, 0), own[2], own[0], own[1]),
        ((last_one, 0), after[2], after[0], after[1]),
    )
    for place, blocks in enumerate(sources):

        @on_shard(place)
        def _():
            for index, (ref, block) in enumerate(blocks):
                out_ref[:, index * cols : (index + 1) * cols] = ref[:, block * cols : (block + 1) * cols]


def moved(value, pairs):
    return lax.ppermute(value, "ctx", pairs)


def handed(value, pairs):
    sections, count = lax.axis_size("section"), lax.axis_size("ctx")
    return lax.ppermute(
        value,
        ("section", "ctx"),
        [
            (s * count + a, (s + 1) % sections * count + b)
            for s in range(sections)
            for a, b in pairs
        ],
    )


def on_device(streams, conv_weight, beta_logit, gate_log, norm_gain, w_out):
    count = lax.axis_size("ctx")
    toks, width = streams.shape[1], norm_gain.shape[1]
    x, taps, beta_t, gate_t, edge = load(
        streams[0], conv_weight[0], beta_logit[0].T, gate_log[0].T
    )
    rim = moved(edge, [(c, c + 1) for c in range(count - 1)])
    later_acts = later_activations(x, taps)
    whole = own = w_out[0]
    lefts = [moved(own, [(c, c - 1) for c in range(1, count)])]
    if count == 4:
        top, rest = own[: width // 2], own[width // 2 :]
        rim, later_acts, own, top = lax.optimization_barrier((rim, later_acts, own, top))
        left = moved(own, [(1, 2), (2, 3)])
        top = moved(top, [(0, 1)])
    else:
        rights = [moved(own, [(c, c + 1) for c in range(count - 1)])]
        for turn in range(2, count):
            rights.append(moved(rights[-1], [(c, c + 1) for c in range(turn - 1, count - 1)]))
            lefts.append(moved(lefts[-1], [(c, c - 1) for c in range(1, count - turn + 1)]))
    total_map, total_add, sent, direct, reach, both = shard_terms(
        later_acts, rim, x, taps, beta_t, gate_t
    )
    if count != 4:
        states = [moved(sent, [(0, 1)])]
        for turn in range(1, count - 1):
            states.append(moved(hand_on(total_map, total_add, states[-1]), [(turn, turn + 1)]))
        mixed = project(states, direct, reach, norm_gain, own, rights, lefts)
        return handed(mixed, [(c, c) for c in range(count)])[None]

    right = lefts[0]
    cols = own.shape[1]
    rows = (toks, width)
    one, two, three = ((toks, blocks * cols) for blocks in (1, 2, 3))
    sent, top = lax.optimization_barrier((sent, top))
    both, right = lax.optimization_barrier((both, lefts[0]))
    first = moved(sent, [(0, 1)])
    both = moved(both, [(3, 2), (2, 1)])
    out1 = hand_on(total_map, total_add, first)
    second = moved(out1, [(1, 2)])
    rows0 = call(first_rows_kernel, [direct, norm_gain], [rows])
    far0 = moved(rows0, [(0, 3)])
    rows1 = call(second_rows_kernel, [direct, reach, norm_gain, first], [rows])
    far1 = moved(rows1, [(1, 2)])
    rest = moved(rest, [(0, 1)])
    both, second = lax.optimization_barrier((both, second))
    rows3 = call(fourth_rows_kernel, [total_map, total_add, both, norm_gain, second], [rows])
    far3 = moved(rows3, [(2, 1)])
    own_three, next_three = call(
        near_columns_kernel,
        [direct, reach, norm_gain, second, rows0, rows1, rows3, whole, left, top, rest, right],
        [three, three],
        [rows],
    )
    middle_one = call(
        middle_columns_kernel, [both, norm_gain, out1, far1, top, rest, right], [one], [rows]
    )
    first_two = call(first_columns_kernel, [far0, whole, left], [two])
    far3, middle_one = lax.optimization_barrier((far3, middle_one))
    last_one = call(last_columns_kernel, [far3, top, rest], [one])
    return call(
        assemble_kernel,
        [
            handed(own_three, [(0, 0), (1, 1), (2, 2)]),
            handed(next_three, [(2, 3)]),
            handed(middle_one, [(1, 2), (2, 1)]),
            handed(first_two, [(3, 0)]),
            handed(last_one, [(1, 3)]),
        ],
        [(toks, 4 * cols)],
    )[None]


def solution(mesh):
    placed = (
        P("section", "ctx", None),
        P("section", None, None),
        P("section", "ctx", None),
        P("section", "ctx", None),
        P("section", None),
        P("section", None, "ctx"),
    )
    return jax.shard_map(
        on_device, mesh=mesh, in_specs=placed, out_specs=P("section", "ctx", None), check_vma=False
    )
```

```python
import functools
import jax
import jax.numpy as jnp
from jax import lax
from jax.experimental import pallas as pl
from jax.experimental.pallas import tpu as pltpu
from jax.sharding import PartitionSpec as P

HK = 128
STEPS = 2
CONV = 4
LEVELS = 6
f32, bf16 = jnp.float32, jnp.bfloat16


def dot(a, b):
    return jnp.dot(a, b, preferred_element_type=f32)


def split(x):
    high = x.astype(bf16)
    return high, (x - high.astype(f32)).astype(bf16)


def dot3(a, b):
    ah, al = split(a)
    bh, bl = split(b)
    return dot(
        jnp.concatenate([ah, ah, al], axis=1), jnp.concatenate([bh, bl, bh], axis=0)
    )


def dot2(a, b):
    return dot(jnp.concatenate(split(a), axis=1), jnp.concatenate([b, b], axis=0))


def pair_rows(left, right):
    zero = jnp.zeros_like(left)
    return jnp.concatenate(
        [jnp.concatenate([left, zero], axis=1), jnp.concatenate([zero, right], axis=1)], axis=0
    )


def blockwise(x):
    return pair_rows(x[:, :HK], x[:, HK:])


def half_terms(u, heads, half, acts, beta_t, gate_t):
    size, toks = STEPS * half, 2 * half
    virt = lax.broadcasted_iota(jnp.int32, (size, toks), 0)
    tok = lax.broadcasted_iota(jnp.int32, (size, toks), 1) - u * half
    inside = ((tok >= 0) & (tok <= (virt & (half - 1)))).astype(f32)
    exact = dict(precision=lax.Precision.HIGHEST, preferred_element_type=f32)
    over_lanes = (((1,), (1,)), ((), ()))
    sums = lax.dot_general(inside, gate_t, over_lanes, **exact)
    sums_t = lax.dot_general(gate_t, inside, over_lanes, **exact)
    steps = (1.0 / (1.0 + jnp.exp(-beta_t))).T[u * half : (u + 1) * half]

    row = lax.broadcasted_iota(jnp.int32, (size, size), 0)
    col = lax.broadcasted_iota(jnp.int32, (size, size), 1)
    row_tok, col_tok = row & (half - 1), col & (half - 1)
    apart = row_tok ^ col_tok
    strict = (col_tok < row_tok) | ((apart == 0) & (col < row))
    upto = (col_tok <= row_tok)[:half]
    eye = (row == col).astype(f32)
    twice = lambda x: jnp.concatenate([x, x], axis=1)
    same = twice(apart == 0)
    before = twice(jnp.where(col_tok < row_tok, apart, 0))
    level_masks = [(before >> level) == 1 for level in range(LEVELS)]

    work = []
    for head in range(heads):
        lanes = slice(head * HK, (head + 1) * HK)
        unit = lambda x: x * lax.rsqrt(jnp.sum(x * x, axis=-1, keepdims=True) + 1e-06)
        queries = unit(acts[0][:, lanes])
        keys = unit(jnp.concatenate([acts[1][:, lanes], acts[2][:, lanes]], axis=0))
        vals = jnp.concatenate([acts[3][:, lanes], acts[4][:, lanes]], axis=0)
        size_col = jnp.concatenate(
            [steps[:, head : head + 1], steps[:, heads + head : heads + head + 1]], axis=0
        )
        c_col = sums[:, head : head + 1]
        c_row = sums_t[head : head + 1]
        c_end = c_col[half - 1 : half]
        keys_t = keys.T
        gram = dot3(jnp.concatenate([keys, queries], axis=0), keys_t)
        damp = jnp.exp(jnp.minimum(c_col[:half] - c_row, 0.0))
        lower = jnp.where(
            strict, size_col * jnp.concatenate([damp, damp], axis=0) * gram[:size], 0.0
        )
        scores = jnp.where(upto, damp * gram[size:], 0.0)
        grown = jnp.exp(c_col)
        right = jnp.concatenate([size_col * vals, (size_col * grown) * keys], axis=1)
        to_end_t = keys_t * jnp.exp(c_end - c_row)
        outer = jnp.concatenate([to_end_t, scores], axis=0)
        work.append((lower, right, outer, queries * grown[:half], jnp.exp(c_end) * eye))

    pairs = range(heads // 2)
    lows, invs = [], []
    for i in pairs:
        low = jnp.concatenate([work[2 * i][0], work[2 * i + 1][0]], axis=1)
        lows.append(low.astype(bf16))
        invs.append((twice(eye) - jnp.where(same, low, 0.0)).astype(bf16))
    for mask in level_masks:
        inner = [
            dot(jnp.where(mask, lows[i], jnp.zeros_like(lows[i])), blockwise(invs[i])).astype(bf16)
            for i in pairs
        ]
        invs = [invs[i] - dot(invs[i], blockwise(inner[i])).astype(bf16) for i in pairs]

    every = range(heads)
    of_head = lambda head: invs[head // 2][:, head % 2 * HK : (head % 2 + 1) * HK]
    firsts = [dot(of_head(head), work[head][1].astype(bf16)).astype(bf16) for head in every]
    rests = [
        work[head][1] - firsts[head].astype(f32) - dot2(work[head][0], firsts[head]) for head in every
    ]
    solved = [
        firsts[head].astype(f32) + dot(of_head(head), rests[head].astype(bf16)) for head in every
    ]
    joint = [dot3(work[head][2], solved[head]) for head in every]
    results = [
        (
            work[head][4] - joint[head][:size, HK:],
            joint[head][:size, :HK],
            joint[head][size:, :HK],
            work[head][3] - joint[head][size:, HK:],
        )
        for head in every
    ]
    return results


def activations(ext, taps_ref, half, heads):
    width = heads * HK
    acts = []
    for part in range(5):
        lanes = slice(part * width, (part + 1) * width)
        total = None
        for tap in range(CONV):
            low = 8 - (CONV - 1) + tap
            term = taps_ref[tap : tap + 1, lanes].astype(f32) * ext[low : low + half, lanes]
            total = term if total is None else total + term
        acts.append(total * (1.0 / (1.0 + jnp.exp(-total))))
    return acts


def load_kernel(*refs):
    sources, targets, edge_ref, sems = refs[:4], refs[4:8], refs[8], refs[9]
    copies = [
        pltpu.make_async_copy(source, target, sems.at[index])
        for index, (source, target) in enumerate(zip(sources, targets))
    ]
    for copy in copies:
        copy.start()
    for copy in copies:
        copy.wait()
    toks = targets[0].shape[0]
    edge_ref[...] = targets[0][toks - 16 :].astype(f32)[16 - (CONV - 1) :].astype(bf16)


def conv_kernel(x_ref, taps_ref, out_ref, ext):
    half, channels = out_ref.shape
    ext[...] = x_ref[half - 16 :].astype(f32)[8:]
    width = channels // 5
    for part, act in enumerate(activations(ext, taps_ref, half, width // HK)):
        out_ref[:, part * width : (part + 1) * width] = act


def later_kernel(act_ref, beta_ref, gate_ref, map_ref, add_ref, direct_ref, reach_ref):
    heads, toks = gate_ref.shape
    width = heads * HK
    acts = [act_ref[:, part * width : (part + 1) * width] for part in range(5)]
    found = half_terms(1, heads, toks // 2, acts, beta_ref[...], gate_ref[...])
    for head, (map2, add2, direct2, reach2) in enumerate(found):
        lanes = slice(head * HK, (head + 1) * HK)
        map_ref[head] = map2
        add_ref[head] = add2
        direct_ref[:, lanes] = direct2
        reach_ref[:, lanes] = reach2


def earlier_kernel(
    rim_ref, x_ref, taps_ref, beta_ref, gate_ref, map2_ref, add2_ref, direct2_ref, reach2_ref,
    map_ref, add_ref, sent_ref, direct_ref, reach_ref, both_ref, ext,
):
    heads, toks = gate_ref.shape
    half = toks // 2
    ext[8 - (CONV - 1) : 8] = rim_ref[...].astype(f32)
    ext[8:] = x_ref[:half].astype(f32)
    acts = activations(ext, taps_ref, half, heads)
    found = half_terms(0, heads, half, acts, beta_ref[...], gate_ref[...])
    all_joined = [
        dot3(
            jnp.concatenate(
                [map2_ref[head], reach2_ref[:, head * HK : (head + 1) * HK]], axis=0
            ),
            jnp.concatenate([map1, add1], axis=1),
        )
        for head, (map1, add1, _, _) in enumerate(found)
    ]
    for head, (_, _, direct1, reach1) in enumerate(found):
        lanes = slice(head * HK, (head + 1) * HK)
        joined = all_joined[head]
        total = joined[:HK, HK:] + add2_ref[head]
        map_ref[head] = joined[:HK, :HK]
        add_ref[head] = total
        sent_ref[head] = total.astype(bf16)
        for rows, direct, reach in (
            (slice(0, half), direct1, reach1),
            (slice(half, toks), joined[HK:, HK:] + direct2_ref[:, lanes], joined[HK:, :HK]),
        ):
            direct_ref[rows, lanes] = direct
            reach_ref[rows, lanes] = reach
            both_ref[0, rows, lanes] = direct.astype(bf16)
            both_ref[1, rows, lanes] = reach.astype(bf16)


def kernel_call(kernel, operands, out_shapes, limit=16, scratch=(), cost=2**16, space=pltpu.VMEM):
    return pl.pallas_call(
        kernel,
        in_specs=[pl.BlockSpec(memory_space=space)] * len(operands),
        out_specs=[pl.BlockSpec(memory_space=pltpu.VMEM)] * len(out_shapes),
        out_shape=[jax.ShapeDtypeStruct(*shape) for shape in out_shapes],
        scratch_shapes=scratch,
        compiler_params=pltpu.CompilerParams(vmem_limit_bytes=limit * 2**20),
        cost_estimate=pl.CostEstimate(flops=2**20, bytes_accessed=cost, transcendentals=0),
    )(*operands)


def load(*sources):
    sources = [pltpu.with_memory_space_constraint(x, pltpu.HBM) for x in sources]
    edge = ((CONV - 1, sources[0].shape[1]), bf16)
    return pl.pallas_call(
        load_kernel,
        in_specs=[pl.BlockSpec(memory_space=pltpu.HBM)] * len(sources),
        out_specs=[pl.BlockSpec(memory_space=pltpu.VMEM)] * (len(sources) + 1),
        out_shape=[pltpu.VMEM(x.shape, x.dtype) for x in sources] + [pltpu.VMEM(*edge)],
        scratch_shapes=[pltpu.SemaphoreType.DMA((len(sources),))],
        compiler_params=pltpu.CompilerParams(vmem_limit_bytes=2**22),
    )(*sources)


def later_activations(x, taps):
    toks, channels = x.shape
    half = toks // 2
    return kernel_call(
        conv_kernel,
        (x, taps),
        [((half, channels), f32)],
        scratch=[pltpu.VMEM((8 + half, channels), f32)],
    )[0]


def shard_terms(later_acts, rim, x, taps, beta_t, gate_t):
    toks, channels = x.shape
    heads = gate_t.shape[0]
    half = toks // 2
    square, rows, half_rows = (heads, HK, HK), (toks, heads * HK), (half, heads * HK)
    later = kernel_call(
        later_kernel,
        (later_acts, beta_t, gate_t),
        [(square, f32)] * 2 + [(half_rows, f32)] * 2,
        limit=32,
    )
    return kernel_call(
        earlier_kernel,
        (rim, x, taps, beta_t, gate_t, *later),
        [(square, f32)] * 2 + [(square, bf16)] + [(rows, f32)] * 2 + [((2,) + rows, bf16)],
        limit=32,
        scratch=[pltpu.VMEM((8 + half, channels), f32)],
    )


def hand_on_kernel(map_ref, add_ref, state_ref, out_ref):
    for head in range(map_ref.shape[0]):
        high, low = split(map_ref[head])
        state = state_ref[head]
        grown = dot(
            jnp.concatenate([high, low], axis=1), jnp.concatenate([state, state], axis=0)
        )
        out_ref[head] = (grown + add_ref[head]).astype(bf16)


def hand_on(total_map, total_add, state):
    heads = total_map.shape[0]
    return pl.pallas_call(
        hand_on_kernel,
        out_shape=jax.ShapeDtypeStruct(state.shape, bf16),
        compiler_params=pltpu.CompilerParams(vmem_limit_bytes=16 * 2**20),
        cost_estimate=pl.CostEstimate(
            flops=4 * heads * HK**3, bytes_accessed=heads * HK * HK * 12, transcendentals=0
        ),
    )(total_map, total_add, state)


def project_kernel(count, *refs):
    states = refs[: count - 1]
    direct_ref, reach_ref, gain_ref, own_ref = refs[count - 1 : count + 3]
    rights = refs[count + 3 : 2 * count + 2]
    lefts = refs[2 * count + 2 : 3 * count + 1]
    out_ref, slots, sems = refs[3 * count + 1 :]
    mine = lax.axis_index("ctx")
    heads = states[0].shape[0]
    cols = own_ref.shape[1]

    def copy(source, slot):
        return pltpu.make_async_copy(source, slots.at[slot], sems.at[slot])

    copy(own_ref, 0).start()
    for turn in range(1, count):
        pl.when(mine >= turn)(lambda: copy(rights[turn - 1], turn).start())
        pl.when(mine < turn)(lambda: copy(lefts[count - turn - 1], turn).start())
    parts = []
    for head in range(heads):
        lanes = slice(head * HK, (head + 1) * HK)
        state = states[0][head]
        for other in states[1:]:
            state = state + other[head]
        high, low = split(reach_ref[:, lanes])
        out = direct_ref[:, lanes] + dot(
            jnp.concatenate([high, low], axis=1), jnp.concatenate([state, state], axis=0)
        )
        inverse = lax.rsqrt(jnp.mean(out * out, axis=-1, keepdims=True) + 1e-05)
        parts.append((out * inverse * gain_ref[:, lanes]).astype(bf16))
    normed = jnp.concatenate(parts, axis=1)
    for turn in range(count):
        copy(own_ref, turn).wait()
        owner = lax.rem(mine + count - turn, count)
        place = pl.ds(pl.multiple_of(owner * cols, HK), cols)
        out_ref[:, place] = dot(normed, slots[turn]).astype(bf16)


def project(states, direct, reach, gain, own, rights, lefts):
    count = len(states) + 1
    toks, width = direct.shape
    cols = own.shape[1]
    vmem = pl.BlockSpec(memory_space=pltpu.VMEM)
    hbm = pl.BlockSpec(memory_space=pl.ANY)
    return pl.pallas_call(
        functools.partial(project_kernel, count),
        in_specs=[vmem] * (count - 1) + [vmem] * 3 + [hbm] * (2 * count - 1),
        out_specs=vmem,
        out_shape=jax.ShapeDtypeStruct((toks, count * cols), bf16),
        scratch_shapes=[
            pltpu.VMEM((count, width, cols), bf16),
            pltpu.SemaphoreType.DMA((count,)),
        ],
        compiler_params=pltpu.CompilerParams(vmem_limit_bytes=32 * 2**20),
        cost_estimate=pl.CostEstimate(
            flops=2 * toks * width * count * cols,
            bytes_accessed=2 * width * count * cols,
            transcendentals=0,
        ),
    )(*states, direct, reach, gain, own, *rights, *lefts)


def on_shard(place):
    return pl.when(lax.axis_index("ctx") == place)


def head_lanes(heads):
    return [(head, slice(head * HK, (head + 1) * HK)) for head in range(heads)]


def normed_rows(out, gain):
    return (out * lax.rsqrt(jnp.mean(out * out, axis=-1, keepdims=True) + 1e-05) * gain).astype(bf16)


def project_to(out_ref, rows, *weights):
    cols = out_ref.shape[1] // len(weights)
    for index, weight in enumerate(weights):
        parts = weight if isinstance(weight, tuple) else (weight,)
        depth = rows.shape[1] // len(parts)
        found = sum(dot(rows[:, i * depth : (i + 1) * depth], part[...]) for i, part in enumerate(parts))
        out_ref[:, index * cols : (index + 1) * cols] = found.astype(bf16)


def rows_with_state(direct_ref, reach_ref, gain_ref, state_ref, out_ref):
    places = head_lanes(state_ref.shape[0])
    outs = [
        direct_ref[:, lanes]
        + dot(
            jnp.concatenate(split(reach_ref[:, lanes]), axis=1),
            jnp.concatenate([state_ref[head], state_ref[head]], axis=0),
        )
        for head, lanes in places
    ]
    for head, lanes in places:
        out_ref[:, lanes] = normed_rows(outs[head], gain_ref[:, lanes])


def rows_of_next(both_ref, gain_ref, states, out_ref):
    places = head_lanes(len(states))
    outs = [
        both_ref[0, :, lanes].astype(f32) + dot(both_ref[1, :, lanes], states[head])
        for head, lanes in places
    ]
    for head, lanes in places:
        out_ref[:, lanes] = normed_rows(outs[head], gain_ref[:, lanes])


def first_rows_kernel(direct_ref, gain_ref, out_ref):
    @on_shard(0)
    def _():
        for head, lanes in head_lanes(direct_ref.shape[1] // HK):
            out_ref[:, lanes] = normed_rows(direct_ref[:, lanes], gain_ref[:, lanes])


def second_rows_kernel(direct_ref, reach_ref, gain_ref, state_ref, out_ref):
    @on_shard(1)
    def _():
        rows_with_state(direct_ref, reach_ref, gain_ref, state_ref, out_ref)


def middle_columns_kernel(both_ref, gain_ref, state_ref, rows1_ref, left_a, left_b, right_ref, out_ref, rows_ref):
    @on_shard(1)
    def _():
        states = [state_ref[head] for head in range(state_ref.shape[0])]
        rows_of_next(both_ref, gain_ref, states, rows_ref)
        project_to(out_ref, rows_ref[...], (left_a, left_b))

    @on_shard(2)
    def _():
        project_to(out_ref, rows1_ref[...], right_ref)


def fourth_rows_kernel(map_ref, add_ref, both_ref, gain_ref, state_ref, out_ref):
    @on_shard(2)
    def _():
        lefts = [
            add_ref[head]
            + dot(
                jnp.concatenate(split(map_ref[head]), axis=1),
                jnp.concatenate([state_ref[head], state_ref[head]], axis=0),
            )
            for head in range(state_ref.shape[0])
        ]
        rows_of_next(both_ref, gain_ref, [left.astype(bf16) for left in lefts], out_ref)


def near_columns_kernel(
    direct_ref, reach_ref, gain_ref, state_ref, rows0_ref, rows1_ref, rows3_ref, own_ref, left_ref, left_a, left_b, right_ref,
    own_three, next_three, rows_ref,
):
    @on_shard(0)
    def _():
        project_to(own_three.at[:, : 2 * own_ref.shape[1]], rows0_ref[...], own_ref, right_ref)

    @on_shard(1)
    def _():
        project_to(own_three, rows1_ref[...], own_ref, right_ref, (left_a, left_b))

    @on_shard(2)
    def _():
        weights = (own_ref, right_ref, left_ref)
        project_to(next_three, rows3_ref[...], *weights)
        rows_with_state(direct_ref, reach_ref, gain_ref, state_ref, rows_ref)
        project_to(own_three, rows_ref[...], *weights)


def first_columns_kernel(rows_ref, own_ref, left_ref, out_ref):
    @on_shard(3)
    def _():
        project_to(out_ref, rows_ref[...], left_ref, own_ref)


def last_columns_kernel(rows3_ref, left_a, left_b, out_ref):
    @on_shard(1)
    def _():
        project_to(out_ref, rows3_ref[...], (left_a, left_b))


def call(kernel, operands, out_shapes, scratch=()):
    vmem = pl.BlockSpec(memory_space=pltpu.VMEM)
    shapes = [jax.ShapeDtypeStruct(shape, bf16) for shape in out_shapes]
    found = pl.pallas_call(
        kernel,
        in_specs=[vmem] * len(operands),
        out_specs=[vmem] * len(shapes),
        out_shape=shapes,
        scratch_shapes=[pltpu.VMEM(shape, bf16) for shape in scratch],
        compiler_params=pltpu.CompilerParams(vmem_limit_bytes=16 * 2**20),
        cost_estimate=pl.CostEstimate(flops=2**20, bytes_accessed=2**16, transcendentals=0),
    )(*operands)
    return found if len(shapes) > 1 else found[0]


def assemble_kernel(own_three, next_three, middle_one, first_two, last_one, out_ref):
    cols = last_one.shape[1]
    own = [(own_three, index) for index in range(3)]
    after = [(next_three, index) for index in range(3)]
    sources = (
        (own[0], own[1], (first_two, 0), (first_two, 1)),
        (own[2], own[0], own[1], (middle_one, 0)),
        ((middle_one, 0), own[2], own[0], own[1]),
        ((last_one, 0), after[2], after[0], after[1]),
    )
    for place, blocks in enumerate(sources):

        @on_shard(place)
        def _():
            for index, (ref, block) in enumerate(blocks):
                out_ref[:, index * cols : (index + 1) * cols] = ref[:, block * cols : (block + 1) * cols]


def moved(value, pairs):
    return lax.ppermute(value, "ctx", pairs)


def handed(value, pairs):
    sections, count = lax.axis_size("section"), lax.axis_size("ctx")
    return lax.ppermute(
        value,
        ("section", "ctx"),
        [
            (s * count + a, (s + 1) % sections * count + b)
            for s in range(sections)
            for a, b in pairs
        ],
    )


def on_device(streams, conv_weight, beta_logit, gate_log, norm_gain, w_out):
    count = lax.axis_size("ctx")
    toks, width = streams.shape[1], norm_gain.shape[1]
    x, taps, beta_t, gate_t, edge = load(
        streams[0], conv_weight[0], beta_logit[0].T, gate_log[0].T
    )
    rim = moved(edge, [(c, c + 1) for c in range(count - 1)])
    later_acts = later_activations(x, taps)
    whole = own = w_out[0]
    lefts = [moved(own, [(c, c - 1) for c in range(1, count)])]
    if count == 4:
        top, rest = own[: width // 2], own[width // 2 :]
        rim, later_acts, own, top = lax.optimization_barrier((rim, later_acts, own, top))
        left = moved(own, [(1, 2), (2, 3)])
        top = moved(top, [(0, 1)])
    else:
        rights = [moved(own, [(c, c + 1) for c in range(count - 1)])]
        for turn in range(2, count):
            rights.append(moved(rights[-1], [(c, c + 1) for c in range(turn - 1, count - 1)]))
            lefts.append(moved(lefts[-1], [(c, c - 1) for c in range(1, count - turn + 1)]))
    total_map, total_add, sent, direct, reach, both = shard_terms(
        later_acts, rim, x, taps, beta_t, gate_t
    )
    if count != 4:
        states = [moved(sent, [(0, 1)])]
        for turn in range(1, count - 1):
            states.append(moved(hand_on(total_map, total_add, states[-1]), [(turn, turn + 1)]))
        mixed = project(states, direct, reach, norm_gain, own, rights, lefts)
        return handed(mixed, [(c, c) for c in range(count)])[None]

    right = lefts[0]
    cols = own.shape[1]
    rows = (toks, width)
    one, two, three = ((toks, blocks * cols) for blocks in (1, 2, 3))
    sent, top = lax.optimization_barrier((sent, top))
    both, right = lax.optimization_barrier((both, lefts[0]))
    first = moved(sent, [(0, 1)])
    both = moved(both, [(3, 2), (2, 1)])
    out1 = hand_on(total_map, total_add, first)
    second = moved(out1, [(1, 2)])
    rows0 = call(first_rows_kernel, [direct, norm_gain], [rows])
    far0 = moved(rows0, [(0, 3)])
    rows1 = call(second_rows_kernel, [direct, reach, norm_gain, first], [rows])
    far1 = moved(rows1, [(1, 2)])
    rest = moved(rest, [(0, 1)])
    both, second = lax.optimization_barrier((both, second))
    rows3 = call(fourth_rows_kernel, [total_map, total_add, both, norm_gain, second], [rows])
    far3 = moved(rows3, [(2, 1)])
    own_three, next_three = call(
        near_columns_kernel,
        [direct, reach, norm_gain, second, rows0, rows1, rows3, whole, left, top, rest, right],
        [three, three],
        [rows],
    )
    middle_one = call(
        middle_columns_kernel, [both, norm_gain, out1, far1, top, rest, right], [one], [rows]
    )
    first_two = call(first_columns_kernel, [far0, whole, left], [two])
    last_one = call(last_columns_kernel, [far3, top, rest], [one])
    return call(
        assemble_kernel,
        [
            handed(own_three, [(0, 0), (1, 1), (2, 2)]),
            handed(next_three, [(2, 3)]),
            handed(middle_one, [(1, 2), (2, 1)]),
            handed(first_two, [(3, 0)]),
            handed(last_one, [(1, 3)]),
        ],
        [(toks, 4 * cols)],
    )[None]


def solution(mesh):
    placed = (
        P("section", "ctx", None),
        P("section", None, None),
        P("section", "ctx", None),
        P("section", "ctx", None),
        P("section", None),
        P("section", None, "ctx"),
    )
    return jax.shard_map(
        on_device, mesh=mesh, in_specs=placed, out_specs=P("section", "ctx", None), check_vma=False
    )
```
